128 devices in a mesh: leaf: 32 (over x, y, core), sub: 4 (over z).
Axes of the slice: x: 4, y: 4, z: 4, core: 2. Of those that a mesh axis runs over, the one named last changes fastest.
Arguments:
- right_sides: bfloat16 [131072, 3, 1024], P(('leaf', 'sub')), may hold values from -6 to 6
- panel_order: int32 [131072], P(('leaf', 'sub')), may hold values from 0 to 131071, as said below
- leaf_inverse: bfloat16 [512, 768, 768], P(('leaf', 'sub')), may hold values from -0.21875 to 0.21875
- test_basis: bfloat16 [3, 131072, 3, 128], P(None, ('leaf', 'sub')), may hold values from -0.01953125 to 0.01953125
- update_basis: bfloat16 [3, 131072, 3, 128], P(None, ('leaf', 'sub')), may hold values from -0.25 to 0.25
- coupling: float32 [3, 32, 256, 256], P(None, 'leaf'), as said below
Outputs:
- solution: float32 [131072, 3, 1024], P(('leaf', 'sub'))
The draws below stay inside these ranges and needn't reach their ends.
Inputs may be any that keep to these rules, and one draw needn't show every extreme that they name: `panel_order`: each run of 1024 positions that starts at a multiple of 1024 holds each panel number of that same run once. `coupling`: for each level l, the 32 / 2^l leaf ranges of one node hold equal copies of that node's matrix.
All inputs are finite; a program needn't handle non-finite values.
Results may differ from the reference program's by a relative error of at most 0.0059.
Values sent between devices are 32-bit elements; how exact they have to be, the bound alone decides.
A program may use at most 128 MiB of HBM per device.

```python
import math
import jax
import jax.numpy as jnp
from jax import lax

R = 128
COMP = 3
LEVELS = 3
NRHS = 1024
LEAF_ROWS = 768
PANELS_DEV = 1024
PANELS = 131072
LEAVES = 512
RANGES = 32


def draw_panel_order(key, part):
    key = jax.random.fold_in(key, 11)
    block_count = PANELS // PANELS_DEV
    block_keys = jax.random.split(key, block_count)
    orders = jax.vmap(lambda single: jax.random.permutation(single, PANELS_DEV))(block_keys)
    offsets = (jnp.arange(block_count, dtype=jnp.int32) * PANELS_DEV)[:, None]
    return (orders.astype(jnp.int32) + offsets).reshape(PANELS).astype(jnp.int32)


def draw_coupling(key, part):
    key = jax.random.fold_in(key, 23)
    width = 2 * R
    noise = jax.random.normal(key, (LEVELS, RANGES, width, width), jnp.float32) * (0.5 / math.sqrt(width))
    identity = jnp.eye(width, dtype=jnp.float32) * 0.8
    levels_out = []
    for tree_level in range(LEVELS):
        node_span = RANGES // 2 ** tree_level
        owners = jnp.arange(RANGES, dtype=jnp.int32) // node_span * node_span
        levels_out.append(jnp.take(noise[tree_level], owners, axis=0) + identity[None])
    return jnp.stack(levels_out, axis=0).astype(jnp.float32)


def steps_of(key, extent, pieces, least, top_value):
    level, own = 1.0, jax.random.fold_in(key, 6)
    for dim, shards_of in pieces:
        heights = jnp.exp(jax.random.uniform(jax.random.fold_in(own, dim), (shards_of,), jnp.float32, least / len(pieces), top_value / len(pieces)))
        level = level * jnp.repeat(heights, extent[dim] // shards_of).reshape([-1 if axis == dim else 1 for axis in range(len(extent))])
    return level


def gaussian(own_key, shape, scale, limit, shards=(), held_as=jnp.bfloat16):
    result = scale * jax.random.normal(own_key, shape, jnp.float32)
    if shards:
        result = result * steps_of(own_key, shape, shards, -0.22, 0.18)
    return jnp.clip(result, -limit, limit).astype(held_as)


def setup_inputs(seed: int = 0) -> dict:
    keys = jax.random.split(jax.random.key(seed), 7)
    return {
        "right_sides": gaussian(keys[0], (PANELS, COMP, NRHS), 1.0, 6.0, ((0, 128),)),
        "panel_order": draw_panel_order(jax.random.fold_in(keys[6], 71), 0),
        "leaf_inverse": gaussian(keys[2], (LEAVES, LEAF_ROWS, LEAF_ROWS), LEAF_ROWS ** -0.5, 0.21875, ((0, 128),)),
        "test_basis": gaussian(keys[3], (LEVELS, PANELS, COMP, R), (PANELS * COMP // 4) ** -0.5, 0.01953125, ((1, 128),)),
        "update_basis": gaussian(keys[4], (LEVELS, PANELS, COMP, R), (4 * R) ** -0.5, 0.25, ((1, 128),)),
        "coupling": draw_coupling(jax.random.fold_in(keys[6], 71), 0),
    }


def solve_leaf(operands):
    return jnp.dot(operands[0], operands[1], preferred_element_type=jnp.float32)


def project_group(operands):
    return jnp.einsum("pr,pn->rn", operands[0], operands[1], preferred_element_type=jnp.float32)


def apply_group(operands):
    return jnp.dot(operands[0], operands[1], preferred_element_type=jnp.float32)


def reference(right_sides, panel_order, leaf_inverse, test_basis, update_basis, coupling):
    ordered = jnp.take(right_sides, panel_order, axis=0)
    blocks = ordered.reshape(LEAVES, LEAF_ROWS, NRHS)
    field = lax.map(solve_leaf, (leaf_inverse, blocks)).reshape(PANELS * COMP, NRHS)
    for tree_level in range(LEVELS):
        groups = 2 ** (tree_level + 1)
        group_rows = PANELS * COMP // groups
        rounded = field.astype(jnp.bfloat16).reshape(groups, group_rows, NRHS)
        test_rows = test_basis[tree_level].reshape(groups, group_rows, R)
        group_sums = lax.map(project_group, (test_rows, rounded))
        paired = group_sums.reshape(groups // 2, 2 * R, NRHS)
        node_span = RANGES // 2 ** tree_level
        inverses = coupling[tree_level, ::node_span]
        weights = jnp.einsum("nij,njk->nik", inverses, paired, precision=lax.Precision.HIGHEST)
        weights = weights.astype(jnp.bfloat16).reshape(groups, R, NRHS)
        updates = update_basis[tree_level].reshape(groups, group_rows, R)
        correction = lax.map(apply_group, (updates, weights))
        field = field - correction.reshape(PANELS * COMP, NRHS)
    return field.reshape(PANELS, COMP, NRHS)
```

```python
import jax
import jax.numpy as jnp
from jax import lax
from jax.experimental import pallas as pl
from jax.experimental.pallas import tpu as pltpu
from jax.sharding import PartitionSpec as P

BF = jnp.bfloat16
F32 = jnp.float32
MIB = 1 << 20
MESH = pl.DeviceIdType.MESH
HIGH = lax.Precision.HIGHEST


def in_vmem(a):
    return pltpu.with_memory_space_constraint(a, pltpu.VMEM)


def project_kernel(order, x_hbm, a_hbm, v_hbm, u_hbm, st, gt,
                   xv, av, vv, uv, vsh, vit, bs, bd, bt, sems):
    loads = [pltpu.make_async_copy(s, d, sems.at[i])
             for i, (s, d) in enumerate([(v_hbm, vv), (u_hbm, uv), (a_hbm, av), (x_hbm, xv)])]
    for copy in loads:
        copy.start()
    loads[0].wait()
    for leaf in range(4):
        for level in range(3):
            for c in range(3):
                vsh[level, pl.ds(c, 256, stride=3), :] = vv[level, c, pl.ds(leaf * 256, 256), :].astype(F32)
        for level in range(3):
            vit[leaf, pl.ds(level * 128, 128), :] = vsh[level].astype(BF).T
    loads[1].wait()
    g0 = jnp.zeros((128, 256), F32)
    g1 = jnp.zeros((128, 128), F32)
    over_rows = (((0,), (0,)), ((), ()))
    for c in range(3):
        v12 = jnp.concatenate([vv[1, c], vv[2, c]], axis=1)
        g0 += lax.dot_general(uv[0, c], v12, over_rows, preferred_element_type=F32)
        g1 += lax.dot_general(uv[1, c], vv[2, c], over_rows, preferred_element_type=F32)
    gt[:, 0:128] = g1
    gt[:, 128:384] = g0
    loads[2].wait()
    for leaf in range(4):
        b = jnp.dot(vit[leaf], av[leaf], preferred_element_type=F32)
        for level in range(3):
            bs[pl.ds(leaf * 6144 + level, 768, stride=8), :] = b[level * 128:level * 128 + 128].T

    @pl.loop(0, 64)
    def _(i):
        for j in range(16):
            p = i * 16 + j
            dst = lax.bitwise_and(order[p], 1023) * 8
            for c in range(3):
                bd[pl.ds(pl.multiple_of(c * 8192 + dst, 8), 8), :] = (
                    bs[pl.ds(pl.multiple_of(p * 24 + c * 8, 8), 8), :])

    for c in range(3):
        for level in range(3):
            bt[pl.ds(level * 128, 128), pl.ds(c * 1024, 1024)] = (
                bd[pl.ds(c * 8192 + level, 1024, stride=8), :].astype(BF).T)
    loads[3].wait()
    for n in range(4):
        cols = pl.ds(n * 256, 256)
        total = jnp.dot(bt[...], xv[:, :, cols].reshape(3072, 256), preferred_element_type=F32)
        st[cols, :] = total.T


def project(order, x, a, v, u):
    vm = pl.BlockSpec(memory_space=pltpu.VMEM)
    hbm = pl.BlockSpec(memory_space=pl.ANY)
    return pl.pallas_call(
        project_kernel,
        out_shape=[pltpu.VMEM((1024, 384), F32), pltpu.VMEM((128, 384), F32)],
        in_specs=[pl.BlockSpec(memory_space=pltpu.SMEM), hbm, hbm, hbm, hbm],
        out_specs=[vm, vm],
        scratch_shapes=[
            pltpu.VMEM((3, 1024, 1024), BF),
            pltpu.VMEM((4, 768, 768), BF),
            pltpu.VMEM((3, 3, 1024, 128), BF),
            pltpu.VMEM((3, 3, 1024, 128), BF),
            pltpu.VMEM((3, 768, 128), F32),
            pltpu.VMEM((4, 384, 768), BF),
            pltpu.VMEM((24576, 128), F32),
            pltpu.VMEM((24576, 128), F32),
            pltpu.VMEM((384, 3072), BF),
            pltpu.SemaphoreType.DMA((4,)),
        ],
        compiler_params=pltpu.CompilerParams(vmem_limit_bytes=50 * MIB),
        name="project",
    )(order, x, a, v, u)


def update_kernel(field, u, wt, out, w):
    @pl.when((pl.program_id(0) == 0) & (pl.program_id(1) == 0))
    def _():
        w[...] = wt[...].T.astype(BF)
    c, r = pl.program_id(0), pl.program_id(1)
    rows = u.shape[2]
    ub = jnp.concatenate([u[0, 0], u[1, 0], u[2, 0]], axis=1)
    out[0] = field[c, pl.ds(pl.multiple_of(r * rows, rows), rows), :] - jnp.dot(ub, w[...], preferred_element_type=F32)


def update(field, u, wt, rows=256):
    vm = pl.BlockSpec(memory_space=pltpu.VMEM)
    return pl.pallas_call(
        update_kernel,
        grid=(3, 1024 // rows),
        out_shape=jax.ShapeDtypeStruct((3, 1024, 1024), F32),
        in_specs=[vm, pl.BlockSpec((3, 1, rows, 128), lambda c, r: (0, c, r, 0)), vm],
        out_specs=pl.BlockSpec((1, rows, 1024), lambda c, r: (c, r, 0)),
        scratch_shapes=[pltpu.VMEM((384, 1024), BF)],
        compiler_params=pltpu.CompilerParams(vmem_limit_bytes=16 * MIB),
        name="update",
    )(field, u, wt)


def reduce_kernel(order, x_hbm, a_hbm, st, gt, cp_hbm, field, w, xb, av, ap, xf, xg, ash, cp, r1, r2, p2, r3, r4, p4, r5, wv, rg1, rg2, pg2, rg3, rg3x, gfull, res,
                  lsem, xsem, s1, q1, s2, q2, s3, q3, s4, q4, s5, q5, s6, q6, s7, q7,
                  t1, v1, t2, v2, t3, v3, t3x, v3x, t4, v4, t5, v5):
    place = lax.axis_index("leaf")
    z = lax.axis_index("sub")
    k = lax.rem(place, 2)
    y = lax.rem(place // 2, 4)
    x = place // 8
    ia = jnp.where(k == 0, z, y)
    ib = jnp.where(k == 0, y, z)
    half = y // 2

    def device(xx, yy, kk, zz):
        return ((xx * 4 + yy) * 2 + kk, zz)

    def ring_a(d):
        t = lax.rem(ia + d, 4)
        return device(x, jnp.where(k == 0, y, t), k, jnp.where(k == 0, t, z))

    def ring_b(e, xx=None):
        t = lax.rem(ib + e, 4)
        return device(x if xx is None else xx, jnp.where(k == 0, t, y), k, jnp.where(k == 0, z, t))

    def xor1(v):
        return v + 1 - 2 * lax.rem(v, 2)

    def xor2(v):
        return lax.rem(v + 2, 4)

    sibling = xor1(x)
    other_core = device(x, y, 1 - k, z)
    xs = [device(xx, y, k, z) for xx in (sibling, xor2(x), xor2(sibling))]

    def send(src, dst, ssem, rsem, where):
        copy = pltpu.make_async_remote_copy(src_ref=src, dst_ref=dst, send_sem=ssem, recv_sem=rsem,
                                            device_id=where, device_id_type=MESH)
        copy.start()
        return copy

    xloads = []
    for n in range(4):
        for q in range(4):
            xloads.append(pltpu.make_async_copy(x_hbm.at[:, pl.ds(q * 256, 256), pl.ds(n * 256, 256)], xb.at[n, q], xsem.at[n, q]))
            xloads[-1].start()
    aload = pltpu.make_async_copy(a_hbm, av, lsem.at[1])
    aload.start()
    load = pltpu.make_async_copy(cp_hbm, cp, lsem.at[0])
    load.start()

    xrows = xf.reshape(24576, 128)

    def expand(n):
        for q in range(4):
            xloads[n * 4 + q].wait()

        @pl.loop(0, 64)
        def _(i):
            q = i // 16
            off = pl.multiple_of(lax.rem(i, 16) * 16, 16)
            for c in range(3):
                rows = xb[n, q, c, pl.ds(off, 16), :].astype(F32)
                for h in range(2):
                    for j in range(2):
                        xrows[pl.ds(c * 8192 + i * 128 + h * 64 + n * 2 + j, 8, stride=8), :] = (
                            rows[h * 8:h * 8 + 8, j * 128:j * 128 + 128])

    def permute_rows(leaf):
        if leaf == 0:
            aload.wait()
        for j in range(6):
            ash[j] = av[leaf, :, pl.ds(j * 128, 128)].astype(F32)
        for j in range(6):
            for c in range(3):
                ap[leaf, pl.ds(c * 256, 256), pl.ds(j * 128, 128)] = (
                    ash[j, pl.ds(c, 256, stride=3), :].astype(BF))

    def gather(leaf):
        @pl.loop(0, 16)
        def _(i):
            for kk in range(16):
                p = i * 16 + kk
                src = lax.rem(order[leaf * 256 + p], 1024)
                for c in range(3):
                    xg[pl.ds(pl.multiple_of(p * 24 + c * 8, 8), 8), :] = xf[c, src]

    def repack(leaf):
        @pl.loop(0, 48)
        def _(i):
            c = i // 16
            off = pl.multiple_of(lax.rem(i, 16) * 16, 16)
            for j in range(8):
                lo = xg[pl.ds(i * 128 + j, 8, stride=8), :]
                hi = xg[pl.ds(i * 128 + 64 + j, 8, stride=8), :]
                both = jnp.concatenate([lo, hi], axis=0).astype(BF)
                xb[j // 2, leaf, c, pl.ds(off, 16), pl.ds((j % 2) * 128, 128)] = both

    def multiply(leaf, n):
        f = jnp.dot(ap[leaf], xb[n, leaf].reshape(768, 256), preferred_element_type=F32)
        field[:, pl.ds(leaf * 256, 256), pl.ds(n * 256, 256)] = f.reshape(3, 256, 256)

    pieces = [lambda n=n: expand(n) for n in range(4)]
    for leaf in range(4):
        pieces += [lambda leaf=leaf: permute_rows(leaf), lambda leaf=leaf: gather(leaf), lambda leaf=leaf: repack(leaf)]
        pieces += [lambda leaf=leaf, n=n: multiply(leaf, n) for n in range(4)]

    def work(count):
        for _ in range(min(count, len(pieces))):
            pieces.pop(0)()

    partners = [other_core] + xs
    for d in range(1, 4):
        partners += [ring_a(d), ring_b(d), ring_b(d, sibling)]
    barrier = pltpu.get_barrier_semaphore()
    for where in partners:
        pl.semaphore_signal(barrier, inc=1, device_id=where, device_id_type=MESH)
    work(1)
    pl.semaphore_wait(barrier, len(partners))

    sends = []
    g1 = send(gt.at[pl.ds((1 - k) * 64, 64)], rg1, t1.at[0], v1.at[0], other_core)
    sends.append(g1)
    c1 = {}
    for d in (1, 2, 3, 0):
        rows = pl.multiple_of((1 - k) * 512 + lax.rem(ib + d, 4) * 128, 128)
        c1[d] = send(st.at[pl.ds(rows, 128)], r1.at[d], s1.at[d], q1.at[d], other_core)
        sends.append(c1[d])

    g1.wait_recv()
    rg1[...] += gt[pl.ds(pl.multiple_of(k * 64, 64), 64), :]
    g2 = []
    for d in range(1, 4):
        rows = pl.multiple_of(lax.rem(ia + d, 4) * 16, 16)
        g2.append(send(rg1.at[pl.ds(rows, 16)], rg2.at[d - 1], t2.at[d - 1], v2.at[d - 1], ring_a(d)))
    sends += g2
    c2 = {}
    for d in (1, 2, 3, 0):
        work({1: 1, 2: 1, 3: 1, 0: 1}[d])
        c1[d].wait_recv()
        rows = pl.multiple_of(k * 512 + lax.rem(ia + d, 4) * 128, 128)
        r1[d] += st[pl.ds(rows, 128), :]
        if d:
            for e in (1, 2, 3, 0):
                sub = pl.multiple_of(lax.rem(ib + e, 4) * 32, 32)
                c2[d, e] = send(r1.at[d, pl.ds(sub, 32)], r2.at[d - 1, e], s2.at[d - 1, e], q2.at[d - 1, e], ring_a(d))
                sends.append(c2[d, e])

    halves = [half] + [jnp.where(k == 0, half, lax.rem(y + 4 - d, 4) // 2) for d in range(1, 4)]

    def split(parts, h):
        return sum(jnp.where(hh == h, part, 0.0) for hh, part in zip(halves, parts))

    work(1)
    for copy in g2:
        copy.wait_recv()
    gp = [rg1[pl.ds(pl.multiple_of(ia * 16, 16), 16), :]] + [rg2[d] for d in range(3)]
    pg2[:, 0:128] = sum(p[:, 128:256] for p in gp)
    for h in range(2):
        pg2[:, 128 + h * 128:256 + h * 128] = split([p[:, 256:384] for p in gp], h)
        pg2[:, 384 + h * 128:512 + h * 128] = split([p[:, 0:128] for p in gp], h)
    g3, g3x = [], []
    for e in range(1, 4):
        g3.append(send(pg2, rg3.at[e - 1], t3.at[e - 1], v3.at[e - 1], ring_b(e)))
    for e in range(4):
        g3x.append(send(pg2.at[:, pl.ds(0, 128)], rg3x.at[e], t3x.at[e], v3x.at[e], ring_b(e, sibling)))
    sends += g3 + g3x
    c3 = []
    for e in (1, 2, 3, 0):
        work({1: 2, 2: 1, 3: 1, 0: 1}[e])
        for d in range(1, 4):
            c2[d, e].wait_recv()
        sub = pl.multiple_of(lax.rem(ib + e, 4) * 32, 32)
        parts = [r1[0, pl.ds(sub, 32), :]] + [r2[d, e] for d in range(3)]
        p2[e, :, 0:256] = sum(p[:, 0:256] for p in parts)
        for h in range(2):
            p2[e, :, 256 + h * 128:384 + h * 128] = split([p[:, 256:384] for p in parts], h)
        if e:
            c3.append(send(p2.at[e], r3.at[e - 1], s3.at[e - 1], q3.at[e - 1], ring_b(e)))
    sends += c3

    work(1)
    for copy in g3 + g3x:
        copy.wait_recv()
    grows = pl.multiple_of(k * 64 + ia * 16, 16)
    gfull[pl.ds(grows, 16), 0:640] = pg2[...] + rg3[0] + rg3[1] + rg3[2]
    gfull[pl.ds(grows, 16), 640:768] = rg3x[0] + rg3x[1] + rg3x[2] + rg3x[3]
    g4 = [send(gfull.at[pl.ds(grows, 16)], gfull.at[pl.ds(grows, 16)], t4.at[d - 1], v4.at[d - 1], ring_a(d))
          for d in range(1, 4)]
    sends += g4
    work(2)
    for copy in c3:
        copy.wait_recv()
    p4[...] = p2[0] + r3[0] + r3[1] + r3[2]
    c4 = [send(p4.at[:, pl.ds(0, 256)], r4.at[0], s4.at[0], q4.at[0], xs[0])]
    c4 += [send(p4.at[:, pl.ds(0, 128)], r4.at[i, :, pl.ds(0, 128)], s4.at[i], q4.at[i], xs[i]) for i in (1, 2)]
    sends += c4
    work(1)
    for copy in g4:
        copy.wait_recv()
    ghalf = gfull.at[pl.ds(pl.multiple_of(k * 64, 64), 64)]
    g5 = send(ghalf, ghalf, t5.at[0], v5.at[0], other_core)
    sends.append(g5)

    def dot(a, b):
        return lax.dot_general(a, b, (((1,), (0,)), ((), ())), precision=HIGH, preferred_element_type=F32)

    def dot_t(a, b):
        return lax.dot_general(a, b, (((1,), (1,)), ((), ())), precision=HIGH, preferred_element_type=F32)

    def rounded(a):
        return a.astype(BF).astype(F32)

    def pair(own_first, own, other):
        return jnp.concatenate([jnp.where(own_first, own, other), jnp.where(own_first, other, own)], axis=1)

    work(2)
    load.wait()
    for copy in c4:
        copy.wait_recv()
    upper = x // 2
    odd = lax.rem(x, 2)
    own0 = p4[:, 0:128] + r4[0, :, 0:128]
    far0 = r4[1, :, 0:128] + r4[2, :, 0:128]
    w0 = rounded(dot_t(pair(upper == 0, own0, far0), cp[0, pl.ds(pl.multiple_of(upper * 128, 128), 128), :]))
    work(1)
    g5.wait_recv()
    own1 = p4[:, 128:256] - dot(w0, gfull[:, 0:128])
    far1 = r4[0, :, 128:256] - dot(w0, gfull[:, 640:768])
    w1 = rounded(dot_t(pair(odd == 0, own1, far1), cp[1, pl.ds(pl.multiple_of(odd * 128, 128), 128), :]))
    s2h = [p4[:, 256 + h * 128:384 + h * 128] - dot(w0, gfull[:, 128 + h * 128:256 + h * 128])
           - dot(w1, gfull[:, 384 + h * 128:512 + h * 128]) for h in range(2)]
    w2 = rounded(dot_t(jnp.concatenate(s2h, axis=1), cp[2]))
    res[:, 0:128] = w0
    res[:, 128:256] = w1
    res[:, 256:512] = w2

    c5 = [send(res, r5.at[e - 1], s5.at[e - 1], q5.at[e - 1], ring_b(e)) for e in range(1, 4)]
    sends += c5
    c6 = {}
    for e in range(4):
        work({0: 0, 1: 3, 2: 1, 3: 1}[e])
        if e:
            c5[e - 1].wait_recv()
        block = res[...] if e == 0 else r5[e - 1]
        rows = pl.multiple_of(k * 512 + ia * 128 + lax.rem(ib + 4 - e, 4) * 32, 32)
        for h in range(2):
            wv[h, e, :, 0:256] = block[:, 0:256]
            wv[h, e, :, 256:384] = block[:, 256 + h * 128:384 + h * 128]
        w[pl.ds(rows, 32), 0:256] = block[:, 0:256]
        w[pl.ds(rows, 32), 256:384] = jnp.where(half == 0, block[:, 256:384], block[:, 384:512])
        for d in range(1, 4):
            far_half = jnp.where(k == 0, half, lax.rem(y + d, 4) // 2)
            c6[d, e] = send(wv.at[far_half, e], w.at[pl.ds(rows, 32)], s6.at[d - 1, e], q6.at[d - 1, e], ring_a(d))
            sends.append(c6[d, e])
    c7 = []
    for d in range(4):
        work({0: 0, 1: 5, 2: 1, 3: 1}[d])
        if d:
            for e in range(4):
                c6[d, e].wait_recv()
        part = w.at[pl.ds(pl.multiple_of(k * 512 + lax.rem(ia + 4 - d, 4) * 128, 128), 128)]
        c7.append(send(part, part, s7.at[d], q7.at[d], other_core))
    sends += c7
    work(99)
    for copy in c7:
        copy.wait_recv()
    for copy in sends:
        copy.wait_send()


def reduce(order, x, a, st, gt, cp):
    vm = pl.BlockSpec(memory_space=pltpu.VMEM)
    hbm = pl.BlockSpec(memory_space=pl.ANY)
    dma = pltpu.SemaphoreType.DMA
    shape = lambda *dims: pltpu.VMEM(dims, F32)
    sems = [(2,), (4, 4)] + [s for s in [(4,), (3, 4), (3,), (3,), (3,), (3, 4), (4,), (1,), (3,), (3,), (4,), (3,), (1,)] for _ in range(2)]
    return pl.pallas_call(
        reduce_kernel,
        out_shape=[pltpu.VMEM((3, 1024, 1024), F32), pltpu.VMEM((1024, 384), F32)],
        in_specs=[pl.BlockSpec(memory_space=pltpu.SMEM), hbm, hbm, vm, vm, hbm],
        out_specs=[vm, vm],
        scratch_shapes=[
            pltpu.VMEM((4, 4, 3, 256, 256), BF), pltpu.VMEM((4, 768, 768), BF), pltpu.VMEM((4, 768, 768), BF),
            shape(3, 1024, 8, 128), shape(6144, 128), shape(6, 768, 128),
            shape(3, 256, 256), shape(4, 128, 384), shape(3, 4, 32, 384), shape(4, 32, 512), shape(3, 32, 512),
            shape(3, 32, 256), shape(32, 512), shape(3, 32, 512), shape(2, 4, 32, 384),
            shape(64, 384), shape(3, 16, 384), shape(16, 640), shape(3, 16, 640), shape(4, 16, 128),
            shape(128, 768), shape(32, 512),
        ] + [dma(s) for s in sems],
        compiler_params=pltpu.CompilerParams(vmem_limit_bytes=40 * MIB, collective_id=0, has_side_effects=True),
        name="reduce_and_solve",
    )(order, x, a, st, gt, cp)


def body(right_sides, panel_order, leaf_inverse, test_basis, update_basis, coupling):
    sides = jnp.transpose(right_sides, (1, 0, 2))
    test = jnp.transpose(test_basis, (0, 2, 1, 3))
    upd = jnp.transpose(update_basis, (0, 2, 1, 3))
    st, gt = project(panel_order, sides, leaf_inverse, test, upd)
    field, w = reduce(panel_order, sides, leaf_inverse, in_vmem(st), in_vmem(gt), coupling.reshape(3, 256, 256))
    out = update(in_vmem(field), upd, in_vmem(w))
    return jnp.transpose(out, (1, 0, 2))


def solution(mesh):
    in_specs = (
        P(("leaf", "sub"), None, None),
        P(("leaf", "sub")),
        P(("leaf", "sub"), None, None),
        P(None, ("leaf", "sub"), None, None),
        P(None, ("leaf", "sub"), None, None),
        P(None, "leaf", None, None),
    )
    out_specs = P(("leaf", "sub"), None, None)
    return jax.shard_map(body, mesh=mesh, in_specs=in_specs, out_specs=out_specs, check_vma=False)
```

```python
import jax
import jax.numpy as jnp
from jax import lax
from jax.experimental import pallas as pl
from jax.experimental.pallas import tpu as pltpu
from jax.sharding import PartitionSpec as P

BF = jnp.bfloat16
F32 = jnp.float32
MIB = 1 << 20
MESH = pl.DeviceIdType.MESH
HIGH = lax.Precision.HIGHEST
CHUNKS = 2
WIDE = 1024 // CHUNKS
CORE = WIDE // 2
RING = CORE // 4
OWN = RING // 4


def in_vmem(a):
    return pltpu.with_memory_space_constraint(a, pltpu.VMEM)


def solve_kernel(order, x_hbm, a_hbm, v_hbm, u_hbm, cp_hbm, field, w,
                 xb, av, ap, vv, uv, vsh, vit, xf, xg, ash, bw, cp, st, gt,
                 r1, ra, rb, rc, x13, p2, r3, p4, r4, wf, fa, fw,
                 rg1, rg2, pg2, rg3, rg3x, gfull,
                 lsem, xsem, s1, q1, s2, q2, s3, q3, s4, q4, s5, q5, s6, q6, s7, q7,
                 t1, v1, t2, v2, t3, v3, t3x, v3x, t4, v4, t5, v5):
    place = lax.axis_index("leaf")
    z = lax.axis_index("sub")
    k = lax.rem(place, 2)
    y = lax.rem(place // 2, 4)
    x = place // 8
    ia = jnp.where(k == 0, z, y)
    ib = jnp.where(k == 0, y, z)
    half = y // 2

    def device(xx, yy, kk, zz):
        return ((xx * 4 + yy) * 2 + kk, zz)

    def ring_a(d):
        t = lax.rem(ia + d, 4)
        return device(x, jnp.where(k == 0, y, t), k, jnp.where(k == 0, t, z))

    def ring_b(e, xx=None):
        t = lax.rem(ib + e, 4)
        return device(x if xx is None else xx, jnp.where(k == 0, t, y), k, jnp.where(k == 0, z, t))

    sibling = x + 1 - 2 * lax.rem(x, 2)
    other_core = device(x, y, 1 - k, z)
    xs = [device(xx, y, k, z) for xx in (sibling, lax.rem(x + 2, 4), lax.rem(sibling + 2, 4))]
    half_of = {d: jnp.where(k == 0, half, lax.rem(y + d, 4) // 2) for d in (1, 2, 3)}
    half_of[0] = half
    sends = []

    def send(src, dst, ssem, rsem, where):
        copy = pltpu.make_async_remote_copy(src_ref=src, dst_ref=dst, send_sem=ssem, recv_sem=rsem,
                                            device_id=where, device_id_type=MESH)
        copy.start()
        sends.append(copy)
        return copy

    def load(src, dst, sem):
        copy = pltpu.make_async_copy(src, dst, sem)
        copy.start()
        return copy

    vload = load(v_hbm, vv, lsem.at[0])
    xloads = {}
    for c in range(3):
        for q in range(4):
            xloads[c, q] = load(x_hbm.at[c, pl.ds(q * 256, 256), :], xb.at[q, c], xsem.at[c, q])
        if c == 0:
            uload = load(u_hbm.at[pl.ds(0, 2)], uv, lsem.at[1])
    aload = load(a_hbm, av, lsem.at[2])
    cload = load(cp_hbm, cp, lsem.at[3])

    partners = [other_core] + xs
    for d in range(1, 4):
        partners += [ring_a(d), ring_b(d), ring_b(d, sibling)]
    barrier = pltpu.get_barrier_semaphore()
    for where in partners:
        pl.semaphore_signal(barrier, inc=1, device_id=where, device_id_type=MESH)

    vload.wait()
    for leaf in range(4):
        for level in range(3):
            for c in range(3):
                vsh[level, pl.ds(c, 256, stride=3), :] = vv[level, c, pl.ds(leaf * 256, 256), :].astype(F32)
        for level in range(3):
            vit[leaf, pl.ds(level * 128, 128), :] = vsh[level].astype(BF).T

    xrows = xf.reshape(24576, 128)

    def expand(c):
        for q in range(4):
            xloads[c, q].wait()

        @pl.loop(0, 64, unroll=4)
        def _(i):
            q = i // 16
            rows = xb[q, c, pl.ds(pl.multiple_of(lax.rem(i, 16) * 16, 16), 16), :].astype(F32)
            for h in range(2):
                for j in range(8):
                    xrows[pl.ds(c * 8192 + i * 128 + h * 64 + j, 8, stride=8), :] = (
                        rows[h * 8:h * 8 + 8, j * 128:j * 128 + 128])

    def gather(leaf):
        @pl.loop(0, 16, unroll=2)
        def _(i):
            for kk in range(16):
                p = i * 16 + kk
                src = lax.bitwise_and(order[leaf * 256 + p], 1023)
                for c in range(3):
                    xg[pl.ds(pl.multiple_of(p * 24 + c * 8, 8), 8), :] = xf[c, src]

        @pl.loop(0, 48, unroll=4)
        def _(i):
            c = i // 16
            off = pl.multiple_of(lax.rem(i, 16) * 16, 16)
            for j in range(8):
                lo = xg[pl.ds(i * 128 + j, 8, stride=8), :]
                hi = xg[pl.ds(i * 128 + 64 + j, 8, stride=8), :]
                xb[leaf, c, pl.ds(off, 16), pl.ds(j * 128, 128)] = jnp.concatenate([lo, hi], axis=0).astype(BF)

    expand(0)
    uload.wait()
    g0 = jnp.zeros((128, 256), F32)
    g1 = jnp.zeros((128, 128), F32)
    over_rows = (((0,), (0,)), ((), ()))
    for c in range(3):
        v12 = jnp.concatenate([vv[1, c], vv[2, c]], axis=1)
        g0 += lax.dot_general(uv[0, c], v12, over_rows, preferred_element_type=F32)
        g1 += lax.dot_general(uv[1, c], vv[2, c], over_rows, preferred_element_type=F32)
    gt[:, 0:128] = g1
    gt[:, 128:384] = g0
    pl.semaphore_wait(barrier, len(partners))
    gc1 = send(gt.at[pl.ds(pl.multiple_of((1 - k) * 64, 64), 64)], rg1, t1.at[0], v1.at[0], other_core)
    expand(1)
    gc1.wait_recv()
    rg1[...] += gt[pl.ds(pl.multiple_of(k * 64, 64), 64), :]
    gc2 = []
    for d in range(1, 4):
        rows = pl.multiple_of(lax.rem(ia + d, 4) * 16, 16)
        gc2.append(send(rg1.at[pl.ds(rows, 16)], rg2.at[d - 1], t2.at[d - 1], v2.at[d - 1], ring_a(d)))
    expand(2)
    aload.wait()
    for leaf in range(4):
        bw[leaf] = jnp.dot(vit[leaf], av[leaf], preferred_element_type=F32).astype(BF)
    for copy in gc2:
        copy.wait_recv()
    gp = [rg1[pl.ds(pl.multiple_of(ia * 16, 16), 16), :]] + [rg2[d] for d in range(3)]
    ghalf = [half] + [half_of[4 - d] for d in range(1, 4)]

    def split(parts, h):
        return sum(jnp.where(hh == h, part, 0.0) for hh, part in zip(ghalf, parts))

    pg2[:, 0:128] = sum(p[:, 128:256] for p in gp)
    for h in range(2):
        pg2[:, 128 + h * 128:256 + h * 128] = split([p[:, 256:384] for p in gp], h)
        pg2[:, 384 + h * 128:512 + h * 128] = split([p[:, 0:128] for p in gp], h)
    gc3 = []
    for e in range(1, 4):
        gc3.append(send(pg2, rg3.at[e - 1], t3.at[e - 1], v3.at[e - 1], ring_b(e)))
    for e in range(4):
        gc3.append(send(pg2.at[:, pl.ds(0, 128)], rg3x.at[e], t3x.at[e], v3x.at[e], ring_b(e, sibling)))
    gather(0)
    gather(1)
    for copy in gc3:
        copy.wait_recv()
    grows = pl.multiple_of(k * 64 + ia * 16, 16)
    gfull[pl.ds(grows, 16), 0:640] = pg2[...] + rg3[0] + rg3[1] + rg3[2]
    gfull[pl.ds(grows, 16), 640:768] = rg3x[0] + rg3x[1] + rg3x[2] + rg3x[3]
    gc4 = [send(gfull.at[pl.ds(grows, 16)], gfull.at[pl.ds(grows, 16)], t4.at[d - 1], v4.at[d - 1], ring_a(d))
           for d in range(1, 4)]
    gather(2)
    gather(3)
    for copy in gc4:
        copy.wait_recv()
    gown = gfull.at[pl.ds(pl.multiple_of(k * 64, 64), 64)]
    gc5 = send(gown, gown, t5.at[0], v5.at[0], other_core)

    def permute_rows(leaf):
        for j in range(6):
            ash[j] = av[leaf, :, pl.ds(j * 128, 128)].astype(F32)
        for j in range(6):
            for c in range(3):
                ap[leaf, pl.ds(c * 256, 256), pl.ds(j * 128, 128)] = (
                    ash[j, pl.ds(c, 256, stride=3), :].astype(BF))

    def multiply(leaf, n):
        cols = pl.ds(n * 256, 256)
        f = jnp.dot(ap[leaf], xb[leaf, :, :, cols].reshape(768, 256), preferred_element_type=F32)
        field[:, pl.ds(leaf * 256, 256), cols] = f.reshape(3, 256, 256)

    pieces = []
    for leaf in range(4):
        pieces.append(lambda leaf=leaf: permute_rows(leaf))
        pieces += [lambda leaf=leaf, n=n: multiply(leaf, n) for n in range(4)]

    def work(count):
        for _ in range(min(count, len(pieces))):
            pieces.pop(0)()

    def dot(a, b):
        return lax.dot_general(a, b, (((1,), (0,)), ((), ())), precision=HIGH, preferred_element_type=F32)

    def dot_t(a, b):
        return lax.dot_general(a, b, (((1,), (1,)), ((), ())), precision=HIGH, preferred_element_type=F32)

    def rounded(a):
        return a.astype(BF).astype(F32)

    def pair(own_first, own, other):
        return jnp.concatenate([jnp.where(own_first, own, other), jnp.where(own_first, other, own)], axis=1)

    def widen(part, hh):
        last = part[:, 256:384]
        return jnp.concatenate([part[:, 0:256], jnp.where(hh == 0, last, 0.0), jnp.where(hh == 1, last, 0.0)], axis=1)

    def narrow(block, hh):
        return jnp.concatenate([block[:, 0:256], jnp.where(hh == 0, block[:, 256:384], block[:, 384:512])], axis=1)

    def project(ch):
        cols = pl.ds(ch * WIDE, WIDE)
        total = jnp.zeros((384, WIDE), F32)
        for leaf in range(4):
            total += jnp.dot(bw[leaf], xb[leaf, :, :, cols].reshape(768, WIDE), preferred_element_type=F32)
        st[cols, :] = total.T

    lower, upper = pl.ds(0, RING // 2), pl.ds(RING // 2, RING // 2)
    at = {}

    def block_rows(ch, core, t, rows):
        return pl.ds(pl.multiple_of(ch * WIDE + core * CORE + t * RING, rows), rows)

    def to_core(ch):
        for d in (2, 1, 3, 0):
            src = st.at[block_rows(ch, 1 - k, lax.rem(ib + d, 4), RING)]
            at["c1", ch, d] = send(src, r1.at[ch, d], s1.at[ch, d], q1.at[ch, d], other_core)

    def to_ring_a(ch):
        for d in (2, 1, 3, 0):
            at["c1", ch, d].wait_recv()
            r1[ch, d] += st[block_rows(ch, k, lax.rem(ia + d, 4), RING), :]
            if d == 2:
                at["ra", ch, 0] = send(r1.at[ch, 2, lower], ra.at[ch, 0], s2.at[ch, 0], q2.at[ch, 0], ring_a(1))
                at["ra", ch, 1] = send(r1.at[ch, 2, upper], ra.at[ch, 1], s2.at[ch, 1], q2.at[ch, 1], ring_a(3))
            elif d == 1:
                at["rb", ch, 0] = send(r1.at[ch, 1, upper], rb.at[ch, 0], s2.at[ch, 2], q2.at[ch, 2], ring_a(1))
            elif d == 3:
                at["rb", ch, 1] = send(r1.at[ch, 3, lower], rb.at[ch, 1], s2.at[ch, 3], q2.at[ch, 3], ring_a(3))

    def along_ring_a(ch):
        at["ra", ch, 0].wait_recv()
        x13[ch, 0] = widen(r1[ch, 1, lower], half) + widen(ra[ch, 0], half_of[3])
        at["rc", ch, 0] = send(x13.at[ch, 0], rc.at[ch, 0], s2.at[ch, 4], q2.at[ch, 4], ring_a(1))
        at["ra", ch, 1].wait_recv()
        x13[ch, 1] = widen(r1[ch, 3, upper], half) + widen(ra[ch, 1], half_of[1])
        at["rc", ch, 1] = send(x13.at[ch, 1], rc.at[ch, 1], s2.at[ch, 5], q2.at[ch, 5], ring_a(3))

    def to_ring_b(ch):
        at["rb", ch, 0].wait_recv()
        at["rb", ch, 1].wait_recv()
        at["rc", ch, 0].wait_recv()
        p2[ch, lower] = widen(r1[ch, 0, lower], half) + rc[ch, 0] + widen(rb[ch, 1], half_of[1])
        at["rc", ch, 1].wait_recv()
        p2[ch, upper] = widen(r1[ch, 0, upper], half) + rc[ch, 1] + widen(rb[ch, 0], half_of[3])
        for e in (2, 1, 3):
            rows = pl.ds(pl.multiple_of(lax.rem(ib + e, 4) * OWN, OWN), OWN)
            at["c3", ch, e] = send(p2.at[ch, rows], r3.at[ch, e - 1], s3.at[ch, e - 1], q3.at[ch, e - 1], ring_b(e))

    def to_x(ch):
        for e in (1, 2, 3):
            at["c3", ch, e].wait_recv()
        rows = pl.ds(pl.multiple_of(ib * OWN, OWN), OWN)
        p4[ch] = p2[ch, rows, :] + r3[ch, 0] + r3[ch, 1] + r3[ch, 2]
        for i, lanes in ((2, 128), (1, 128), (0, 256)):
            at["c4", ch, i] = send(p4.at[ch, :, pl.ds(0, lanes)], r4.at[ch, i, :, pl.ds(0, lanes)],
                                   s4.at[ch, i], q4.at[ch, i], xs[i])

    def small_systems(ch):
        if ch == 0:
            cload.wait()
            gc5.wait_recv()
        for i in range(3):
            at["c4", ch, i].wait_recv()
        top = x // 2
        odd = lax.rem(x, 2)
        own0 = p4[ch, :, 0:128] + r4[ch, 0, :, 0:128]
        far0 = r4[ch, 1, :, 0:128] + r4[ch, 2, :, 0:128]
        w0 = rounded(dot_t(pair(top == 0, own0, far0), cp[0, pl.ds(pl.multiple_of(top * 128, 128), 128), :]))
        own1 = p4[ch, :, 128:256] - dot(w0, gfull[:, 0:128])
        far1 = r4[ch, 0, :, 128:256] - dot(w0, gfull[:, 640:768])
        w1 = rounded(dot_t(pair(odd == 0, own1, far1), cp[1, pl.ds(pl.multiple_of(odd * 128, 128), 128), :]))
        both = [p4[ch, :, 256 + h * 128:384 + h * 128] - dot(w0, gfull[:, 128 + h * 128:256 + h * 128])
                - dot(w1, gfull[:, 384 + h * 128:512 + h * 128]) for h in range(2)]
        w2 = rounded(dot_t(jnp.concatenate(both, axis=1), cp[2]))
        rows = pl.ds(pl.multiple_of(ib * OWN, OWN), OWN)
        wf[ch, rows, 0:128] = w0
        wf[ch, rows, 128:256] = w1
        wf[ch, rows, 256:512] = w2
        part = wf.at[ch, rows]
        for e in (2, 1, 3):
            at["c5", ch, e] = send(part, part, s5.at[ch, e - 1], q5.at[ch, e - 1], ring_b(e))

    def part_of_w(ch, d, rows=None):
        t = lax.rem(ia + d, 4)
        if rows is None:
            return block_rows(ch, k, t, RING)
        return pl.ds(pl.multiple_of(ch * WIDE + k * CORE + t * RING + rows * (RING // 2), RING // 2), RING // 2)

    def to_partner(ch, d):
        part = w.at[part_of_w(ch, d)]
        at["c7", ch, d] = send(part, part, s7.at[ch, d], q7.at[ch, d], other_core)

    def back_ring_a(ch):
        for e in (1, 2, 3):
            at["c5", ch, e].wait_recv()
        at["fa", ch, 0] = send(wf.at[ch], fa.at[ch, 0], s6.at[ch, 0], q6.at[ch, 0], ring_a(1))
        at["fa", ch, 1] = send(wf.at[ch], fa.at[ch, 1], s6.at[ch, 1], q6.at[ch, 1], ring_a(3))
        w[part_of_w(ch, 0), :] = narrow(wf[ch], half)
        to_partner(ch, 0)

    def back_along(ch):
        at["fa", ch, 0].wait_recv()
        fw[ch, 0] = narrow(fa[ch, 0, lower, :], half_of[1])
        at["fw", ch, 0] = send(fw.at[ch, 0], w.at[part_of_w(ch, 3, 0)], s6.at[ch, 2], q6.at[ch, 2], ring_a(1))
        at["fa", ch, 1].wait_recv()
        fw[ch, 1] = narrow(fa[ch, 1, upper, :], half_of[3])
        at["fw", ch, 1] = send(fw.at[ch, 1], w.at[part_of_w(ch, 1, 1)], s6.at[ch, 3], q6.at[ch, 3], ring_a(3))
        w[part_of_w(ch, 3), :] = narrow(fa[ch, 0], half)
        to_partner(ch, 3)
        w[part_of_w(ch, 1), :] = narrow(fa[ch, 1], half)
        to_partner(ch, 1)

    def back_core(ch):
        at["fw", ch, 0].wait_recv()
        at["fw", ch, 1].wait_recv()
        to_partner(ch, 2)

    project(0)
    to_core(0)
    project(1)
    to_core(1)
    to_ring_a(0)
    work(2)
    along_ring_a(0)
    to_ring_a(1)
    work(2)
    along_ring_a(1)
    to_ring_b(0)
    work(3)
    to_x(0)
    to_ring_b(1)
    work(3)
    small_systems(0)
    to_x(1)
    work(3)
    back_ring_a(0)
    small_systems(1)
    work(3)
    back_along(0)
    back_ring_a(1)
    back_core(0)
    work(99)
    back_along(1)
    back_core(1)
    work(99)
    for ch in range(CHUNKS):
        for d in range(4):
            at["c7", ch, d].wait_recv()
    for copy in sends:
        copy.wait_send()


def solve(order, x, a, v, u, cp):
    vm = pl.BlockSpec(memory_space=pltpu.VMEM)
    hbm = pl.BlockSpec(memory_space=pl.ANY)
    dma = pltpu.SemaphoreType.DMA

    def shape(*dims):
        return pltpu.VMEM(dims, F32)

    n = CHUNKS
    sems = [(4,), (3, 4)]
    for s in [(n, 4), (n, 6), (n, 3), (n, 3), (n, 3), (n, 4), (n, 4), (1,), (3,), (3,), (4,), (3,), (1,)]:
        sems += [s, s]
    return pl.pallas_call(
        solve_kernel,
        out_shape=[pltpu.VMEM((3, 1024, 1024), F32), pltpu.VMEM((1024, 384), F32)],
        in_specs=[pl.BlockSpec(memory_space=pltpu.SMEM), hbm, hbm, hbm, hbm, hbm],
        out_specs=[vm, vm],
        scratch_shapes=[
            pltpu.VMEM((4, 3, 256, 1024), BF), pltpu.VMEM((4, 768, 768), BF), pltpu.VMEM((4, 768, 768), BF),
            pltpu.VMEM((3, 3, 1024, 128), BF), pltpu.VMEM((2, 3, 1024, 128), BF), shape(3, 768, 128),
            pltpu.VMEM((4, 384, 768), BF), shape(3, 1024, 8, 128), shape(6144, 128), shape(6, 768, 128),
            pltpu.VMEM((4, 384, 768), BF), shape(3, 256, 256), shape(1024, 384), shape(128, 384),
            shape(n, 4, RING, 384), shape(n, 2, RING // 2, 384), shape(n, 2, RING // 2, 384),
            shape(n, 2, RING // 2, 512), shape(n, 2, RING // 2, 512), shape(n, RING, 512),
            shape(n, 3, OWN, 512), shape(n, OWN, 512), shape(n, 3, OWN, 256), shape(n, RING, 512),
            shape(n, 2, RING, 512), shape(n, 2, RING // 2, 384),
            shape(64, 384), shape(3, 16, 384), shape(16, 640), shape(3, 16, 640), shape(4, 16, 128), shape(128, 768),
        ] + [dma(s) for s in sems],
        compiler_params=pltpu.CompilerParams(vmem_limit_bytes=49 * MIB, collective_id=0, has_side_effects=True),
        name="leaf_solve_and_levels",
    )(order, x, a, v, u, cp)


ROWS = 512


def update_kernel(field, u_hbm, wt, out, u, w, buf, usem, sem):
    loads = {}
    for c in range(3):
        for level in range(3):
            loads[c, level] = pltpu.make_async_copy(
                u_hbm.at[level, c], u.at[c, :, pl.ds(level * 128, 128)], usem.at[c, level])
            loads[c, level].start()
    w[...] = (-wt[...].T).astype(BF)
    copies = []
    for c in range(3):
        for level in range(3):
            loads[c, level].wait()
        for r in range(1024 // ROWS):
            rows = pl.ds(r * ROWS, ROWS)
            i = len(copies)
            slot = i % 4
            if i >= 4:
                copies[i - 4].wait()
            buf[slot] = field[c, rows, :] + jnp.dot(u[c, rows, :], w[...], preferred_element_type=F32)
            copies.append(pltpu.make_async_copy(buf.at[slot], out.at[c, rows, :], sem.at[slot]))
            copies[-1].start()
    for copy in copies[-4:]:
        copy.wait()


def update(field, u, wt):
    vm = pl.BlockSpec(memory_space=pltpu.VMEM)
    hbm = pl.BlockSpec(memory_space=pl.ANY)
    return pl.pallas_call(
        update_kernel,
        out_shape=jax.ShapeDtypeStruct((3, 1024, 1024), F32),
        in_specs=[vm, hbm, vm],
        out_specs=hbm,
        scratch_shapes=[
            pltpu.VMEM((3, 1024, 384), BF),
            pltpu.VMEM((384, 1024), BF),
            pltpu.VMEM((4, ROWS, 1024), F32),
            pltpu.SemaphoreType.DMA((3, 3)),
            pltpu.SemaphoreType.DMA((4,)),
        ],
        compiler_params=pltpu.CompilerParams(vmem_limit_bytes=20 * MIB),
        name="update",
    )(field, u, wt)


def body(right_sides, panel_order, leaf_inverse, test_basis, update_basis, coupling):
    sides = jnp.transpose(right_sides, (1, 0, 2))
    test = jnp.transpose(test_basis, (0, 2, 1, 3))
    upd = jnp.transpose(update_basis, (0, 2, 1, 3))
    field, w = solve(panel_order, sides, leaf_inverse, test, upd, coupling.reshape(3, 256, 256))
    out = update(in_vmem(field), upd, in_vmem(w))
    return jnp.transpose(out, (1, 0, 2))


def solution(mesh):
    in_specs = (
        P(("leaf", "sub"), None, None),
        P(("leaf", "sub")),
        P(("leaf", "sub"), None, None),
        P(None, ("leaf", "sub"), None, None),
        P(None, ("leaf", "sub"), None, None),
        P(None, "leaf", None, None),
    )
    out_specs = P(("leaf", "sub"), None, None)
    return jax.shard_map(body, mesh=mesh, in_specs=in_specs, out_specs=out_specs, check_vma=False)
```

```python
import jax
import jax.numpy as jnp
from jax import lax
from jax.experimental import pallas as pl
from jax.experimental.pallas import tpu as pltpu
from jax.sharding import PartitionSpec as P

BF = jnp.bfloat16
F32 = jnp.float32
MIB = 1 << 20
MESH = pl.DeviceIdType.MESH
HIGH = lax.Precision.HIGHEST
CHUNKS = 2
WIDE = 1024 // CHUNKS
CORE = WIDE // 2
RING = CORE // 4
OWN = RING // 4


def in_vmem(a):
    return pltpu.with_memory_space_constraint(a, pltpu.VMEM)


def project_kernel(order, x_hbm, a_hbm, v_hbm, u_hbm, st, gt,
                   xv, av, vv, uv, vsh, vit, bs, bd, bt, sems):
    loads = [pltpu.make_async_copy(s, d, sems.at[i])
             for i, (s, d) in enumerate([(v_hbm, vv), (u_hbm, uv), (a_hbm, av), (x_hbm, xv)])]
    for copy in loads:
        copy.start()
    loads[0].wait()
    for leaf in range(4):
        for level in range(3):
            for c in range(3):
                vsh[level, pl.ds(c, 256, stride=3), :] = vv[level, c, pl.ds(leaf * 256, 256), :].astype(F32)
        for level in range(3):
            vit[leaf, pl.ds(level * 128, 128), :] = vsh[level].astype(BF).T
    loads[1].wait()
    g0 = jnp.zeros((128, 256), F32)
    g1 = jnp.zeros((128, 128), F32)
    over_rows = (((0,), (0,)), ((), ()))
    for c in range(3):
        v12 = jnp.concatenate([vv[1, c], vv[2, c]], axis=1)
        g0 += lax.dot_general(uv[0, c], v12, over_rows, preferred_element_type=F32)
        g1 += lax.dot_general(uv[1, c], vv[2, c], over_rows, preferred_element_type=F32)
    gt[:, 0:128] = g1
    gt[:, 128:384] = g0
    loads[2].wait()
    for leaf in range(4):
        b = jnp.dot(vit[leaf], av[leaf], preferred_element_type=F32)
        for level in range(3):
            bs[pl.ds(leaf * 6144 + level, 768, stride=8), :] = b[level * 128:level * 128 + 128].T

    @pl.loop(0, 64)
    def _(i):
        for j in range(16):
            p = i * 16 + j
            dst = lax.bitwise_and(order[p], 1023) * 8
            for c in range(3):
                bd[pl.ds(pl.multiple_of(c * 8192 + dst, 8), 8), :] = (
                    bs[pl.ds(pl.multiple_of(p * 24 + c * 8, 8), 8), :])

    for c in range(3):
        for level in range(3):
            bt[pl.ds(level * 128, 128), pl.ds(c * 1024, 1024)] = (
                bd[pl.ds(c * 8192 + level, 1024, stride=8), :].astype(BF).T)
    loads[3].wait()
    for n in range(2):
        cols = pl.ds(n * 512, 512)
        total = jnp.zeros((384, 512), F32)
        for c in range(3):
            total += jnp.dot(bt[:, pl.ds(c * 1024, 1024)], xv[c, :, cols], preferred_element_type=F32)
        st[cols, :] = total.T


def project(order, x, a, v, u):
    vm = pl.BlockSpec(memory_space=pltpu.VMEM)
    hbm = pl.BlockSpec(memory_space=pl.ANY)
    return pl.pallas_call(
        project_kernel,
        out_shape=[pltpu.VMEM((1024, 384), F32), pltpu.VMEM((128, 384), F32)],
        in_specs=[pl.BlockSpec(memory_space=pltpu.SMEM), hbm, hbm, hbm, hbm],
        out_specs=[vm, vm],
        scratch_shapes=[
            pltpu.VMEM((3, 1024, 1024), BF),
            pltpu.VMEM((4, 768, 768), BF),
            pltpu.VMEM((3, 3, 1024, 128), BF),
            pltpu.VMEM((3, 3, 1024, 128), BF),
            pltpu.VMEM((3, 768, 128), F32),
            pltpu.VMEM((4, 384, 768), BF),
            pltpu.VMEM((24576, 128), F32),
            pltpu.VMEM((24576, 128), F32),
            pltpu.VMEM((384, 3072), BF),
            pltpu.SemaphoreType.DMA((4,)),
        ],
        compiler_params=pltpu.CompilerParams(vmem_limit_bytes=50 * MIB),
        name="project",
    )(order, x, a, v, u)


def solve_kernel(order, x_hbm, a_hbm, st, gt, cp_hbm, field, w,
                 xb, av, ap, xf, xg, ash, cp,
                 r1, r2, p2, r3, p4, r4, wf, nv,
                 rg1, rg2, pg2, rg3, rg3x, gfull,
                 lsem, xsem, s1, q1, s2, q2, s3, q3, s4, q4, s5, q5, s6, q6, s7, q7,
                 t1, v1, t2, v2, t3, v3, t3x, v3x, t4, v4, t5, v5):
    place = lax.axis_index("leaf")
    z = lax.axis_index("sub")
    k = lax.rem(place, 2)
    y = lax.rem(place // 2, 4)
    x = place // 8
    ia = jnp.where(k == 0, z, y)
    ib = jnp.where(k == 0, y, z)
    half = y // 2

    def device(xx, yy, kk, zz):
        return ((xx * 4 + yy) * 2 + kk, zz)

    def ring_a(d):
        t = lax.rem(ia + d, 4)
        return device(x, jnp.where(k == 0, y, t), k, jnp.where(k == 0, t, z))

    def ring_b(e, xx=None):
        t = lax.rem(ib + e, 4)
        return device(x if xx is None else xx, jnp.where(k == 0, t, y), k, jnp.where(k == 0, z, t))

    sibling = x + 1 - 2 * lax.rem(x, 2)
    other_core = device(x, y, 1 - k, z)
    xs = [device(xx, y, k, z) for xx in (sibling, lax.rem(x + 2, 4), lax.rem(sibling + 2, 4))]
    half_of = {d: jnp.where(k == 0, half, lax.rem(y + d, 4) // 2) for d in (1, 2, 3)}
    half_of[0] = half
    sends = []

    def send(src, dst, ssem, rsem, where):
        copy = pltpu.make_async_remote_copy(src_ref=src, dst_ref=dst, send_sem=ssem, recv_sem=rsem,
                                            device_id=where, device_id_type=MESH)
        copy.start()
        sends.append(copy)
        return copy

    def load(src, dst, sem):
        copy = pltpu.make_async_copy(src, dst, sem)
        copy.start()
        return copy

    xloads = {}
    for c in range(3):
        for q in range(4):
            xloads[c, q] = load(x_hbm.at[c, pl.ds(q * 256, 256), :], xb.at[q, c], xsem.at[c, q])
    aload = load(a_hbm, av, lsem.at[2])
    cload = load(cp_hbm, cp, lsem.at[3])

    partners = [other_core] + xs
    for d in range(1, 4):
        partners += [ring_a(d), ring_b(d), ring_b(d, sibling)]
    barrier = pltpu.get_barrier_semaphore()
    for where in partners:
        pl.semaphore_signal(barrier, inc=1, device_id=where, device_id_type=MESH)

    xrows = xf.reshape(24576, 128)

    def expand(c):
        for q in range(4):
            xloads[c, q].wait()

        @pl.loop(0, 64, unroll=4)
        def _(i):
            q = i // 16
            rows = xb[q, c, pl.ds(pl.multiple_of(lax.rem(i, 16) * 16, 16), 16), :].astype(F32)
            for h in range(2):
                for j in range(8):
                    xrows[pl.ds(c * 8192 + i * 128 + h * 64 + j, 8, stride=8), :] = (
                        rows[h * 8:h * 8 + 8, j * 128:j * 128 + 128])

    def gather(leaf):
        @pl.loop(0, 16, unroll=2)
        def _(i):
            for kk in range(16):
                p = i * 16 + kk
                src = lax.bitwise_and(order[leaf * 256 + p], 1023)
                for c in range(3):
                    xg[pl.ds(pl.multiple_of(p * 24 + c * 8, 8), 8), :] = xf[c, src]

    def repack(leaf):
        @pl.loop(0, 48, unroll=4)
        def _(i):
            c = i // 16
            off = pl.multiple_of(lax.rem(i, 16) * 16, 16)
            for j in range(8):
                lo = xg[pl.ds(i * 128 + j, 8, stride=8), :]
                hi = xg[pl.ds(i * 128 + 64 + j, 8, stride=8), :]
                xb[leaf, c, pl.ds(off, 16), pl.ds(j * 128, 128)] = jnp.concatenate([lo, hi], axis=0).astype(BF)

    expand(0)
    pl.semaphore_wait(barrier, len(partners))
    at = {}
    ghalf = [half] + [half_of[4 - d] for d in range(1, 4)]
    grows = pl.multiple_of(k * 64 + ia * 16, 16)

    def split(parts, h):
        return sum(jnp.where(hh == h, part, 0.0) for hh, part in zip(ghalf, parts))

    def bases_1():
        at["g1"] = send(gt.at[pl.ds(pl.multiple_of((1 - k) * 64, 64), 64)], rg1, t1.at[0], v1.at[0], other_core)

    def bases_2():
        at["g1"].wait_recv()
        rg1[...] += gt[pl.ds(pl.multiple_of(k * 64, 64), 64), :]
        for d in range(1, 4):
            rows = pl.multiple_of(lax.rem(ia + d, 4) * 16, 16)
            at["g2", d] = send(rg1.at[pl.ds(rows, 16)], rg2.at[d - 1], t2.at[d - 1], v2.at[d - 1], ring_a(d))

    def bases_3():
        for d in range(1, 4):
            at["g2", d].wait_recv()
        gp = [rg1[pl.ds(pl.multiple_of(ia * 16, 16), 16), :]] + [rg2[d] for d in range(3)]
        pg2[:, 0:128] = sum(p[:, 128:256] for p in gp)
        for h in range(2):
            pg2[:, 128 + h * 128:256 + h * 128] = split([p[:, 256:384] for p in gp], h)
            pg2[:, 384 + h * 128:512 + h * 128] = split([p[:, 0:128] for p in gp], h)
        for e in range(1, 4):
            at["g3", e] = send(pg2, rg3.at[e - 1], t3.at[e - 1], v3.at[e - 1], ring_b(e))
        for e in range(4):
            at["g3", 4 + e] = send(pg2.at[:, pl.ds(0, 128)], rg3x.at[e], t3x.at[e], v3x.at[e], ring_b(e, sibling))

    def bases_4():
        for e in range(1, 8):
            at["g3", e].wait_recv()
        gfull[pl.ds(grows, 16), 0:640] = pg2[...] + rg3[0] + rg3[1] + rg3[2]
        gfull[pl.ds(grows, 16), 640:768] = rg3x[0] + rg3x[1] + rg3x[2] + rg3x[3]
        for d in range(1, 4):
            part = gfull.at[pl.ds(grows, 16)]
            at["g4", d] = send(part, part, t4.at[d - 1], v4.at[d - 1], ring_a(d))

    def bases_5():
        for d in range(1, 4):
            at["g4", d].wait_recv()
        part = gfull.at[pl.ds(pl.multiple_of(k * 64, 64), 64)]
        at["g5"] = send(part, part, t5.at[0], v5.at[0], other_core)

    def permute_rows(leaf):
        if leaf == 0:
            aload.wait()
        for j in range(6):
            ash[j] = av[leaf, :, pl.ds(j * 128, 128)].astype(F32)
        for j in range(6):
            for c in range(3):
                ap[leaf, pl.ds(c * 256, 256), pl.ds(j * 128, 128)] = (
                    ash[j, pl.ds(c, 256, stride=3), :].astype(BF))

    def multiply(leaf, n):
        cols = pl.ds(n * 256, 256)
        f = jnp.dot(ap[leaf], xb[leaf, :, :, cols].reshape(768, 256), preferred_element_type=F32)
        field[:, pl.ds(leaf * 256, 256), cols] = f.reshape(3, 256, 256)

    pieces = [lambda: expand(1), lambda: expand(2)]
    for leaf in range(4):
        pieces += [lambda leaf=leaf: gather(leaf), lambda leaf=leaf: repack(leaf), lambda leaf=leaf: permute_rows(leaf)]
        pieces += [lambda leaf=leaf, n=n: multiply(leaf, n) for n in range(4)]

    def work(count):
        for _ in range(min(count, len(pieces))):
            pieces.pop(0)()

    def dot(a, b):
        return lax.dot_general(a, b, (((1,), (0,)), ((), ())), precision=HIGH, preferred_element_type=F32)

    def dot_t(a, b):
        return lax.dot_general(a, b, (((1,), (1,)), ((), ())), precision=HIGH, preferred_element_type=F32)

    def rounded(a):
        return a.astype(BF).astype(F32)

    def pair(own_first, own, other):
        return jnp.concatenate([jnp.where(own_first, own, other), jnp.where(own_first, other, own)], axis=1)

    def widen(part, hh):
        last = part[:, 256:384]
        return jnp.concatenate([part[:, 0:256], jnp.where(hh == 0, last, 0.0), jnp.where(hh == 1, last, 0.0)], axis=1)

    def narrow(block, hh):
        return jnp.concatenate([block[:, 0:256], jnp.where(hh == 0, block[:, 256:384], block[:, 384:512])], axis=1)

    def block_rows(ch, core, t, rows):
        return pl.ds(pl.multiple_of(ch * WIDE + core * CORE + t * RING, rows), rows)

    def to_core(ch):
        for d in (2, 1, 3, 0):
            src = st.at[block_rows(ch, 1 - k, lax.rem(ib + d, 4), RING)]
            at["c1", ch, d] = send(src, r1.at[ch, d], s1.at[ch, d], q1.at[ch, d], other_core)

    def to_ring_a(ch):
        for d in (2, 1, 3, 0):
            at["c1", ch, d].wait_recv()
            r1[ch, d] += st[block_rows(ch, k, lax.rem(ia + d, 4), RING), :]
            if d:
                at["c2", ch, d] = send(r1.at[ch, d], r2.at[ch, d - 1], s2.at[ch, d - 1], q2.at[ch, d - 1], ring_a(d))

    def to_ring_b(ch):
        for d in (1, 2, 3):
            at["c2", ch, d].wait_recv()
        total = widen(r1[ch, 0], half)
        for d in (1, 2, 3):
            total += widen(r2[ch, d - 1], half_of[4 - d])
        p2[ch] = total
        for e in (2, 1, 3):
            rows = pl.ds(pl.multiple_of(lax.rem(ib + e, 4) * OWN, OWN), OWN)
            at["c3", ch, e] = send(p2.at[ch, rows], r3.at[ch, e - 1], s3.at[ch, e - 1], q3.at[ch, e - 1], ring_b(e))

    def to_x(ch):
        for e in (1, 2, 3):
            at["c3", ch, e].wait_recv()
        rows = pl.ds(pl.multiple_of(ib * OWN, OWN), OWN)
        p4[ch] = p2[ch, rows, :] + r3[ch, 0] + r3[ch, 1] + r3[ch, 2]
        for i, lanes in ((2, 128), (1, 128), (0, 256)):
            at["c4", ch, i] = send(p4.at[ch, :, pl.ds(0, lanes)], r4.at[ch, i, :, pl.ds(0, lanes)],
                                   s4.at[ch, i], q4.at[ch, i], xs[i])

    def small_systems(ch):
        if ch == 0:
            cload.wait()
            at["g5"].wait_recv()
        for i in range(3):
            at["c4", ch, i].wait_recv()
        top = x // 2
        odd = lax.rem(x, 2)
        own0 = p4[ch, :, 0:128] + r4[ch, 0, :, 0:128]
        far0 = r4[ch, 1, :, 0:128] + r4[ch, 2, :, 0:128]
        w0 = rounded(dot_t(pair(top == 0, own0, far0), cp[0, pl.ds(pl.multiple_of(top * 128, 128), 128), :]))
        own1 = p4[ch, :, 128:256] - dot(w0, gfull[:, 0:128])
        far1 = r4[ch, 0, :, 128:256] - dot(w0, gfull[:, 640:768])
        w1 = rounded(dot_t(pair(odd == 0, own1, far1), cp[1, pl.ds(pl.multiple_of(odd * 128, 128), 128), :]))
        both = [p4[ch, :, 256 + h * 128:384 + h * 128] - dot(w0, gfull[:, 128 + h * 128:256 + h * 128])
                - dot(w1, gfull[:, 384 + h * 128:512 + h * 128]) for h in range(2)]
        w2 = rounded(dot_t(jnp.concatenate(both, axis=1), cp[2]))
        rows = pl.ds(pl.multiple_of(ib * OWN, OWN), OWN)
        wf[ch, rows, 0:128] = w0
        wf[ch, rows, 128:256] = w1
        wf[ch, rows, 256:512] = w2
        part = wf.at[ch, rows]
        for e in (2, 1, 3):
            at["c5", ch, e] = send(part, part, s5.at[ch, e - 1], q5.at[ch, e - 1], ring_b(e))

    def to_partner(ch, d):
        part = w.at[block_rows(ch, k, lax.rem(ia + d, 4), RING)]
        at["c7", ch, d] = send(part, part, s7.at[ch, d], q7.at[ch, d], other_core)

    def back_ring_a(ch):
        for e in (1, 2, 3):
            at["c5", ch, e].wait_recv()
        for h in range(2):
            nv[ch, h] = narrow(wf[ch], h)
        rows = block_rows(ch, k, ia, RING)
        for d in (2, 1, 3):
            at["c6", ch, d] = send(nv.at[ch, half_of[d]], w.at[rows], s6.at[ch, d - 1], q6.at[ch, d - 1], ring_a(d))
        w[rows, :] = narrow(wf[ch], half)
        to_partner(ch, 0)

    def back_core(ch):
        for d in (1, 3, 2):
            at["c6", ch, d].wait_recv()
            to_partner(ch, 4 - d)

    bases_1()
    to_core(0)
    to_core(1)
    work(1)
    bases_2()
    to_ring_a(0)
    to_ring_a(1)
    work(2)
    bases_3()
    work(2)
    to_ring_b(0)
    work(1)
    bases_4()
    work(1)
    to_ring_b(1)
    work(2)
    to_x(0)
    bases_5()
    work(5)
    to_x(1)
    small_systems(0)
    work(5)
    small_systems(1)
    work(99)
    back_ring_a(0)
    back_ring_a(1)
    back_core(0)
    back_core(1)
    work(99)
    for ch in range(CHUNKS):
        for d in range(4):
            at["c7", ch, d].wait_recv()
    for copy in sends:
        copy.wait_send()


def solve(order, x, a, st, gt, cp):
    vm = pl.BlockSpec(memory_space=pltpu.VMEM)
    hbm = pl.BlockSpec(memory_space=pl.ANY)
    dma = pltpu.SemaphoreType.DMA

    def shape(*dims):
        return pltpu.VMEM(dims, F32)

    n = CHUNKS
    sems = [(4,), (3, 4)]
    for s in [(n, 4), (n, 3), (n, 3), (n, 3), (n, 3), (n, 3), (n, 4), (1,), (3,), (3,), (4,), (3,), (1,)]:
        sems += [s, s]
    return pl.pallas_call(
        solve_kernel,
        out_shape=[pltpu.VMEM((3, 1024, 1024), F32), pltpu.VMEM((1024, 384), F32)],
        in_specs=[pl.BlockSpec(memory_space=pltpu.SMEM), hbm, hbm, vm, vm, hbm],
        out_specs=[vm, vm],
        scratch_shapes=[
            pltpu.VMEM((4, 3, 256, 1024), BF), pltpu.VMEM((4, 768, 768), BF), pltpu.VMEM((4, 768, 768), BF),
            shape(3, 1024, 8, 128), shape(6144, 128), shape(6, 768, 128), shape(3, 256, 256),
            shape(n, 4, RING, 384), shape(n, 3, RING, 384), shape(n, RING, 512),
            shape(n, 3, OWN, 512), shape(n, OWN, 512), shape(n, 3, OWN, 256), shape(n, RING, 512),
            shape(n, 2, RING, 384),
            shape(64, 384), shape(3, 16, 384), shape(16, 640), shape(3, 16, 640), shape(4, 16, 128), shape(128, 768),
        ] + [dma(s) for s in sems],
        compiler_params=pltpu.CompilerParams(vmem_limit_bytes=42 * MIB, collective_id=0, has_side_effects=True),
        name="leaf_solve_and_levels",
    )(order, x, a, st, gt, cp)


ROWS = 512


def update_kernel(field, u_hbm, wt, out, u, w, buf, usem, sem):
    loads = {}
    for c in range(3):
        for level in range(3):
            loads[c, level] = pltpu.make_async_copy(
                u_hbm.at[level, c], u.at[c, :, pl.ds(level * 128, 128)], usem.at[c, level])
            loads[c, level].start()
    w[...] = (-wt[...].T).astype(BF)
    copies = []
    for c in range(3):
        for level in range(3):
            loads[c, level].wait()
        for r in range(1024 // ROWS):
            rows = pl.ds(r * ROWS, ROWS)
            i = len(copies)
            slot = i % 4
            if i >= 4:
                copies[i - 4].wait()
            buf[slot] = field[c, rows, :] + jnp.dot(u[c, rows, :], w[...], preferred_element_type=F32)
            copies.append(pltpu.make_async_copy(buf.at[slot], out.at[c, rows, :], sem.at[slot]))
            copies[-1].start()
    for copy in copies[-4:]:
        copy.wait()


def update(field, u, wt):
    vm = pl.BlockSpec(memory_space=pltpu.VMEM)
    hbm = pl.BlockSpec(memory_space=pl.ANY)
    return pl.pallas_call(
        update_kernel,
        out_shape=jax.ShapeDtypeStruct((3, 1024, 1024), F32),
        in_specs=[vm, hbm, vm],
        out_specs=hbm,
        scratch_shapes=[
            pltpu.VMEM((3, 1024, 384), BF),
            pltpu.VMEM((384, 1024), BF),
            pltpu.VMEM((4, ROWS, 1024), F32),
            pltpu.SemaphoreType.DMA((3, 3)),
            pltpu.SemaphoreType.DMA((4,)),
        ],
        compiler_params=pltpu.CompilerParams(vmem_limit_bytes=20 * MIB),
        name="update",
    )(field, u, wt)


def body(right_sides, panel_order, leaf_inverse, test_basis, update_basis, coupling):
    sides = jnp.transpose(right_sides, (1, 0, 2))
    test = jnp.transpose(test_basis, (0, 2, 1, 3))
    upd = jnp.transpose(update_basis, (0, 2, 1, 3))
    st, gt = project(panel_order, sides, leaf_inverse, test, upd)
    field, w = solve(panel_order, sides, leaf_inverse, in_vmem(st), in_vmem(gt), coupling.reshape(3, 256, 256))
    out = update(in_vmem(field), upd, in_vmem(w))
    return jnp.transpose(out, (1, 0, 2))


def solution(mesh):
    in_specs = (
        P(("leaf", "sub"), None, None),
        P(("leaf", "sub")),
        P(("leaf", "sub"), None, None),
        P(None, ("leaf", "sub"), None, None),
        P(None, ("leaf", "sub"), None, None),
        P(None, "leaf", None, None),
    )
    out_specs = P(("leaf", "sub"), None, None)
    return jax.shard_map(body, mesh=mesh, in_specs=in_specs, out_specs=out_specs, check_vma=False)
```

```python
import jax
import jax.numpy as jnp
from jax import lax
from jax.experimental import pallas as pl
from jax.experimental.pallas import tpu as pltpu
from jax.sharding import PartitionSpec as P

BF = jnp.bfloat16
F32 = jnp.float32
MIB = 1 << 20
MESH = pl.DeviceIdType.MESH
HIGH = lax.Precision.HIGHEST
CHUNKS = 2
WIDE = 1024 // CHUNKS
CORE = WIDE // 2
RING = CORE // 4
OWN = RING // 4


def in_vmem(a):
    return pltpu.with_memory_space_constraint(a, pltpu.VMEM)


def project_kernel(order, x_hbm, a_hbm, v_hbm, u_hbm, st, gt,
                   xv, av, vv, uv, vsh, vit, bs, bd, bt, acc, places, sems):
    pairs = [(v_hbm, vv)] + [(a_hbm.at[leaf], av.at[leaf]) for leaf in range(4)]
    pairs += [(order, places), (u_hbm.at[pl.ds(0, 2)], uv), (x_hbm, xv)]
    loads = [pltpu.make_async_copy(s, d, sems.at[i]) for i, (s, d) in enumerate(pairs)]
    for copy in loads:
        copy.start()
    loads[0].wait()
    for leaf in range(4):
        for level in range(3):
            for c in range(3):
                vsh[level, pl.ds(c, 256, stride=3), :] = vv[level, c, pl.ds(leaf * 256, 256), :].astype(F32)
        for level in range(3):
            vit[leaf, pl.ds(level * 128, 128), :] = vsh[level].astype(BF).T
    for leaf in range(4):
        loads[1 + leaf].wait()
        b = jnp.dot(vit[leaf], av[leaf], preferred_element_type=F32)
        for level in range(3):
            bs[pl.ds(leaf * 6144 + level, 768, stride=8), :] = b[level * 128:level * 128 + 128].T

    loads[6].wait()
    g0 = jnp.zeros((128, 256), F32)
    g1 = jnp.zeros((128, 128), F32)
    over_rows = (((0,), (0,)), ((), ()))
    for c in range(3):
        v12 = jnp.concatenate([vv[1, c], vv[2, c]], axis=1)
        g0 += lax.dot_general(uv[0, c], v12, over_rows, preferred_element_type=F32)
        g1 += lax.dot_general(uv[1, c], vv[2, c], over_rows, preferred_element_type=F32)
    gt[:, 0:128] = g1
    gt[:, 128:384] = g0
    loads[5].wait()

    @pl.loop(0, 64)
    def _(i):
        for j in range(16):
            p = i * 16 + j
            dst = lax.bitwise_and(places[p], 1023) * 8
            for c in range(3):
                bd[pl.ds(pl.multiple_of(c * 8192 + dst, 8), 8), :] = (
                    bs[pl.ds(pl.multiple_of(p * 24 + c * 8, 8), 8), :])

    loads[7].wait()
    for c in range(3):
        for level in range(3):
            bt[pl.ds(level * 128, 128), pl.ds(c * 1024, 1024)] = (
                bd[pl.ds(c * 8192 + level, 1024, stride=8), :].astype(BF).T)
        for n in range(2):
            cols = pl.ds(n * 512, 512)
            part = jnp.dot(bt[:, pl.ds(c * 1024, 1024)], xv[c, :, cols], preferred_element_type=F32)
            if c == 0:
                acc[:, cols] = part
            elif c == 1:
                acc[:, cols] += part
            else:
                st[cols, :] = (acc[:, cols] + part).T


def project(order, x, a, v, u):
    vm = pl.BlockSpec(memory_space=pltpu.VMEM)
    hbm = pl.BlockSpec(memory_space=pl.ANY)
    return pl.pallas_call(
        project_kernel,
        out_shape=[pltpu.VMEM((1024, 384), F32), pltpu.VMEM((128, 384), F32)],
        in_specs=[pl.BlockSpec(memory_space=pltpu.HBM), hbm, hbm, hbm, hbm],
        out_specs=[vm, vm],
        scratch_shapes=[
            pltpu.VMEM((3, 1024, 1024), BF),
            pltpu.VMEM((4, 768, 768), BF),
            pltpu.VMEM((3, 3, 1024, 128), BF),
            pltpu.VMEM((2, 3, 1024, 128), BF),
            pltpu.VMEM((3, 768, 128), F32),
            pltpu.VMEM((4, 384, 768), BF),
            pltpu.VMEM((24576, 128), F32),
            pltpu.VMEM((24576, 128), F32),
            pltpu.VMEM((384, 3072), BF),
            pltpu.VMEM((384, 1024), F32),
            pltpu.SMEM((1024,), jnp.int32),
            pltpu.SemaphoreType.DMA((8,)),
        ],
        compiler_params=pltpu.CompilerParams(vmem_limit_bytes=50 * MIB),
        name="project",
    )(order, x, a, v, u)


def solve_kernel(order, x_hbm, a_hbm, st, gt, cp_hbm, field, w,
                 xb, av, ap, xf, xg, ash, cp,
                 r1, r2, ro, ra, rb, x3, rc, p2, r3, p4, r4, wf, nv, fa, fw,
                 rg1, rg2, pg2, rg3, rg3x, gfull,
                 lsem, xsem, s1, q1, s2, q2, s3, q3, s4, q4, s5, q5, s6, q6, s7, q7,
                 t1, v1, t2, v2, t3, v3, t3x, v3x, t4, v4, t5, v5):
    place = lax.axis_index("leaf")
    z = lax.axis_index("sub")
    k = lax.rem(place, 2)
    y = lax.rem(place // 2, 4)
    x = place // 8
    ia = jnp.where(k == 0, z, y)
    ib = jnp.where(k == 0, y, z)
    half = y // 2

    def device(xx, yy, kk, zz):
        return ((xx * 4 + yy) * 2 + kk, zz)

    def ring_a(d):
        t = lax.rem(ia + d, 4)
        return device(x, jnp.where(k == 0, y, t), k, jnp.where(k == 0, t, z))

    def ring_b(e, xx=None):
        t = lax.rem(ib + e, 4)
        return device(x if xx is None else xx, jnp.where(k == 0, t, y), k, jnp.where(k == 0, z, t))

    sibling = x + 1 - 2 * lax.rem(x, 2)
    other_core = device(x, y, 1 - k, z)
    xs = [device(xx, y, k, z) for xx in (sibling, lax.rem(x + 2, 4), lax.rem(sibling + 2, 4))]
    half_of = {d: jnp.where(k == 0, half, lax.rem(y + d, 4) // 2) for d in (1, 2, 3)}
    half_of[0] = half
    sends = []

    def send(src, dst, ssem, rsem, where):
        copy = pltpu.make_async_remote_copy(src_ref=src, dst_ref=dst, send_sem=ssem, recv_sem=rsem,
                                            device_id=where, device_id_type=MESH)
        copy.start()
        sends.append(copy)
        return copy

    def load(src, dst, sem):
        copy = pltpu.make_async_copy(src, dst, sem)
        copy.start()
        return copy

    xloads = {}
    for c in range(3):
        for q in range(4):
            xloads[c, q] = load(x_hbm.at[c, pl.ds(q * 256, 256), :], xb.at[q, c], xsem.at[c, q])
    aload = load(a_hbm, av, lsem.at[2])
    cload = load(cp_hbm, cp, lsem.at[3])

    partners = [other_core] + xs
    for d in range(1, 4):
        partners += [ring_a(d), ring_b(d), ring_b(d, sibling)]
    barrier = pltpu.get_barrier_semaphore()
    for where in partners:
        pl.semaphore_signal(barrier, inc=1, device_id=where, device_id_type=MESH)

    xrows = xf.reshape(24576, 128)

    def expand(c):
        for q in range(4):
            xloads[c, q].wait()

        @pl.loop(0, 64, unroll=4)
        def _(i):
            q = i // 16
            rows = xb[q, c, pl.ds(pl.multiple_of(lax.rem(i, 16) * 16, 16), 16), :].astype(F32)
            for h in range(2):
                for j in range(8):
                    xrows[pl.ds(c * 8192 + i * 128 + h * 64 + j, 8, stride=8), :] = (
                        rows[h * 8:h * 8 + 8, j * 128:j * 128 + 128])

    def gather(leaf):
        @pl.loop(0, 16, unroll=2)
        def _(i):
            for kk in range(16):
                p = i * 16 + kk
                src = lax.bitwise_and(order[leaf * 256 + p], 1023)
                for c in range(3):
                    xg[pl.ds(pl.multiple_of(p * 24 + c * 8, 8), 8), :] = xf[c, src]

    def repack(leaf):
        @pl.loop(0, 48, unroll=4)
        def _(i):
            c = i // 16
            off = pl.multiple_of(lax.rem(i, 16) * 16, 16)
            for j in range(8):
                lo = xg[pl.ds(i * 128 + j, 8, stride=8), :]
                hi = xg[pl.ds(i * 128 + 64 + j, 8, stride=8), :]
                xb[leaf, c, pl.ds(off, 16), pl.ds(j * 128, 128)] = jnp.concatenate([lo, hi], axis=0).astype(BF)

    expand(0)
    pl.semaphore_wait(barrier, len(partners))
    at = {}
    ghalf = [half] + [half_of[4 - d] for d in range(1, 4)]
    grows = pl.multiple_of(k * 64 + ia * 16, 16)

    def split(parts, h):
        return sum(jnp.where(hh == h, part, 0.0) for hh, part in zip(ghalf, parts))

    def bases_1():
        at["g1"] = send(gt.at[pl.ds(pl.multiple_of((1 - k) * 64, 64), 64)], rg1, t1.at[0], v1.at[0], other_core)

    def bases_2():
        at["g1"].wait_recv()
        rg1[...] += gt[pl.ds(pl.multiple_of(k * 64, 64), 64), :]
        for d in range(1, 4):
            rows = pl.multiple_of(lax.rem(ia + d, 4) * 16, 16)
            at["g2", d] = send(rg1.at[pl.ds(rows, 16)], rg2.at[d - 1], t2.at[d - 1], v2.at[d - 1], ring_a(d))

    def bases_3():
        for d in range(1, 4):
            at["g2", d].wait_recv()
        gp = [rg1[pl.ds(pl.multiple_of(ia * 16, 16), 16), :]] + [rg2[d] for d in range(3)]
        pg2[:, 0:128] = sum(p[:, 128:256] for p in gp)
        for h in range(2):
            pg2[:, 128 + h * 128:256 + h * 128] = split([p[:, 256:384] for p in gp], h)
            pg2[:, 384 + h * 128:512 + h * 128] = split([p[:, 0:128] for p in gp], h)
        for e in range(1, 4):
            at["g3", e] = send(pg2, rg3.at[e - 1], t3.at[e - 1], v3.at[e - 1], ring_b(e))
        for e in range(4):
            at["g3", 4 + e] = send(pg2.at[:, pl.ds(0, 128)], rg3x.at[e], t3x.at[e], v3x.at[e], ring_b(e, sibling))

    def bases_4():
        for e in range(1, 8):
            at["g3", e].wait_recv()
        gfull[pl.ds(grows, 16), 0:640] = pg2[...] + rg3[0] + rg3[1] + rg3[2]
        gfull[pl.ds(grows, 16), 640:768] = rg3x[0] + rg3x[1] + rg3x[2] + rg3x[3]
        for d in range(1, 4):
            part = gfull.at[pl.ds(grows, 16)]
            at["g4", d] = send(part, part, t4.at[d - 1], v4.at[d - 1], ring_a(d))

    def bases_5():
        for d in range(1, 4):
            at["g4", d].wait_recv()
        part = gfull.at[pl.ds(pl.multiple_of(k * 64, 64), 64)]
        at["g5"] = send(part, part, t5.at[0], v5.at[0], other_core)

    def permute_rows(leaf):
        if leaf == 0:
            aload.wait()
        for j in range(6):
            ash[j] = av[leaf, :, pl.ds(j * 128, 128)].astype(F32)
        for j in range(6):
            for c in range(3):
                ap[leaf, pl.ds(c * 256, 256), pl.ds(j * 128, 128)] = (
                    ash[j, pl.ds(c, 256, stride=3), :].astype(BF))

    def multiply(leaf, n):
        cols = pl.ds(n * 256, 256)
        f = jnp.dot(ap[leaf], xb[leaf, :, :, cols].reshape(768, 256), preferred_element_type=F32)
        field[:, pl.ds(leaf * 256, 256), cols] = f.reshape(3, 256, 256)

    pieces = [lambda: expand(1), lambda: expand(2)]
    for leaf in range(4):
        pieces += [lambda leaf=leaf: gather(leaf), lambda leaf=leaf: repack(leaf), lambda leaf=leaf: permute_rows(leaf)]
        pieces += [lambda leaf=leaf, n=n: multiply(leaf, n) for n in range(4)]

    def work(count):
        for _ in range(min(count, len(pieces))):
            pieces.pop(0)()

    def dot(a, b):
        return lax.dot_general(a, b, (((1,), (0,)), ((), ())), precision=HIGH, preferred_element_type=F32)

    def dot_t(a, b):
        return lax.dot_general(a, b, (((1,), (1,)), ((), ())), precision=HIGH, preferred_element_type=F32)

    def rounded(a):
        return a.astype(BF).astype(F32)

    def pair(own_first, own, other):
        return jnp.concatenate([jnp.where(own_first, own, other), jnp.where(own_first, other, own)], axis=1)

    def widen(part, hh):
        last = part[:, 256:384]
        return jnp.concatenate([part[:, 0:256], jnp.where(hh == 0, last, 0.0), jnp.where(hh == 1, last, 0.0)], axis=1)

    def narrow(block, hh):
        return jnp.concatenate([block[:, 0:256], jnp.where(hh == 0, block[:, 256:384], block[:, 384:512])], axis=1)

    lower, upper = pl.ds(0, RING // 2), pl.ds(RING // 2, RING // 2)

    def block_rows(ch, core, t, rows):
        return pl.ds(pl.multiple_of(ch * WIDE + core * CORE + t * RING, rows), rows)

    def to_core(ch):
        for d in (2, 1, 3, 0):
            src = st.at[block_rows(ch, 1 - k, lax.rem(ib + d, 4), RING)]
            at["c1", ch, d] = send(src, r1.at[ch, d], s1.at[ch, d], q1.at[ch, d], other_core)

    def to_ring_a(ch):
        for d in (2, 1, 3, 0):
            at["c1", ch, d].wait_recv()
            r1[ch, d] += st[block_rows(ch, k, lax.rem(ia + d, 4), RING), :]
            if d == 2:
                at["ra", ch] = send(r1.at[ch, 2, upper], ra.at[ch], s2.at[ch, 0], q2.at[ch, 0], ring_a(3))
                at["ro", ch] = send(r1.at[ch, 2, lower], ro.at[ch], s2.at[ch, 1], q2.at[ch, 1], ring_a(2))
            elif d == 1:
                at["r2", ch] = send(r1.at[ch, 1], r2.at[ch], s2.at[ch, 2], q2.at[ch, 2], ring_a(1))
            elif d == 3:
                at["rb", ch] = send(r1.at[ch, 3, lower], rb.at[ch], s2.at[ch, 3], q2.at[ch, 3], ring_a(3))

    def along_ring_a(ch):
        at["ra", ch].wait_recv()
        x3[ch] = widen(r1[ch, 3, upper], half) + widen(ra[ch], half_of[1])
        at["rc", ch] = send(x3.at[ch], rc.at[ch], s2.at[ch, 4], q2.at[ch, 4], ring_a(3))

    def to_ring_b(ch):
        for name in ("r2", "ro", "rb"):
            at[name, ch].wait_recv()
        p2[ch, lower] = (widen(r1[ch, 0, lower], half) + widen(r2[ch, lower], half_of[3])
                         + widen(ro[ch], half_of[2]) + widen(rb[ch], half_of[1]))
        at["rc", ch].wait_recv()
        p2[ch, upper] = widen(r1[ch, 0, upper], half) + widen(r2[ch, upper], half_of[3]) + rc[ch]
        for e in (2, 1, 3):
            rows = pl.ds(pl.multiple_of(lax.rem(ib + e, 4) * OWN, OWN), OWN)
            at["c3", ch, e] = send(p2.at[ch, rows], r3.at[ch, e - 1], s3.at[ch, e - 1], q3.at[ch, e - 1], ring_b(e))

    def to_x(ch):
        for e in (1, 2, 3):
            at["c3", ch, e].wait_recv()
        rows = pl.ds(pl.multiple_of(ib * OWN, OWN), OWN)
        p4[ch] = p2[ch, rows, :] + r3[ch, 0] + r3[ch, 1] + r3[ch, 2]
        for i, lanes in ((2, 128), (1, 128), (0, 256)):
            at["c4", ch, i] = send(p4.at[ch, :, pl.ds(0, lanes)], r4.at[ch, i, :, pl.ds(0, lanes)],
                                   s4.at[ch, i], q4.at[ch, i], xs[i])

    def small_systems(ch):
        if ch == 0:
            cload.wait()
            at["g5"].wait_recv()
        for i in range(3):
            at["c4", ch, i].wait_recv()
        top = x // 2
        odd = lax.rem(x, 2)
        own0 = p4[ch, :, 0:128] + r4[ch, 0, :, 0:128]
        far0 = r4[ch, 1, :, 0:128] + r4[ch, 2, :, 0:128]
        w0 = rounded(dot_t(pair(top == 0, own0, far0), cp[0, pl.ds(pl.multiple_of(top * 128, 128), 128), :]))
        own1 = p4[ch, :, 128:256] - dot(w0, gfull[:, 0:128])
        far1 = r4[ch, 0, :, 128:256] - dot(w0, gfull[:, 640:768])
        w1 = rounded(dot_t(pair(odd == 0, own1, far1), cp[1, pl.ds(pl.multiple_of(odd * 128, 128), 128), :]))
        both = [p4[ch, :, 256 + h * 128:384 + h * 128] - dot(w0, gfull[:, 128 + h * 128:256 + h * 128])
                - dot(w1, gfull[:, 384 + h * 128:512 + h * 128]) for h in range(2)]
        w2 = rounded(dot_t(jnp.concatenate(both, axis=1), cp[2]))
        rows = pl.ds(pl.multiple_of(ib * OWN, OWN), OWN)
        wf[ch, rows, 0:128] = w0
        wf[ch, rows, 128:256] = w1
        wf[ch, rows, 256:512] = w2
        part = wf.at[ch, rows]
        for e in (2, 1, 3):
            at["c5", ch, e] = send(part, part, s5.at[ch, e - 1], q5.at[ch, e - 1], ring_b(e))

    def to_partner(ch, d):
        part = w.at[block_rows(ch, k, lax.rem(ia + d, 4), RING)]
        at["c7", ch, d] = send(part, part, s7.at[ch, d], q7.at[ch, d], other_core)

    def half_rows(ch, d, top):
        start = ch * WIDE + k * CORE + lax.rem(ia + d, 4) * RING + top * (RING // 2)
        return pl.ds(pl.multiple_of(start, RING // 2), RING // 2)

    def back_ring_a(ch):
        for e in (1, 2, 3):
            at["c5", ch, e].wait_recv()
        at["fa", ch] = send(wf.at[ch, upper], fa.at[ch], s6.at[ch, 0], q6.at[ch, 0], ring_a(3))
        for h in range(2):
            nv[ch, h] = narrow(wf[ch], h)
        rows, low = block_rows(ch, k, ia, RING), half_rows(ch, 0, 0)
        at["c6", ch, 2] = send(nv.at[ch, half_of[2], lower], w.at[low], s6.at[ch, 1], q6.at[ch, 1], ring_a(2))
        at["c6", ch, 1] = send(nv.at[ch, half_of[1]], w.at[rows], s6.at[ch, 2], q6.at[ch, 2], ring_a(1))
        at["c6", ch, 3] = send(nv.at[ch, half_of[3], lower], w.at[low], s6.at[ch, 3], q6.at[ch, 3], ring_a(3))
        w[rows, :] = narrow(wf[ch], half)
        to_partner(ch, 0)

    def back_along(ch):
        at["fa", ch].wait_recv()
        fw[ch] = narrow(fa[ch], half_of[3])
        rows = half_rows(ch, 1, 1)
        at["fw", ch] = send(fw.at[ch], w.at[rows], s6.at[ch, 4], q6.at[ch, 4], ring_a(3))
        w[rows, :] = narrow(fa[ch], half)

    def back_core(ch):
        at["c6", ch, 1].wait_recv()
        to_partner(ch, 3)
        at["c6", ch, 3].wait_recv()
        to_partner(ch, 1)
        at["c6", ch, 2].wait_recv()
        at["fw", ch].wait_recv()
        to_partner(ch, 2)

    bases_1()
    to_core(0)
    to_core(1)
    work(1)
    bases_2()
    to_ring_a(0)
    to_ring_a(1)
    work(2)
    along_ring_a(0)
    bases_3()
    work(1)
    along_ring_a(1)
    work(5)
    to_ring_b(0)
    work(1)
    to_ring_b(1)
    bases_4()
    work(4)
    to_x(0)
    work(3)
    to_x(1)
    work(1)
    bases_5()
    small_systems(0)
    small_systems(1)
    work(5)
    back_ring_a(0)
    work(1)
    back_ring_a(1)
    work(1)
    back_along(0)
    work(3)
    back_along(1)
    work(99)
    back_core(0)
    back_core(1)
    work(99)
    for ch in range(CHUNKS):
        for d in range(4):
            at["c7", ch, d].wait_recv()
    for copy in sends:
        copy.wait_send()


def solve(order, x, a, st, gt, cp):
    vm = pl.BlockSpec(memory_space=pltpu.VMEM)
    hbm = pl.BlockSpec(memory_space=pl.ANY)
    dma = pltpu.SemaphoreType.DMA

    def shape(*dims):
        return pltpu.VMEM(dims, F32)

    n = CHUNKS
    sems = [(4,), (3, 4)]
    for s in [(n, 4), (n, 5), (n, 3), (n, 3), (n, 3), (n, 5), (n, 4), (1,), (3,), (3,), (4,), (3,), (1,)]:
        sems += [s, s]
    return pl.pallas_call(
        solve_kernel,
        out_shape=[pltpu.VMEM((3, 1024, 1024), F32), pltpu.VMEM((1024, 384), F32)],
        in_specs=[pl.BlockSpec(memory_space=pltpu.SMEM), hbm, hbm, vm, vm, hbm],
        out_specs=[vm, vm],
        scratch_shapes=[
            pltpu.VMEM((4, 3, 256, 1024), BF), pltpu.VMEM((4, 768, 768), BF), pltpu.VMEM((4, 768, 768), BF),
            shape(3, 1024, 8, 128), shape(6144, 128), shape(6, 768, 128), shape(3, 256, 256),
            shape(n, 4, RING, 384), shape(n, RING, 384), shape(n, RING // 2, 384), shape(n, RING // 2, 384),
            shape(n, RING // 2, 384), shape(n, RING // 2, 512), shape(n, RING // 2, 512), shape(n, RING, 512),
            shape(n, 3, OWN, 512), shape(n, OWN, 512), shape(n, 3, OWN, 256), shape(n, RING, 512),
            shape(n, 2, RING, 384), shape(n, RING // 2, 512), shape(n, RING // 2, 384),
            shape(64, 384), shape(3, 16, 384), shape(16, 640), shape(3, 16, 640), shape(4, 16, 128), shape(128, 768),
        ] + [dma(s) for s in sems],
        compiler_params=pltpu.CompilerParams(vmem_limit_bytes=42 * MIB, collective_id=0, has_side_effects=True),
        name="leaf_solve_and_levels",
    )(order, x, a, st, gt, cp)


ROWS = 512


def update_kernel(field, u_hbm, wt, out, u, w, buf, usem, sem):
    loads = {}
    for c in range(3):
        for level in range(3):
            loads[c, level] = pltpu.make_async_copy(
                u_hbm.at[level, c], u.at[c, :, pl.ds(level * 128, 128)], usem.at[c, level])
            loads[c, level].start()
    w[...] = (-wt[...].T).astype(BF)
    copies = []
    for c in range(3):
        for level in range(3):
            loads[c, level].wait()
        for r in range(1024 // ROWS):
            rows = pl.ds(r * ROWS, ROWS)
            i = len(copies)
            slot = i % 4
            if i >= 4:
                copies[i - 4].wait()
            buf[slot] = field[c, rows, :] + jnp.dot(u[c, rows, :], w[...], preferred_element_type=F32)
            copies.append(pltpu.make_async_copy(buf.at[slot], out.at[c, rows, :], sem.at[slot]))
            copies[-1].start()
    for copy in copies[-4:]:
        copy.wait()


def update(field, u, wt):
    vm = pl.BlockSpec(memory_space=pltpu.VMEM)
    hbm = pl.BlockSpec(memory_space=pl.ANY)
    return pl.pallas_call(
        update_kernel,
        out_shape=jax.ShapeDtypeStruct((3, 1024, 1024), F32),
        in_specs=[vm, hbm, vm],
        out_specs=hbm,
        scratch_shapes=[
            pltpu.VMEM((3, 1024, 384), BF),
            pltpu.VMEM((384, 1024), BF),
            pltpu.VMEM((4, ROWS, 1024), F32),
            pltpu.SemaphoreType.DMA((3, 3)),
            pltpu.SemaphoreType.DMA((4,)),
        ],
        compiler_params=pltpu.CompilerParams(vmem_limit_bytes=20 * MIB),
        name="update",
    )(field, u, wt)


def body(right_sides, panel_order, leaf_inverse, test_basis, update_basis, coupling):
    sides = jnp.transpose(right_sides, (1, 0, 2))
    test = jnp.transpose(test_basis, (0, 2, 1, 3))
    upd = jnp.transpose(update_basis, (0, 2, 1, 3))
    st, gt = project(panel_order, sides, leaf_inverse, test, upd)
    field, w = solve(panel_order, sides, leaf_inverse, in_vmem(st), in_vmem(gt), coupling.reshape(3, 256, 256))
    out = update(in_vmem(field), upd, in_vmem(w))
    return jnp.transpose(out, (1, 0, 2))


def solution(mesh):
    in_specs = (
        P(("leaf", "sub"), None, None),
        P(("leaf", "sub")),
        P(("leaf", "sub"), None, None),
        P(None, ("leaf", "sub"), None, None),
        P(None, ("leaf", "sub"), None, None),
        P(None, "leaf", None, None),
    )
    out_specs = P(("leaf", "sub"), None, None)
    return jax.shard_map(body, mesh=mesh, in_specs=in_specs, out_specs=out_specs, check_vma=False)
```

```python
import jax
import jax.numpy as jnp
from jax import lax
from jax.experimental import pallas as pl
from jax.experimental.pallas import tpu as pltpu
from jax.sharding import PartitionSpec as P

BF = jnp.bfloat16
F32 = jnp.float32
MIB = 1 << 20
MESH = pl.DeviceIdType.MESH
HIGH = lax.Precision.HIGHEST
CHUNKS = 2
WIDE = 1024 // CHUNKS
CORE = WIDE // 2
RING = CORE // 4
OWN = RING // 4


def in_vmem(a):
    return pltpu.with_memory_space_constraint(a, pltpu.VMEM)


def solve_kernel(order, order_hbm, x_hbm, a_hbm, v_hbm, u_hbm, cp_hbm, field, w,
                 xb, av, ap, xf, xg, cp, st, gt, vv, uv, vit, bt, acc, ov, iv, inverse,
                 r1, r2, p2, r3, p4, r4, wf, nv,
                 rg1, rg2, pg2, rg3, rg3x, gfull,
                 lsem, xsem, s1, q1, s2, q2, s3, q3, s4, q4, s5, q5, s6, q6, s7, q7,
                 t1, v1, t2, v2, t3, v3, t3x, v3x, t4, v4, t5, v5, asem, isem):
    place = lax.axis_index("leaf")
    z = lax.axis_index("sub")
    k = lax.rem(place, 2)
    y = lax.rem(place // 2, 4)
    x = place // 8
    ia = jnp.where(k == 0, z, y)
    ib = jnp.where(k == 0, y, z)
    half = y // 2

    def device(xx, yy, kk, zz):
        return ((xx * 4 + yy) * 2 + kk, zz)

    def ring_a(d):
        t = lax.rem(ia + d, 4)
        return device(x, jnp.where(k == 0, y, t), k, jnp.where(k == 0, t, z))

    def ring_b(e, xx=None):
        t = lax.rem(ib + e, 4)
        return device(x if xx is None else xx, jnp.where(k == 0, t, y), k, jnp.where(k == 0, z, t))

    sibling = x + 1 - 2 * lax.rem(x, 2)
    other_core = device(x, y, 1 - k, z)
    xs = [device(xx, y, k, z) for xx in (sibling, lax.rem(x + 2, 4), lax.rem(sibling + 2, 4))]
    half_of = {d: jnp.where(k == 0, half, lax.rem(y + d, 4) // 2) for d in (1, 2, 3)}
    half_of[0] = half
    sends = []

    def send(src, dst, ssem, rsem, where):
        copy = pltpu.make_async_remote_copy(src_ref=src, dst_ref=dst, send_sem=ssem, recv_sem=rsem,
                                            device_id=where, device_id_type=MESH)
        copy.start()
        sends.append(copy)
        return copy

    def load(src, dst, sem):
        copy = pltpu.make_async_copy(src, dst, sem)
        copy.start()
        return copy

    vload = load(v_hbm, vv, lsem.at[0])
    oload = load(order_hbm, ov, lsem.at[1])
    aloads = [load(a_hbm.at[leaf], av.at[leaf], asem.at[leaf]) for leaf in range(4)]
    uload = load(u_hbm.at[pl.ds(0, 2)], uv, lsem.at[2])
    xloads = {}
    for c in range(3):
        for q in range(4):
            xloads[c, q] = load(x_hbm.at[c, pl.ds(q * 256, 256), :], xb.at[q, c], xsem.at[c, q])
    cload = load(cp_hbm, cp, lsem.at[3])

    partners = [other_core] + xs
    for d in range(1, 4):
        partners += [ring_a(d), ring_b(d), ring_b(d, sibling)]
    barrier = pltpu.get_barrier_semaphore()
    for where in partners:
        pl.semaphore_signal(barrier, inc=1, device_id=where, device_id_type=MESH)

    oload.wait()
    places = lax.bitwise_and(ov[...], 1023).T
    panel = lax.broadcasted_iota(jnp.int32, (128, 1024), 1)
    position = lax.broadcasted_iota(jnp.int32, (128, 1024), 0)
    found = jnp.zeros((1, 1024), jnp.int32)
    for r in range(8):
        hit = places[:, r:r + 1] == panel
        found += jnp.sum(jnp.where(hit, position + r * 128, 0), axis=0, keepdims=True)
    found = jnp.minimum(found, 1023)
    for r in range(8):
        iv[r:r + 1, :] = found[:, r * 128:r * 128 + 128]
    icopy = load(iv, inverse, isem.at[0])

    vload.wait()
    for leaf in range(4):
        for level in range(3):
            for c in range(3):
                xg[pl.ds(level * 768 + c, 256, stride=3), :] = vv[level, c, pl.ds(leaf * 256, 256), :].astype(F32)
        for level in range(3):
            vit[leaf, pl.ds(level * 128, 128), :] = xg[pl.ds(level * 768, 768), :].astype(BF).T
    frows = field.reshape(24576, 128)
    ftiles = field.reshape(3072, 8, 128)
    for leaf in range(4):
        aloads[leaf].wait()
        b = jnp.dot(vit[leaf], av[leaf], preferred_element_type=F32)
        for level in range(3):
            frows[pl.ds(leaf * 6144 + level, 768, stride=8), :] = b[level * 128:level * 128 + 128].T
    uload.wait()
    g0 = jnp.zeros((128, 256), F32)
    g1 = jnp.zeros((128, 128), F32)
    over_rows = (((0,), (0,)), ((), ()))
    for c in range(3):
        v12 = jnp.concatenate([vv[1, c], vv[2, c]], axis=1)
        g0 += lax.dot_general(uv[0, c], v12, over_rows, preferred_element_type=F32)
        g1 += lax.dot_general(uv[1, c], vv[2, c], over_rows, preferred_element_type=F32)
    gt[:, 0:128] = g1
    gt[:, 128:384] = g0

    xrows = xf.reshape(24576, 128)

    def expand(c):
        @pl.loop(0, 64, unroll=4)
        def _(i):
            q = i // 16
            rows = xb[q, c, pl.ds(pl.multiple_of(lax.rem(i, 16) * 16, 16), 16), :].astype(F32)
            for h in range(2):
                for j in range(8):
                    xrows[pl.ds(c * 8192 + i * 128 + h * 64 + j, 8, stride=8), :] = (
                        rows[h * 8:h * 8 + 8, j * 128:j * 128 + 128])

    def gather(leaf):
        @pl.loop(0, 16, unroll=2)
        def _(i):
            for kk in range(16):
                p = i * 16 + kk
                src = lax.bitwise_and(order[leaf * 256 + p], 1023)
                for c in range(3):
                    xg[pl.ds(pl.multiple_of(p * 24 + c * 8, 8), 8), :] = xf[c, src]

    def repack(leaf):
        @pl.loop(0, 48, unroll=4)
        def _(i):
            c = i // 16
            off = pl.multiple_of(lax.rem(i, 16) * 16, 16)
            for j in range(8):
                lo = xg[pl.ds(i * 128 + j, 8, stride=8), :]
                hi = xg[pl.ds(i * 128 + 64 + j, 8, stride=8), :]
                xb[leaf, c, pl.ds(off, 16), pl.ds(j * 128, 128)] = jnp.concatenate([lo, hi], axis=0).astype(BF)

    def to_panels(part):
        @pl.loop(part * 32, part * 32 + 32)
        def _(i):
            for j in range(16):
                q = i * 16 + j
                src = inverse[i // 8, lax.rem(i, 8) * 16 + j] * 3
                for c in range(3):
                    xrows[pl.ds(pl.multiple_of(c * 8192 + q * 8, 8), 8), :] = ftiles[src + c]

    def basis_rows(c):
        for level in range(3):
            bt[pl.ds(level * 128, 128), pl.ds(c * 1024, 1024)] = (
                xrows[pl.ds(c * 8192 + level, 1024, stride=8), :].astype(BF).T)

    def project(c, ch):
        if ch == 0:
            for q in range(4):
                xloads[c, q].wait()
        cols = pl.ds(ch * WIDE, WIDE)
        part = jnp.dot(bt[:, pl.ds(c * 1024, 1024)], xb[:, c, :, cols].reshape(1024, WIDE), preferred_element_type=F32)
        if c == 0:
            acc[...] = part
        elif c == 1:
            acc[...] += part
        else:
            st[cols, :] = (acc[...] + part).T

    pl.semaphore_wait(barrier, len(partners))
    at = {}
    ghalf = [half] + [half_of[4 - d] for d in range(1, 4)]
    grows = pl.multiple_of(k * 64 + ia * 16, 16)

    def split(parts, h):
        return sum(jnp.where(hh == h, part, 0.0) for hh, part in zip(ghalf, parts))

    def bases_1():
        at["g1"] = send(gt.at[pl.ds(pl.multiple_of((1 - k) * 64, 64), 64)], rg1, t1.at[0], v1.at[0], other_core)

    def bases_2():
        at["g1"].wait_recv()
        rg1[...] += gt[pl.ds(pl.multiple_of(k * 64, 64), 64), :]
        for d in range(1, 4):
            rows = pl.multiple_of(lax.rem(ia + d, 4) * 16, 16)
            at["g2", d] = send(rg1.at[pl.ds(rows, 16)], rg2.at[d - 1], t2.at[d - 1], v2.at[d - 1], ring_a(d))

    def bases_3():
        for d in range(1, 4):
            at["g2", d].wait_recv()
        gp = [rg1[pl.ds(pl.multiple_of(ia * 16, 16), 16), :]] + [rg2[d] for d in range(3)]
        pg2[:, 0:128] = sum(p[:, 128:256] for p in gp)
        for h in range(2):
            pg2[:, 128 + h * 128:256 + h * 128] = split([p[:, 256:384] for p in gp], h)
            pg2[:, 384 + h * 128:512 + h * 128] = split([p[:, 0:128] for p in gp], h)
        for e in range(1, 4):
            at["g3", e] = send(pg2, rg3.at[e - 1], t3.at[e - 1], v3.at[e - 1], ring_b(e))
        for e in range(4):
            at["g3", 4 + e] = send(pg2.at[:, pl.ds(0, 128)], rg3x.at[e], t3x.at[e], v3x.at[e], ring_b(e, sibling))

    def bases_4():
        for e in range(1, 8):
            at["g3", e].wait_recv()
        gfull[pl.ds(grows, 16), 0:640] = pg2[...] + rg3[0] + rg3[1] + rg3[2]
        gfull[pl.ds(grows, 16), 640:768] = rg3x[0] + rg3x[1] + rg3x[2] + rg3x[3]
        for d in range(1, 4):
            part = gfull.at[pl.ds(grows, 16)]
            at["g4", d] = send(part, part, t4.at[d - 1], v4.at[d - 1], ring_a(d))

    def bases_5():
        for d in range(1, 4):
            at["g4", d].wait_recv()
        part = gfull.at[pl.ds(pl.multiple_of(k * 64, 64), 64)]
        at["g5"] = send(part, part, t5.at[0], v5.at[0], other_core)

    def permute_rows(leaf):
        for j in range(6):
            xg[pl.ds(j * 768, 768), :] = av[leaf, :, pl.ds(j * 128, 128)].astype(F32)
        for j in range(6):
            for c in range(3):
                ap[leaf, pl.ds(c * 256, 256), pl.ds(j * 128, 128)] = (
                    xg[pl.ds(j * 768 + c, 256, stride=3), :].astype(BF))

    def multiply(leaf, n):
        cols = pl.ds(n * 256, 256)
        f = jnp.dot(ap[leaf], xb[leaf, :, :, cols].reshape(768, 256), preferred_element_type=F32)
        for j in range(2):
            field[:, n * 2 + j, pl.ds(leaf * 256, 256), :] = f[:, j * 128:j * 128 + 128].reshape(3, 256, 128)

    pieces = [lambda c=c: expand(c) for c in range(3)]
    for leaf in range(4):
        pieces += [lambda leaf=leaf: gather(leaf), lambda leaf=leaf: repack(leaf), lambda leaf=leaf: permute_rows(leaf)]
        pieces += [lambda leaf=leaf, n=n: multiply(leaf, n) for n in range(4)]

    def work(count):
        for _ in range(min(count, len(pieces))):
            pieces.pop(0)()

    def dot(a, b):
        return lax.dot_general(a, b, (((1,), (0,)), ((), ())), precision=HIGH, preferred_element_type=F32)

    def dot_t(a, b):
        return lax.dot_general(a, b, (((1,), (1,)), ((), ())), precision=HIGH, preferred_element_type=F32)

    def rounded(a):
        return a.astype(BF).astype(F32)

    def pair(own_first, own, other):
        return jnp.concatenate([jnp.where(own_first, own, other), jnp.where(own_first, other, own)], axis=1)

    def widen(part, hh):
        last = part[:, 256:384]
        return jnp.concatenate([part[:, 0:256], jnp.where(hh == 0, last, 0.0), jnp.where(hh == 1, last, 0.0)], axis=1)

    def narrow(block, hh):
        return jnp.concatenate([block[:, 0:256], jnp.where(hh == 0, block[:, 256:384], block[:, 384:512])], axis=1)

    def block_rows(ch, core, t, rows):
        return pl.ds(pl.multiple_of(ch * WIDE + core * CORE + t * RING, rows), rows)

    def to_core(ch):
        for d in (2, 1, 3, 0):
            src = st.at[block_rows(ch, 1 - k, lax.rem(ib + d, 4), RING)]
            at["c1", ch, d] = send(src, r1.at[ch, d], s1.at[ch, d], q1.at[ch, d], other_core)

    def to_ring_a(ch):
        for d in (2, 1, 3, 0):
            at["c1", ch, d].wait_recv()
            r1[ch, d] += st[block_rows(ch, k, lax.rem(ia + d, 4), RING), :]
            if d:
                at["c2", ch, d] = send(r1.at[ch, d], r2.at[ch, d - 1], s2.at[ch, d - 1], q2.at[ch, d - 1], ring_a(d))

    def to_ring_b(ch):
        for d in (1, 2, 3):
            at["c2", ch, d].wait_recv()
        total = widen(r1[ch, 0], half)
        for d in (1, 2, 3):
            total += widen(r2[ch, d - 1], half_of[4 - d])
        p2[ch] = total
        for e in (2, 1, 3):
            rows = pl.ds(pl.multiple_of(lax.rem(ib + e, 4) * OWN, OWN), OWN)
            at["c3", ch, e] = send(p2.at[ch, rows], r3.at[ch, e - 1], s3.at[ch, e - 1], q3.at[ch, e - 1], ring_b(e))

    def to_x(ch):
        for e in (1, 2, 3):
            at["c3", ch, e].wait_recv()
        rows = pl.ds(pl.multiple_of(ib * OWN, OWN), OWN)
        p4[ch] = p2[ch, rows, :] + r3[ch, 0] + r3[ch, 1] + r3[ch, 2]
        for i, lanes in ((2, 128), (1, 128), (0, 256)):
            at["c4", ch, i] = send(p4.at[ch, :, pl.ds(0, lanes)], r4.at[ch, i, :, pl.ds(0, lanes)],
                                   s4.at[ch, i], q4.at[ch, i], xs[i])

    def small_systems(ch):
        if ch == 0:
            cload.wait()
            at["g5"].wait_recv()
        for i in range(3):
            at["c4", ch, i].wait_recv()
        top = x // 2
        odd = lax.rem(x, 2)
        own0 = p4[ch, :, 0:128] + r4[ch, 0, :, 0:128]
        far0 = r4[ch, 1, :, 0:128] + r4[ch, 2, :, 0:128]
        w0 = rounded(dot_t(pair(top == 0, own0, far0), cp[0, pl.ds(pl.multiple_of(top * 128, 128), 128), :]))
        own1 = p4[ch, :, 128:256] - dot(w0, gfull[:, 0:128])
        far1 = r4[ch, 0, :, 128:256] - dot(w0, gfull[:, 640:768])
        w1 = rounded(dot_t(pair(odd == 0, own1, far1), cp[1, pl.ds(pl.multiple_of(odd * 128, 128), 128), :]))
        both = [p4[ch, :, 256 + h * 128:384 + h * 128] - dot(w0, gfull[:, 128 + h * 128:256 + h * 128])
                - dot(w1, gfull[:, 384 + h * 128:512 + h * 128]) for h in range(2)]
        w2 = rounded(dot_t(jnp.concatenate(both, axis=1), cp[2]))
        rows = pl.ds(pl.multiple_of(ib * OWN, OWN), OWN)
        wf[ch, rows, 0:128] = w0
        wf[ch, rows, 128:256] = w1
        wf[ch, rows, 256:512] = w2
        part = wf.at[ch, rows]
        for e in (2, 1, 3):
            at["c5", ch, e] = send(part, part, s5.at[ch, e - 1], q5.at[ch, e - 1], ring_b(e))

    def to_partner(ch, d):
        part = w.at[block_rows(ch, k, lax.rem(ia + d, 4), RING)]
        at["c7", ch, d] = send(part, part, s7.at[ch, d], q7.at[ch, d], other_core)

    def back_ring_a(ch):
        for e in (1, 2, 3):
            at["c5", ch, e].wait_recv()
        for h in range(2):
            nv[ch, h] = narrow(wf[ch], h)
        rows = block_rows(ch, k, ia, RING)
        for d in (2, 1, 3):
            at["c6", ch, d] = send(nv.at[ch, half_of[d]], w.at[rows], s6.at[ch, d - 1], q6.at[ch, d - 1], ring_a(d))
        w[rows, :] = narrow(wf[ch], half)
        to_partner(ch, 0)

    def back_core(ch):
        for d in (1, 3, 2):
            at["c6", ch, d].wait_recv()
            to_partner(ch, 4 - d)

    bases_1()
    icopy.wait()
    to_panels(0)
    bases_2()
    to_panels(1)
    for c in range(3):
        basis_rows(c)
        project(c, 0)
        if c == 1:
            bases_3()
    to_core(0)
    for c in range(3):
        project(c, 1)
    to_core(1)
    to_ring_a(0)
    work(1)
    to_ring_a(1)
    bases_4()
    work(4)
    to_ring_b(0)
    bases_5()
    work(6)
    to_ring_b(1)
    work(1)
    to_x(0)
    work(6)
    to_x(1)
    work(1)
    small_systems(0)
    work(3)
    small_systems(1)
    work(4)
    back_ring_a(0)
    work(3)
    back_ring_a(1)
    work(99)
    back_core(0)
    back_core(1)
    work(99)
    for ch in range(CHUNKS):
        for d in range(4):
            at["c7", ch, d].wait_recv()
    for copy in sends:
        copy.wait_send()


def solve(order, x, a, v, u, cp):
    vm = pl.BlockSpec(memory_space=pltpu.VMEM)
    hbm = pl.BlockSpec(memory_space=pl.ANY)
    dma = pltpu.SemaphoreType.DMA

    def shape(*dims):
        return pltpu.VMEM(dims, F32)

    n = CHUNKS
    sems = [(4,), (3, 4)]
    for s in [(n, 4), (n, 3), (n, 3), (n, 3), (n, 3), (n, 3), (n, 4), (1,), (3,), (3,), (4,), (3,), (1,)]:
        sems += [s, s]
    return pl.pallas_call(
        solve_kernel,
        out_shape=[pltpu.VMEM((3, 8, 1024, 128), F32), pltpu.VMEM((1024, 384), F32)],
        in_specs=[pl.BlockSpec(memory_space=pltpu.SMEM), hbm, hbm, hbm, hbm, hbm, hbm],
        out_specs=[vm, vm],
        scratch_shapes=[
            pltpu.VMEM((4, 3, 256, 1024), BF), pltpu.VMEM((4, 768, 768), BF), pltpu.VMEM((4, 768, 768), BF),
            shape(3, 1024, 8, 128), shape(6144, 128), shape(3, 256, 256), shape(1024, 384), shape(128, 384),
            pltpu.VMEM((3, 3, 1024, 128), BF), pltpu.VMEM((2, 3, 1024, 128), BF), pltpu.VMEM((4, 384, 768), BF),
            pltpu.VMEM((384, 3072), BF), shape(384, WIDE), pltpu.VMEM((8, 128), jnp.int32),
            pltpu.VMEM((8, 128), jnp.int32), pltpu.SMEM((8, 128), jnp.int32),
            shape(n, 4, RING, 384), shape(n, 3, RING, 384), shape(n, RING, 512),
            shape(n, 3, OWN, 512), shape(n, OWN, 512), shape(n, 3, OWN, 256), shape(n, RING, 512),
            shape(n, 2, RING, 384),
            shape(64, 384), shape(3, 16, 384), shape(16, 640), shape(3, 16, 640), shape(4, 16, 128), shape(128, 768),
        ] + [dma(s) for s in sems] + [dma((4,)), dma((1,))],
        compiler_params=pltpu.CompilerParams(vmem_limit_bytes=48 * MIB, collective_id=0, has_side_effects=True),
        name="leaf_solve_and_levels",
    )(order, order.reshape(8, 128), x, a, v, u, cp)


ROWS = 512


def update_kernel(field, u_hbm, wt, out, u, w, buf, usem, sem):
    loads = {}
    for c in range(3):
        for level in range(3):
            loads[c, level] = pltpu.make_async_copy(
                u_hbm.at[level, c], u.at[c, :, pl.ds(level * 128, 128)], usem.at[c, level])
            loads[c, level].start()
    w[...] = (-wt[...].T).astype(BF)
    copies = []
    for c in range(3):
        for level in range(3):
            loads[c, level].wait()
        for r in range(1024 // ROWS):
            rows = pl.ds(r * ROWS, ROWS)
            i = len(copies)
            slot = i % 4
            if i >= 4:
                copies[i - 4].wait()
            change = jnp.dot(u[c, rows, :], w[...], preferred_element_type=F32)
            for j in range(8):
                lanes = slice(j * 128, j * 128 + 128)
                buf[slot, :, lanes] = field[c, j, rows, :] + change[:, lanes]
            copies.append(pltpu.make_async_copy(buf.at[slot], out.at[c, rows, :], sem.at[slot]))
            copies[-1].start()
    for copy in copies[-4:]:
        copy.wait()


def update(field, u, wt):
    vm = pl.BlockSpec(memory_space=pltpu.VMEM)
    hbm = pl.BlockSpec(memory_space=pl.ANY)
    return pl.pallas_call(
        update_kernel,
        out_shape=jax.ShapeDtypeStruct((3, 1024, 1024), F32),
        in_specs=[vm, hbm, vm],
        out_specs=hbm,
        scratch_shapes=[
            pltpu.VMEM((3, 1024, 384), BF),
            pltpu.VMEM((384, 1024), BF),
            pltpu.VMEM((4, ROWS, 1024), F32),
            pltpu.SemaphoreType.DMA((3, 3)),
            pltpu.SemaphoreType.DMA((4,)),
        ],
        compiler_params=pltpu.CompilerParams(vmem_limit_bytes=20 * MIB),
        name="update",
    )(field, u, wt)


def body(right_sides, panel_order, leaf_inverse, test_basis, update_basis, coupling):
    sides = jnp.transpose(right_sides, (1, 0, 2))
    test = jnp.transpose(test_basis, (0, 2, 1, 3))
    upd = jnp.transpose(update_basis, (0, 2, 1, 3))
    field, w = solve(panel_order, sides, leaf_inverse, test, upd, coupling.reshape(3, 256, 256))
    out = update(in_vmem(field), upd, in_vmem(w))
    return jnp.transpose(out, (1, 0, 2))


def solution(mesh):
    in_specs = (
        P(("leaf", "sub"), None, None),
        P(("leaf", "sub")),
        P(("leaf", "sub"), None, None),
        P(None, ("leaf", "sub"), None, None),
        P(None, ("leaf", "sub"), None, None),
        P(None, "leaf", None, None),
    )
    out_specs = P(("leaf", "sub"), None, None)
    return jax.shard_map(body, mesh=mesh, in_specs=in_specs, out_specs=out_specs, check_vma=False)
```

```python
import jax
import jax.numpy as jnp
from jax import lax
from jax.experimental import pallas as pl
from jax.experimental.pallas import tpu as pltpu
from jax.sharding import PartitionSpec as P

BF = jnp.bfloat16
F32 = jnp.float32
MIB = 1 << 20
MESH = pl.DeviceIdType.MESH
HIGH = lax.Precision.HIGHEST
CHUNKS = 2
WIDE = 1024 // CHUNKS
CORE = WIDE // 2
RING = CORE // 4
OWN = RING // 4


def in_vmem(a):
    return pltpu.with_memory_space_constraint(a, pltpu.VMEM)


def solve_kernel(order, order_hbm, x_hbm, a_hbm, v_hbm, u_hbm, cp_hbm, field, w,
                 xb, av, ap, xf, xg, cp, st, gt, vv, uv, vit, bt, acc, ov, iv, inverse,
                 r1, r2, p2, r3, p4, r4, wf, nv,
                 rg1, rg2, pg2, rg3, rg3x, gfull,
                 lsem, xsem, s1, q1, s2, q2, s3, q3, s4, q4, s5, q5, s6, q6, s7, q7,
                 t1, v1, t2, v2, t3, v3, t3x, v3x, t4, v4, t5, v5, asem, isem):
    place = lax.axis_index("leaf")
    z = lax.axis_index("sub")
    k = lax.rem(place, 2)
    y = lax.rem(place // 2, 4)
    x = place // 8
    ia = jnp.where(k == 0, z, y)
    ib = jnp.where(k == 0, y, z)
    half = y // 2

    def device(xx, yy, kk, zz):
        return ((xx * 4 + yy) * 2 + kk, zz)

    def ring_a(d):
        t = lax.rem(ia + d, 4)
        return device(x, jnp.where(k == 0, y, t), k, jnp.where(k == 0, t, z))

    def ring_b(e, xx=None):
        t = lax.rem(ib + e, 4)
        return device(x if xx is None else xx, jnp.where(k == 0, t, y), k, jnp.where(k == 0, z, t))

    sibling = x + 1 - 2 * lax.rem(x, 2)
    other_core = device(x, y, 1 - k, z)
    xs = [device(xx, y, k, z) for xx in (sibling, lax.rem(x + 2, 4), lax.rem(sibling + 2, 4))]
    half_of = {d: jnp.where(k == 0, half, lax.rem(y + d, 4) // 2) for d in (1, 2, 3)}
    half_of[0] = half
    sends = []

    def send(src, dst, ssem, rsem, where):
        copy = pltpu.make_async_remote_copy(src_ref=src, dst_ref=dst, send_sem=ssem, recv_sem=rsem,
                                            device_id=where, device_id_type=MESH)
        copy.start()
        sends.append(copy)
        return copy

    def load(src, dst, sem):
        copy = pltpu.make_async_copy(src, dst, sem)
        copy.start()
        return copy

    vload = load(v_hbm, vv, lsem.at[0])
    oload = load(order_hbm, ov, lsem.at[1])
    aloads = [load(a_hbm.at[leaf], av.at[leaf], asem.at[leaf]) for leaf in range(4)]
    uload = load(u_hbm.at[pl.ds(0, 2)], uv, lsem.at[2])
    xloads = {}
    for c in range(3):
        for q in range(4):
            xloads[c, q] = load(x_hbm.at[c, pl.ds(q * 256, 256), :], xb.at[q, c], xsem.at[c, q])
    cload = load(cp_hbm, cp, lsem.at[3])

    partners = [other_core] + xs
    for d in range(1, 4):
        partners += [ring_a(d), ring_b(d), ring_b(d, sibling)]
    barrier = pltpu.get_barrier_semaphore()
    for where in partners:
        pl.semaphore_signal(barrier, inc=1, device_id=where, device_id_type=MESH)

    oload.wait()
    places = lax.bitwise_and(ov[...], 1023).T
    panel = lax.broadcasted_iota(jnp.int32, (128, 1024), 1)
    position = lax.broadcasted_iota(jnp.int32, (128, 1024), 0)
    found = jnp.zeros((1, 1024), jnp.int32)
    for r in range(8):
        hit = places[:, r:r + 1] == panel
        found += jnp.sum(jnp.where(hit, position + r * 128, 0), axis=0, keepdims=True)
    found = jnp.minimum(found, 1023) * 3
    for r in range(8):
        iv[r:r + 1, :] = found[:, r * 128:r * 128 + 128]
    icopy = load(iv, inverse, isem.at[0])

    vload.wait()
    for leaf in range(4):
        for level in range(3):
            for c in range(3):
                xg[pl.ds(level * 768 + c, 256, stride=3), :] = vv[level, c, pl.ds(leaf * 256, 256), :].astype(F32)
        for level in range(3):
            vit[leaf, pl.ds(level * 128, 128), :] = xg[pl.ds(level * 768, 768), :].astype(BF).T
    frows = field.reshape(24576, 128)
    ftiles = field.reshape(3072, 8, 128)
    for leaf in range(4):
        aloads[leaf].wait()
        b = jnp.dot(vit[leaf], av[leaf], preferred_element_type=F32)
        for level in range(3):
            frows[pl.ds(leaf * 6144 + level, 768, stride=8), :] = b[level * 128:level * 128 + 128].T
    uload.wait()
    g0 = jnp.zeros((128, 256), F32)
    g1 = jnp.zeros((128, 128), F32)
    over_rows = (((0,), (0,)), ((), ()))
    for c in range(3):
        v12 = jnp.concatenate([vv[1, c], vv[2, c]], axis=1)
        g0 += lax.dot_general(uv[0, c], v12, over_rows, preferred_element_type=F32)
        g1 += lax.dot_general(uv[1, c], vv[2, c], over_rows, preferred_element_type=F32)
    gt[:, 0:128] = g1
    gt[:, 128:384] = g0

    xrows = xf.reshape(24576, 128)

    def expand(c):
        @pl.loop(0, 64, unroll=4)
        def _(i):
            q = i // 16
            rows = xb[q, c, pl.ds(pl.multiple_of(lax.rem(i, 16) * 16, 16), 16), :].astype(F32)
            for h in range(2):
                for j in range(8):
                    xrows[pl.ds(c * 8192 + i * 128 + h * 64 + j, 8, stride=8), :] = (
                        rows[h * 8:h * 8 + 8, j * 128:j * 128 + 128])

    def gather(leaf):
        @pl.loop(0, 16, unroll=2)
        def _(i):
            for kk in range(16):
                p = i * 16 + kk
                src = lax.bitwise_and(order[leaf * 256 + p], 1023)
                for c in range(3):
                    xg[pl.ds(pl.multiple_of(p * 24 + c * 8, 8), 8), :] = xf[c, src]

    def repack(leaf):
        @pl.loop(0, 48, unroll=4)
        def _(i):
            c = i // 16
            off = pl.multiple_of(lax.rem(i, 16) * 16, 16)
            for j in range(8):
                lo = xg[pl.ds(i * 128 + j, 8, stride=8), :]
                hi = xg[pl.ds(i * 128 + 64 + j, 8, stride=8), :]
                xb[leaf, c, pl.ds(off, 16), pl.ds(j * 128, 128)] = jnp.concatenate([lo, hi], axis=0).astype(BF)

    def to_panels(part):
        @pl.loop(0, 8)
        def _(i):
            for j in range(64):
                q = part * 512 + i * 64 + j
                src = inverse[part * 4 + i // 2, lax.rem(i, 2) * 64 + j]
                for c in range(3):
                    xrows[pl.ds(pl.multiple_of(c * 8192 + q * 8, 8), 8), :] = ftiles[src + c]

    def basis_rows(c):
        for level in range(3):
            bt[pl.ds(level * 128, 128), pl.ds(c * 1024, 1024)] = (
                xrows[pl.ds(c * 8192 + level, 1024, stride=8), :].astype(BF).T)

    def project(c, ch):
        if ch == 0:
            for q in range(4):
                xloads[c, q].wait()
        cols = pl.ds(ch * WIDE, WIDE)
        part = jnp.dot(bt[:, pl.ds(c * 1024, 1024)], xb[:, c, :, cols].reshape(1024, WIDE), preferred_element_type=F32)
        if c == 0:
            acc[...] = part
        elif c == 1:
            acc[...] += part
        else:
            st[cols, :] = (acc[...] + part).T

    pl.semaphore_wait(barrier, len(partners))
    at = {}
    ghalf = [half] + [half_of[4 - d] for d in range(1, 4)]
    grows = pl.multiple_of(k * 64 + ia * 16, 16)

    def split(parts, h):
        return sum(jnp.where(hh == h, part, 0.0) for hh, part in zip(ghalf, parts))

    def bases_1():
        at["g1"] = send(gt.at[pl.ds(pl.multiple_of((1 - k) * 64, 64), 64)], rg1, t1.at[0], v1.at[0], other_core)

    def bases_2():
        at["g1"].wait_recv()
        rg1[...] += gt[pl.ds(pl.multiple_of(k * 64, 64), 64), :]
        for d in range(1, 4):
            rows = pl.multiple_of(lax.rem(ia + d, 4) * 16, 16)
            at["g2", d] = send(rg1.at[pl.ds(rows, 16)], rg2.at[d - 1], t2.at[d - 1], v2.at[d - 1], ring_a(d))

    def bases_3():
        for d in range(1, 4):
            at["g2", d].wait_recv()
        gp = [rg1[pl.ds(pl.multiple_of(ia * 16, 16), 16), :]] + [rg2[d] for d in range(3)]
        pg2[:, 0:128] = sum(p[:, 128:256] for p in gp)
        for h in range(2):
            pg2[:, 128 + h * 128:256 + h * 128] = split([p[:, 256:384] for p in gp], h)
            pg2[:, 384 + h * 128:512 + h * 128] = split([p[:, 0:128] for p in gp], h)
        for e in range(1, 4):
            at["g3", e] = send(pg2, rg3.at[e - 1], t3.at[e - 1], v3.at[e - 1], ring_b(e))
        for e in range(4):
            at["g3", 4 + e] = send(pg2.at[:, pl.ds(0, 128)], rg3x.at[e], t3x.at[e], v3x.at[e], ring_b(e, sibling))

    def bases_4():
        for e in range(1, 8):
            at["g3", e].wait_recv()
        gfull[pl.ds(grows, 16), 0:640] = pg2[...] + rg3[0] + rg3[1] + rg3[2]
        gfull[pl.ds(grows, 16), 640:768] = rg3x[0] + rg3x[1] + rg3x[2] + rg3x[3]
        for d in range(1, 4):
            part = gfull.at[pl.ds(grows, 16)]
            at["g4", d] = send(part, part, t4.at[d - 1], v4.at[d - 1], ring_a(d))

    def bases_5():
        for d in range(1, 4):
            at["g4", d].wait_recv()
        part = gfull.at[pl.ds(pl.multiple_of(k * 64, 64), 64)]
        at["g5"] = send(part, part, t5.at[0], v5.at[0], other_core)

    def permute_rows(leaf):
        for j in range(6):
            xg[pl.ds(j * 768, 768), :] = av[leaf, :, pl.ds(j * 128, 128)].astype(F32)
        for j in range(6):
            for c in range(3):
                ap[leaf, pl.ds(c * 256, 256), pl.ds(j * 128, 128)] = (
                    xg[pl.ds(j * 768 + c, 256, stride=3), :].astype(BF))

    def multiply(leaf, n):
        cols = pl.ds(n * 256, 256)
        f = jnp.dot(ap[leaf], xb[leaf, :, :, cols].reshape(768, 256), preferred_element_type=F32)
        for j in range(2):
            field[:, n * 2 + j, pl.ds(leaf * 256, 256), :] = f[:, j * 128:j * 128 + 128].reshape(3, 256, 128)

    pieces = [lambda c=c: expand(c) for c in range(3)]
    for leaf in range(4):
        pieces += [lambda leaf=leaf: gather(leaf), lambda leaf=leaf: repack(leaf), lambda leaf=leaf: permute_rows(leaf)]
        pieces += [lambda leaf=leaf, n=n: multiply(leaf, n) for n in range(4)]

    def work(count):
        for _ in range(min(count, len(pieces))):
            pieces.pop(0)()

    def dot(a, b):
        return lax.dot_general(a, b, (((1,), (0,)), ((), ())), precision=HIGH, preferred_element_type=F32)

    def dot_t(a, b):
        return lax.dot_general(a, b, (((1,), (1,)), ((), ())), precision=HIGH, preferred_element_type=F32)

    def rounded(a):
        return a.astype(BF).astype(F32)

    def pair(own_first, own, other):
        return jnp.concatenate([jnp.where(own_first, own, other), jnp.where(own_first, other, own)], axis=1)

    def widen(part, hh):
        last = part[:, 256:384]
        return jnp.concatenate([part[:, 0:256], jnp.where(hh == 0, last, 0.0), jnp.where(hh == 1, last, 0.0)], axis=1)

    def narrow(block, hh):
        return jnp.concatenate([block[:, 0:256], jnp.where(hh == 0, block[:, 256:384], block[:, 384:512])], axis=1)

    def block_rows(ch, core, t, rows):
        return pl.ds(pl.multiple_of(ch * WIDE + core * CORE + t * RING, rows), rows)

    def to_core(ch):
        for d in (2, 1, 3, 0):
            src = st.at[block_rows(ch, 1 - k, lax.rem(ib + d, 4), RING)]
            at["c1", ch, d] = send(src, r1.at[ch, d], s1.at[ch, d], q1.at[ch, d], other_core)

    def to_ring_a(ch):
        for d in (2, 1, 3, 0):
            at["c1", ch, d].wait_recv()
            r1[ch, d] += st[block_rows(ch, k, lax.rem(ia + d, 4), RING), :]
            if d:
                at["c2", ch, d] = send(r1.at[ch, d], r2.at[ch, d - 1], s2.at[ch, d - 1], q2.at[ch, d - 1], ring_a(d))

    def to_ring_b(ch):
        for d in (1, 2, 3):
            at["c2", ch, d].wait_recv()
        total = widen(r1[ch, 0], half)
        for d in (1, 2, 3):
            total += widen(r2[ch, d - 1], half_of[4 - d])
        p2[ch] = total
        for e in (2, 1, 3):
            rows = pl.ds(pl.multiple_of(lax.rem(ib + e, 4) * OWN, OWN), OWN)
            at["c3", ch, e] = send(p2.at[ch, rows], r3.at[ch, e - 1], s3.at[ch, e - 1], q3.at[ch, e - 1], ring_b(e))

    def to_x(ch):
        for e in (1, 2, 3):
            at["c3", ch, e].wait_recv()
        rows = pl.ds(pl.multiple_of(ib * OWN, OWN), OWN)
        p4[ch] = p2[ch, rows, :] + r3[ch, 0] + r3[ch, 1] + r3[ch, 2]
        for i, lanes in ((2, 128), (1, 128), (0, 256)):
            at["c4", ch, i] = send(p4.at[ch, :, pl.ds(0, lanes)], r4.at[ch, i, :, pl.ds(0, lanes)],
                                   s4.at[ch, i], q4.at[ch, i], xs[i])

    def small_systems(ch):
        if ch == 0:
            cload.wait()
            at["g5"].wait_recv()
        for i in range(3):
            at["c4", ch, i].wait_recv()
        top = x // 2
        odd = lax.rem(x, 2)
        own0 = p4[ch, :, 0:128] + r4[ch, 0, :, 0:128]
        far0 = r4[ch, 1, :, 0:128] + r4[ch, 2, :, 0:128]
        w0 = rounded(dot_t(pair(top == 0, own0, far0), cp[0, pl.ds(pl.multiple_of(top * 128, 128), 128), :]))
        own1 = p4[ch, :, 128:256] - dot(w0, gfull[:, 0:128])
        far1 = r4[ch, 0, :, 128:256] - dot(w0, gfull[:, 640:768])
        w1 = rounded(dot_t(pair(odd == 0, own1, far1), cp[1, pl.ds(pl.multiple_of(odd * 128, 128), 128), :]))
        both = [p4[ch, :, 256 + h * 128:384 + h * 128] - dot(w0, gfull[:, 128 + h * 128:256 + h * 128])
                - dot(w1, gfull[:, 384 + h * 128:512 + h * 128]) for h in range(2)]
        w2 = rounded(dot_t(jnp.concatenate(both, axis=1), cp[2]))
        rows = pl.ds(pl.multiple_of(ib * OWN, OWN), OWN)
        wf[ch, rows, 0:128] = w0
        wf[ch, rows, 128:256] = w1
        wf[ch, rows, 256:512] = w2
        part = wf.at[ch, rows]
        for e in (2, 1, 3):
            at["c5", ch, e] = send(part, part, s5.at[ch, e - 1], q5.at[ch, e - 1], ring_b(e))

    def to_partner(ch, d):
        part = w.at[block_rows(ch, k, lax.rem(ia + d, 4), RING)]
        at["c7", ch, d] = send(part, part, s7.at[ch, d], q7.at[ch, d], other_core)

    def back_ring_a(ch):
        for e in (1, 2, 3):
            at["c5", ch, e].wait_recv()
        for h in range(2):
            nv[ch, h] = narrow(wf[ch], h)
        rows = block_rows(ch, k, ia, RING)
        for d in (2, 1, 3):
            at["c6", ch, d] = send(nv.at[ch, half_of[d]], w.at[rows], s6.at[ch, d - 1], q6.at[ch, d - 1], ring_a(d))
        w[rows, :] = narrow(wf[ch], half)
        to_partner(ch, 0)

    def back_core(ch):
        for d in (1, 3, 2):
            at["c6", ch, d].wait_recv()
            to_partner(ch, 4 - d)

    bases_1()
    icopy.wait()
    to_panels(0)
    bases_2()
    to_panels(1)
    for c in range(3):
        basis_rows(c)
        if c == 0:
            bases_3()
        project(c, 0)
    to_core(0)
    for c in range(3):
        project(c, 1)
        if c == 0:
            bases_4()
    to_core(1)
    to_ring_a(0)
    work(1)
    to_ring_a(1)
    work(4)
    to_ring_b(0)
    bases_5()
    work(6)
    to_ring_b(1)
    work(1)
    to_x(0)
    work(6)
    to_x(1)
    work(1)
    small_systems(0)
    work(1)
    small_systems(1)
    work(4)
    back_ring_a(0)
    work(2)
    back_ring_a(1)
    work(99)
    back_core(0)
    back_core(1)
    work(99)
    for ch in range(CHUNKS):
        for d in range(4):
            at["c7", ch, d].wait_recv()
    for copy in sends:
        copy.wait_send()


def solve(order, x, a, v, u, cp):
    vm = pl.BlockSpec(memory_space=pltpu.VMEM)
    hbm = pl.BlockSpec(memory_space=pl.ANY)
    dma = pltpu.SemaphoreType.DMA

    def shape(*dims):
        return pltpu.VMEM(dims, F32)

    n = CHUNKS
    sems = [(4,), (3, 4)]
    for s in [(n, 4), (n, 3), (n, 3), (n, 3), (n, 3), (n, 3), (n, 4), (1,), (3,), (3,), (4,), (3,), (1,)]:
        sems += [s, s]
    return pl.pallas_call(
        solve_kernel,
        out_shape=[pltpu.VMEM((3, 8, 1024, 128), F32), pltpu.VMEM((1024, 384), F32)],
        in_specs=[pl.BlockSpec(memory_space=pltpu.SMEM), hbm, hbm, hbm, hbm, hbm, hbm],
        out_specs=[vm, vm],
        scratch_shapes=[
            pltpu.VMEM((4, 3, 256, 1024), BF), pltpu.VMEM((4, 768, 768), BF), pltpu.VMEM((4, 768, 768), BF),
            shape(3, 1024, 8, 128), shape(6144, 128), shape(3, 256, 256), shape(1024, 384), shape(128, 384),
            pltpu.VMEM((3, 3, 1024, 128), BF), pltpu.VMEM((2, 3, 1024, 128), BF), pltpu.VMEM((4, 384, 768), BF),
            pltpu.VMEM((384, 3072), BF), shape(384, WIDE), pltpu.VMEM((8, 128), jnp.int32),
            pltpu.VMEM((8, 128), jnp.int32), pltpu.SMEM((8, 128), jnp.int32),
            shape(n, 4, RING, 384), shape(n, 3, RING, 384), shape(n, RING, 512),
            shape(n, 3, OWN, 512), shape(n, OWN, 512), shape(n, 3, OWN, 256), shape(n, RING, 512),
            shape(n, 2, RING, 384),
            shape(64, 384), shape(3, 16, 384), shape(16, 640), shape(3, 16, 640), shape(4, 16, 128), shape(128, 768),
        ] + [dma(s) for s in sems] + [dma((4,)), dma((1,))],
        compiler_params=pltpu.CompilerParams(vmem_limit_bytes=48 * MIB, collective_id=0, has_side_effects=True),
        name="leaf_solve_and_levels",
    )(order, order.reshape(8, 128), x, a, v, u, cp)


ROWS = 512


def update_kernel(field, u_hbm, wt, out, u, w, buf, usem, sem):
    loads = {}
    for c in range(3):
        for level in range(3):
            loads[c, level] = pltpu.make_async_copy(
                u_hbm.at[level, c], u.at[c, :, pl.ds(level * 128, 128)], usem.at[c, level])
            loads[c, level].start()
    w[...] = (-wt[...].T).astype(BF)
    copies = []
    for c in range(3):
        for level in range(3):
            loads[c, level].wait()
        for r in range(1024 // ROWS):
            rows = pl.ds(r * ROWS, ROWS)
            i = len(copies)
            slot = i % 4
            if i >= 4:
                copies[i - 4].wait()
            change = jnp.dot(u[c, rows, :], w[...], preferred_element_type=F32)
            for j in range(8):
                lanes = slice(j * 128, j * 128 + 128)
                buf[slot, :, lanes] = field[c, j, rows, :] + change[:, lanes]
            copies.append(pltpu.make_async_copy(buf.at[slot], out.at[c, rows, :], sem.at[slot]))
            copies[-1].start()
    for copy in copies[-4:]:
        copy.wait()


def update(field, u, wt):
    vm = pl.BlockSpec(memory_space=pltpu.VMEM)
    hbm = pl.BlockSpec(memory_space=pl.ANY)
    return pl.pallas_call(
        update_kernel,
        out_shape=jax.ShapeDtypeStruct((3, 1024, 1024), F32),
        in_specs=[vm, hbm, vm],
        out_specs=hbm,
        scratch_shapes=[
            pltpu.VMEM((3, 1024, 384), BF),
            pltpu.VMEM((384, 1024), BF),
            pltpu.VMEM((4, ROWS, 1024), F32),
            pltpu.SemaphoreType.DMA((3, 3)),
            pltpu.SemaphoreType.DMA((4,)),
        ],
        compiler_params=pltpu.CompilerParams(vmem_limit_bytes=20 * MIB),
        name="update",
    )(field, u, wt)


def body(right_sides, panel_order, leaf_inverse, test_basis, update_basis, coupling):
    sides = jnp.transpose(right_sides, (1, 0, 2))
    test = jnp.transpose(test_basis, (0, 2, 1, 3))
    upd = jnp.transpose(update_basis, (0, 2, 1, 3))
    field, w = solve(panel_order, sides, leaf_inverse, test, upd, coupling.reshape(3, 256, 256))
    out = update(in_vmem(field), upd, in_vmem(w))
    return jnp.transpose(out, (1, 0, 2))


def solution(mesh):
    in_specs = (
        P(("leaf", "sub"), None, None),
        P(("leaf", "sub")),
        P(("leaf", "sub"), None, None),
        P(None, ("leaf", "sub"), None, None),
        P(None, ("leaf", "sub"), None, None),
        P(None, "leaf", None, None),
    )
    out_specs = P(("leaf", "sub"), None, None)
    return jax.shard_map(body, mesh=mesh, in_specs=in_specs, out_specs=out_specs, check_vma=False)
```

```python
import jax
import jax.numpy as jnp
from jax import lax
from jax.experimental import pallas as pl
from jax.experimental.pallas import tpu as pltpu
from jax.sharding import PartitionSpec as P

BF = jnp.bfloat16
F32 = jnp.float32
MIB = 1 << 20
MESH = pl.DeviceIdType.MESH
HIGH = lax.Precision.HIGHEST
CHUNKS = 2
WIDE = 1024 // CHUNKS
CORE = WIDE // 2
RING = CORE // 4
OWN = RING // 4


def in_vmem(a):
    return pltpu.with_memory_space_constraint(a, pltpu.VMEM)


def project_kernel(order, x_hbm, a_hbm, v_hbm, u_hbm, st, gt,
                   xv, av, vv, uv, vsh, vit, bs, bd, bt, acc, places, sems):
    pairs = [(v_hbm, vv)] + [(a_hbm.at[leaf], av.at[leaf]) for leaf in range(4)]
    pairs += [(order, places), (u_hbm.at[pl.ds(0, 2)], uv), (x_hbm, xv)]
    loads = [pltpu.make_async_copy(s, d, sems.at[i]) for i, (s, d) in enumerate(pairs)]
    for copy in loads:
        copy.start()
    loads[0].wait()
    for leaf in range(4):
        for level in range(3):
            for c in range(3):
                vsh[level, pl.ds(c, 256, stride=3), :] = vv[level, c, pl.ds(leaf * 256, 256), :].astype(F32)
        for level in range(3):
            vit[leaf, pl.ds(level * 128, 128), :] = vsh[level].astype(BF).T
    for leaf in range(4):
        loads[1 + leaf].wait()
        b = jnp.dot(vit[leaf], av[leaf], preferred_element_type=F32)
        for level in range(3):
            bs[pl.ds(leaf * 6144 + level, 768, stride=8), :] = b[level * 128:level * 128 + 128].T

    loads[6].wait()
    g0 = jnp.zeros((128, 256), F32)
    g1 = jnp.zeros((128, 128), F32)
    over_rows = (((0,), (0,)), ((), ()))
    for c in range(3):
        v12 = jnp.concatenate([vv[1, c], vv[2, c]], axis=1)
        g0 += lax.dot_general(uv[0, c], v12, over_rows, preferred_element_type=F32)
        g1 += lax.dot_general(uv[1, c], vv[2, c], over_rows, preferred_element_type=F32)
    gt[:, 0:128] = g1
    gt[:, 128:384] = g0
    loads[5].wait()

    @pl.loop(0, 64)
    def _(i):
        for j in range(16):
            p = i * 16 + j
            dst = lax.bitwise_and(places[p], 1023) * 8
            for c in range(3):
                bd[pl.ds(pl.multiple_of(c * 8192 + dst, 8), 8), :] = (
                    bs[pl.ds(pl.multiple_of(p * 24 + c * 8, 8), 8), :])

    loads[7].wait()
    for c in range(3):
        for level in range(3):
            bt[pl.ds(level * 128, 128), pl.ds(c * 1024, 1024)] = (
                bd[pl.ds(c * 8192 + level, 1024, stride=8), :].astype(BF).T)
        for n in range(2):
            cols = pl.ds(n * 512, 512)
            part = jnp.dot(bt[:, pl.ds(c * 1024, 1024)], xv[c, :, cols], preferred_element_type=F32)
            if c == 0:
                acc[:, cols] = part
            elif c == 1:
                acc[:, cols] += part
            else:
                st[cols, :] = (acc[:, cols] + part).T


def project(order, x, a, v, u):
    vm = pl.BlockSpec(memory_space=pltpu.VMEM)
    hbm = pl.BlockSpec(memory_space=pl.ANY)
    return pl.pallas_call(
        project_kernel,
        out_shape=[pltpu.VMEM((1024, 384), F32), pltpu.VMEM((128, 384), F32)],
        in_specs=[pl.BlockSpec(memory_space=pltpu.HBM), hbm, hbm, hbm, hbm],
        out_specs=[vm, vm],
        scratch_shapes=[
            pltpu.VMEM((3, 1024, 1024), BF),
            pltpu.VMEM((4, 768, 768), BF),
            pltpu.VMEM((3, 3, 1024, 128), BF),
            pltpu.VMEM((2, 3, 1024, 128), BF),
            pltpu.VMEM((3, 768, 128), F32),
            pltpu.VMEM((4, 384, 768), BF),
            pltpu.VMEM((24576, 128), F32),
            pltpu.VMEM((24576, 128), F32),
            pltpu.VMEM((384, 3072), BF),
            pltpu.VMEM((384, 1024), F32),
            pltpu.SMEM((1024,), jnp.int32),
            pltpu.SemaphoreType.DMA((8,)),
        ],
        compiler_params=pltpu.CompilerParams(vmem_limit_bytes=50 * MIB),
        name="project",
    )(order, x, a, v, u)


def solve_kernel(order, x_hbm, a_hbm, st, gt, cp_hbm, field, w,
                 xb, av, ap, xf, xg, ash, cp,
                 r1, r2, p2, r3, p4, r4, wf, nv,
                 rg1, rg2, pg2, rg3, rg3x, gfull,
                 lsem, xsem, s1, q1, s2, q2, s3, q3, s4, q4, s5, q5, s6, q6, s7, q7,
                 t1, v1, t2, v2, t3, v3, t3x, v3x, t4, v4, t5, v5):
    place = lax.axis_index("leaf")
    z = lax.axis_index("sub")
    k = lax.rem(place, 2)
    y = lax.rem(place // 2, 4)
    x = place // 8
    ia = jnp.where(k == 0, z, y)
    ib = jnp.where(k == 0, y, z)
    half = y // 2

    def device(xx, yy, kk, zz):
        return ((xx * 4 + yy) * 2 + kk, zz)

    def ring_a(d):
        t = lax.rem(ia + d, 4)
        return device(x, jnp.where(k == 0, y, t), k, jnp.where(k == 0, t, z))

    def ring_b(e, xx=None):
        t = lax.rem(ib + e, 4)
        return device(x if xx is None else xx, jnp.where(k == 0, t, y), k, jnp.where(k == 0, z, t))

    sibling = x + 1 - 2 * lax.rem(x, 2)
    other_core = device(x, y, 1 - k, z)
    xs = [device(xx, y, k, z) for xx in (sibling, lax.rem(x + 2, 4), lax.rem(sibling + 2, 4))]
    half_of = {d: jnp.where(k == 0, half, lax.rem(y + d, 4) // 2) for d in (1, 2, 3)}
    half_of[0] = half
    sends = []

    def send(src, dst, ssem, rsem, where):
        copy = pltpu.make_async_remote_copy(src_ref=src, dst_ref=dst, send_sem=ssem, recv_sem=rsem,
                                            device_id=where, device_id_type=MESH)
        copy.start()
        sends.append(copy)
        return copy

    def load(src, dst, sem):
        copy = pltpu.make_async_copy(src, dst, sem)
        copy.start()
        return copy

    xloads = {}
    for c in range(3):
        for q in range(4):
            xloads[c, q] = load(x_hbm.at[c, pl.ds(q * 256, 256), :], xb.at[q, c], xsem.at[c, q])
    aload = load(a_hbm, av, lsem.at[2])
    cload = load(cp_hbm, cp, lsem.at[3])

    partners = [other_core] + xs
    for d in range(1, 4):
        partners += [ring_a(d), ring_b(d), ring_b(d, sibling)]
    barrier = pltpu.get_barrier_semaphore()
    for where in partners:
        pl.semaphore_signal(barrier, inc=1, device_id=where, device_id_type=MESH)

    xrows = xf.reshape(24576, 128)

    def expand(c):
        for q in range(4):
            xloads[c, q].wait()

        @pl.loop(0, 64, unroll=4)
        def _(i):
            q = i // 16
            rows = xb[q, c, pl.ds(pl.multiple_of(lax.rem(i, 16) * 16, 16), 16), :].astype(F32)
            for h in range(2):
                for j in range(8):
                    xrows[pl.ds(c * 8192 + i * 128 + h * 64 + j, 8, stride=8), :] = (
                        rows[h * 8:h * 8 + 8, j * 128:j * 128 + 128])

    def gather(leaf):
        @pl.loop(0, 16, unroll=2)
        def _(i):
            for kk in range(16):
                p = i * 16 + kk
                src = lax.bitwise_and(order[leaf * 256 + p], 1023)
                for c in range(3):
                    xg[pl.ds(pl.multiple_of(p * 24 + c * 8, 8), 8), :] = xf[c, src]

    def repack(leaf):
        @pl.loop(0, 48, unroll=4)
        def _(i):
            c = i // 16
            off = pl.multiple_of(lax.rem(i, 16) * 16, 16)
            for j in range(8):
                lo = xg[pl.ds(i * 128 + j, 8, stride=8), :]
                hi = xg[pl.ds(i * 128 + 64 + j, 8, stride=8), :]
                xb[leaf, c, pl.ds(off, 16), pl.ds(j * 128, 128)] = jnp.concatenate([lo, hi], axis=0).astype(BF)

    expand(0)
    pl.semaphore_wait(barrier, len(partners))
    at = {}
    ghalf = [half] + [half_of[4 - d] for d in range(1, 4)]
    grows = pl.multiple_of(k * 64 + ia * 16, 16)

    def split(parts, h):
        return sum(jnp.where(hh == h, part, 0.0) for hh, part in zip(ghalf, parts))

    def bases_1():
        at["g1"] = send(gt.at[pl.ds(pl.multiple_of((1 - k) * 64, 64), 64)], rg1, t1.at[0], v1.at[0], other_core)

    def bases_2():
        at["g1"].wait_recv()
        rg1[...] += gt[pl.ds(pl.multiple_of(k * 64, 64), 64), :]
        for d in range(1, 4):
            rows = pl.multiple_of(lax.rem(ia + d, 4) * 16, 16)
            at["g2", d] = send(rg1.at[pl.ds(rows, 16)], rg2.at[d - 1], t2.at[d - 1], v2.at[d - 1], ring_a(d))

    def bases_3():
        for d in range(1, 4):
            at["g2", d].wait_recv()
        gp = [rg1[pl.ds(pl.multiple_of(ia * 16, 16), 16), :]] + [rg2[d] for d in range(3)]
        pg2[:, 0:128] = sum(p[:, 128:256] for p in gp)
        for h in range(2):
            pg2[:, 128 + h * 128:256 + h * 128] = split([p[:, 256:384] for p in gp], h)
            pg2[:, 384 + h * 128:512 + h * 128] = split([p[:, 0:128] for p in gp], h)
        for e in range(1, 4):
            at["g3", e] = send(pg2, rg3.at[e - 1], t3.at[e - 1], v3.at[e - 1], ring_b(e))
        for e in range(4):
            at["g3", 4 + e] = send(pg2.at[:, pl.ds(0, 128)], rg3x.at[e], t3x.at[e], v3x.at[e], ring_b(e, sibling))

    def bases_4():
        for e in range(1, 8):
            at["g3", e].wait_recv()
        gfull[pl.ds(grows, 16), 0:640] = pg2[...] + rg3[0] + rg3[1] + rg3[2]
        gfull[pl.ds(grows, 16), 640:768] = rg3x[0] + rg3x[1] + rg3x[2] + rg3x[3]
        for d in range(1, 4):
            part = gfull.at[pl.ds(grows, 16)]
            at["g4", d] = send(part, part, t4.at[d - 1], v4.at[d - 1], ring_a(d))

    def bases_5():
        for d in range(1, 4):
            at["g4", d].wait_recv()
        part = gfull.at[pl.ds(pl.multiple_of(k * 64, 64), 64)]
        at["g5"] = send(part, part, t5.at[0], v5.at[0], other_core)

    def permute_rows(leaf):
        if leaf == 0:
            aload.wait()
        for j in range(6):
            ash[j] = av[leaf, :, pl.ds(j * 128, 128)].astype(F32)
        for j in range(6):
            for c in range(3):
                ap[leaf, pl.ds(c * 256, 256), pl.ds(j * 128, 128)] = (
                    ash[j, pl.ds(c, 256, stride=3), :].astype(BF))

    def multiply(leaf, n):
        cols = pl.ds(n * 256, 256)
        f = jnp.dot(ap[leaf], xb[leaf, :, :, cols].reshape(768, 256), preferred_element_type=F32)
        field[:, pl.ds(leaf * 256, 256), cols] = f.reshape(3, 256, 256)

    pieces = [lambda: expand(1), lambda: expand(2)]
    for leaf in range(4):
        pieces += [lambda leaf=leaf: gather(leaf), lambda leaf=leaf: repack(leaf), lambda leaf=leaf: permute_rows(leaf)]
        pieces += [lambda leaf=leaf, n=n: multiply(leaf, n) for n in range(4)]

    def work(count):
        for _ in range(min(count, len(pieces))):
            pieces.pop(0)()

    def dot(a, b):
        return lax.dot_general(a, b, (((1,), (0,)), ((), ())), precision=HIGH, preferred_element_type=F32)

    def dot_t(a, b):
        return lax.dot_general(a, b, (((1,), (1,)), ((), ())), precision=HIGH, preferred_element_type=F32)

    def rounded(a):
        return a.astype(BF).astype(F32)

    def pair(own_first, own, other):
        return jnp.concatenate([jnp.where(own_first, own, other), jnp.where(own_first, other, own)], axis=1)

    def widen(part, hh):
        last = part[:, 256:384]
        return jnp.concatenate([part[:, 0:256], jnp.where(hh == 0, last, 0.0), jnp.where(hh == 1, last, 0.0)], axis=1)

    def narrow(block, hh):
        return jnp.concatenate([block[:, 0:256], jnp.where(hh == 0, block[:, 256:384], block[:, 384:512])], axis=1)

    def block_rows(ch, core, t, rows):
        return pl.ds(pl.multiple_of(ch * WIDE + core * CORE + t * RING, rows), rows)

    def to_core(ch):
        for d in (2, 1, 3, 0):
            src = st.at[block_rows(ch, 1 - k, lax.rem(ib + d, 4), RING)]
            at["c1", ch, d] = send(src, r1.at[ch, d], s1.at[ch, d], q1.at[ch, d], other_core)

    def to_ring_a(ch):
        for d in (2, 1, 3, 0):
            at["c1", ch, d].wait_recv()
            r1[ch, d] += st[block_rows(ch, k, lax.rem(ia + d, 4), RING), :]
            if d:
                at["c2", ch, d] = send(r1.at[ch, d], r2.at[ch, d - 1], s2.at[ch, d - 1], q2.at[ch, d - 1], ring_a(d))

    def to_ring_b(ch):
        for d in (1, 2, 3):
            at["c2", ch, d].wait_recv()
        total = widen(r1[ch, 0], half)
        for d in (1, 2, 3):
            total += widen(r2[ch, d - 1], half_of[4 - d])
        p2[ch] = total
        for e in (2, 1, 3):
            rows = pl.ds(pl.multiple_of(lax.rem(ib + e, 4) * OWN, OWN), OWN)
            at["c3", ch, e] = send(p2.at[ch, rows], r3.at[ch, e - 1], s3.at[ch, e - 1], q3.at[ch, e - 1], ring_b(e))

    def to_x(ch):
        for e in (1, 2, 3):
            at["c3", ch, e].wait_recv()
        rows = pl.ds(pl.multiple_of(ib * OWN, OWN), OWN)
        p4[ch] = p2[ch, rows, :] + r3[ch, 0] + r3[ch, 1] + r3[ch, 2]
        for i, lanes in ((2, 128), (1, 128), (0, 256)):
            at["c4", ch, i] = send(p4.at[ch, :, pl.ds(0, lanes)], r4.at[ch, i, :, pl.ds(0, lanes)],
                                   s4.at[ch, i], q4.at[ch, i], xs[i])

    def small_systems(ch):
        if ch == 0:
            cload.wait()
            at["g5"].wait_recv()
        for i in range(3):
            at["c4", ch, i].wait_recv()
        top = x // 2
        odd = lax.rem(x, 2)
        own0 = p4[ch, :, 0:128] + r4[ch, 0, :, 0:128]
        far0 = r4[ch, 1, :, 0:128] + r4[ch, 2, :, 0:128]
        w0 = rounded(dot_t(pair(top == 0, own0, far0), cp[0, pl.ds(pl.multiple_of(top * 128, 128), 128), :]))
        own1 = p4[ch, :, 128:256] - dot(w0, gfull[:, 0:128])
        far1 = r4[ch, 0, :, 128:256] - dot(w0, gfull[:, 640:768])
        w1 = rounded(dot_t(pair(odd == 0, own1, far1), cp[1, pl.ds(pl.multiple_of(odd * 128, 128), 128), :]))
        both = [p4[ch, :, 256 + h * 128:384 + h * 128] - dot(w0, gfull[:, 128 + h * 128:256 + h * 128])
                - dot(w1, gfull[:, 384 + h * 128:512 + h * 128]) for h in range(2)]
        w2 = rounded(dot_t(jnp.concatenate(both, axis=1), cp[2]))
        rows = pl.ds(pl.multiple_of(ib * OWN, OWN), OWN)
        wf[ch, rows, 0:128] = w0
        wf[ch, rows, 128:256] = w1
        wf[ch, rows, 256:512] = w2
        part = wf.at[ch, rows]
        for e in (2, 1, 3):
            at["c5", ch, e] = send(part, part, s5.at[ch, e - 1], q5.at[ch, e - 1], ring_b(e))

    def to_partner(ch, d):
        part = w.at[block_rows(ch, k, lax.rem(ia + d, 4), RING)]
        at["c7", ch, d] = send(part, part, s7.at[ch, d], q7.at[ch, d], other_core)

    def back_ring_a(ch):
        for e in (1, 2, 3):
            at["c5", ch, e].wait_recv()
        for h in range(2):
            nv[ch, h] = narrow(wf[ch], h)
        rows = block_rows(ch, k, ia, RING)
        for d in (2, 1, 3):
            at["c6", ch, d] = send(nv.at[ch, half_of[d]], w.at[rows], s6.at[ch, d - 1], q6.at[ch, d - 1], ring_a(d))
        w[rows, :] = narrow(wf[ch], half)
        to_partner(ch, 0)

    def back_core(ch):
        for d in (1, 3, 2):
            at["c6", ch, d].wait_recv()
            to_partner(ch, 4 - d)

    bases_1()
    to_core(0)
    to_core(1)
    work(1)
    bases_2()
    to_ring_a(0)
    to_ring_a(1)
    work(2)
    bases_3()
    work(6)
    to_ring_b(0)
    work(1)
    bases_4()
    work(1)
    to_ring_b(1)
    work(2)
    to_x(0)
    work(4)
    bases_5()
    to_x(1)
    small_systems(0)
    work(1)
    small_systems(1)
    work(5)
    back_ring_a(0)
    work(2)
    back_ring_a(1)
    work(99)
    back_core(0)
    back_core(1)
    work(99)
    for ch in range(CHUNKS):
        for d in range(4):
            at["c7", ch, d].wait_recv()
    for copy in sends:
        copy.wait_send()


def solve(order, x, a, st, gt, cp):
    vm = pl.BlockSpec(memory_space=pltpu.VMEM)
    hbm = pl.BlockSpec(memory_space=pl.ANY)
    dma = pltpu.SemaphoreType.DMA

    def shape(*dims):
        return pltpu.VMEM(dims, F32)

    n = CHUNKS
    sems = [(4,), (3, 4)]
    for s in [(n, 4), (n, 3), (n, 3), (n, 3), (n, 3), (n, 3), (n, 4), (1,), (3,), (3,), (4,), (3,), (1,)]:
        sems += [s, s]
    return pl.pallas_call(
        solve_kernel,
        out_shape=[pltpu.VMEM((3, 1024, 1024), F32), pltpu.VMEM((1024, 384), F32)],
        in_specs=[pl.BlockSpec(memory_space=pltpu.SMEM), hbm, hbm, vm, vm, hbm],
        out_specs=[vm, vm],
        scratch_shapes=[
            pltpu.VMEM((4, 3, 256, 1024), BF), pltpu.VMEM((4, 768, 768), BF), pltpu.VMEM((4, 768, 768), BF),
            shape(3, 1024, 8, 128), shape(6144, 128), shape(6, 768, 128), shape(3, 256, 256),
            shape(n, 4, RING, 384), shape(n, 3, RING, 384), shape(n, RING, 512),
            shape(n, 3, OWN, 512), shape(n, OWN, 512), shape(n, 3, OWN, 256), shape(n, RING, 512),
            shape(n, 2, RING, 384),
            shape(64, 384), shape(3, 16, 384), shape(16, 640), shape(3, 16, 640), shape(4, 16, 128), shape(128, 768),
        ] + [dma(s) for s in sems],
        compiler_params=pltpu.CompilerParams(vmem_limit_bytes=42 * MIB, collective_id=0, has_side_effects=True),
        name="leaf_solve_and_levels",
    )(order, x, a, st, gt, cp)


ROWS = 512


def update_kernel(field, u_hbm, wt, out, u, w, buf, usem, sem):
    loads = {}
    for c in range(3):
        for level in range(3):
            loads[c, level] = pltpu.make_async_copy(
                u_hbm.at[level, c], u.at[c, :, pl.ds(level * 128, 128)], usem.at[c, level])
            loads[c, level].start()
    w[...] = (-wt[...].T).astype(BF)
    copies = []
    for c in range(3):
        for level in range(3):
            loads[c, level].wait()
        for r in range(1024 // ROWS):
            rows = pl.ds(r * ROWS, ROWS)
            i = len(copies)
            slot = i % 4
            if i >= 4:
                copies[i - 4].wait()
            buf[slot] = field[c, rows, :] + jnp.dot(u[c, rows, :], w[...], preferred_element_type=F32)
            copies.append(pltpu.make_async_copy(buf.at[slot], out.at[c, rows, :], sem.at[slot]))
            copies[-1].start()
    for copy in copies[-4:]:
        copy.wait()


def update(field, u, wt):
    vm = pl.BlockSpec(memory_space=pltpu.VMEM)
    hbm = pl.BlockSpec(memory_space=pl.ANY)
    return pl.pallas_call(
        update_kernel,
        out_shape=jax.ShapeDtypeStruct((3, 1024, 1024), F32),
        in_specs=[vm, hbm, vm],
        out_specs=hbm,
        scratch_shapes=[
            pltpu.VMEM((3, 1024, 384), BF),
            pltpu.VMEM((384, 1024), BF),
            pltpu.VMEM((4, ROWS, 1024), F32),
            pltpu.SemaphoreType.DMA((3, 3)),
            pltpu.SemaphoreType.DMA((4,)),
        ],
        compiler_params=pltpu.CompilerParams(vmem_limit_bytes=20 * MIB),
        name="update",
    )(field, u, wt)


def body(right_sides, panel_order, leaf_inverse, test_basis, update_basis, coupling):
    sides = jnp.transpose(right_sides, (1, 0, 2))
    test = jnp.transpose(test_basis, (0, 2, 1, 3))
    upd = jnp.transpose(update_basis, (0, 2, 1, 3))
    st, gt = project(panel_order, sides, leaf_inverse, test, upd)
    field, w = solve(panel_order, sides, leaf_inverse, in_vmem(st), in_vmem(gt), coupling.reshape(3, 256, 256))
    out = update(in_vmem(field), upd, in_vmem(w))
    return jnp.transpose(out, (1, 0, 2))


def solution(mesh):
    in_specs = (
        P(("leaf", "sub"), None, None),
        P(("leaf", "sub")),
        P(("leaf", "sub"), None, None),
        P(None, ("leaf", "sub"), None, None),
        P(None, ("leaf", "sub"), None, None),
        P(None, "leaf", None, None),
    )
    out_specs = P(("leaf", "sub"), None, None)
    return jax.shard_map(body, mesh=mesh, in_specs=in_specs, out_specs=out_specs, check_vma=False)
```

```python
import jax
import jax.numpy as jnp
from jax import lax
from jax.experimental import pallas as pl
from jax.experimental.pallas import tpu as pltpu
from jax.sharding import PartitionSpec as P

BF = jnp.bfloat16
F32 = jnp.float32
MIB = 1 << 20
MESH = pl.DeviceIdType.MESH
HIGH = lax.Precision.HIGHEST
CHUNKS = 2
WIDE = 1024 // CHUNKS
CORE = WIDE // 2
RING = CORE // 4
OWN = RING // 4


def in_vmem(a):
    return pltpu.with_memory_space_constraint(a, pltpu.VMEM)


def project_kernel(order, x_hbm, a_hbm, v_hbm, u_hbm, st, gt,
                   xv, av, vv, uv, vsh, vit, bs, bd, bt, acc, places, sems):
    pairs = [(v_hbm, vv)] + [(a_hbm.at[leaf], av.at[leaf]) for leaf in range(4)]
    pairs += [(order, places), (u_hbm.at[pl.ds(0, 2)], uv), (x_hbm, xv)]
    loads = [pltpu.make_async_copy(s, d, sems.at[i]) for i, (s, d) in enumerate(pairs)]
    for copy in loads:
        copy.start()
    loads[0].wait()
    for leaf in range(4):
        for level in range(3):
            for c in range(3):
                vsh[level, pl.ds(c, 256, stride=3), :] = vv[level, c, pl.ds(leaf * 256, 256), :].astype(F32)
        for level in range(3):
            vit[leaf, pl.ds(level * 128, 128), :] = vsh[level].astype(BF).T
    for leaf in range(4):
        loads[1 + leaf].wait()
        b = jnp.dot(vit[leaf], av[leaf], preferred_element_type=F32)
        for level in range(3):
            bs[pl.ds(leaf * 6144 + level, 768, stride=8), :] = b[level * 128:level * 128 + 128].T

    loads[6].wait()
    g0 = jnp.zeros((128, 256), F32)
    g1 = jnp.zeros((128, 128), F32)
    over_rows = (((0,), (0,)), ((), ()))
    for c in range(3):
        v12 = jnp.concatenate([vv[1, c], vv[2, c]], axis=1)
        g0 += lax.dot_general(uv[0, c], v12, over_rows, preferred_element_type=F32)
        g1 += lax.dot_general(uv[1, c], vv[2, c], over_rows, preferred_element_type=F32)
    gt[:, 0:128] = g1
    gt[:, 128:384] = g0
    loads[5].wait()

    @pl.loop(0, 64)
    def _(i):
        for j in range(16):
            p = i * 16 + j
            dst = lax.bitwise_and(places[p], 1023) * 8
            for c in range(3):
                bd[pl.ds(pl.multiple_of(c * 8192 + dst, 8), 8), :] = (
                    bs[pl.ds(pl.multiple_of(p * 24 + c * 8, 8), 8), :])

    loads[7].wait()
    for c in range(3):
        for level in range(3):
            bt[pl.ds(level * 128, 128), pl.ds(c * 1024, 1024)] = (
                bd[pl.ds(c * 8192 + level, 1024, stride=8), :].astype(BF).T)
        for n in range(2):
            cols = pl.ds(n * 512, 512)
            part = jnp.dot(bt[:, pl.ds(c * 1024, 1024)], xv[c, :, cols], preferred_element_type=F32)
            if c == 0:
                acc[:, cols] = part
            elif c == 1:
                acc[:, cols] += part
            else:
                st[cols, :] = (acc[:, cols] + part).T


def project(order, x, a, v, u):
    vm = pl.BlockSpec(memory_space=pltpu.VMEM)
    hbm = pl.BlockSpec(memory_space=pl.ANY)
    return pl.pallas_call(
        project_kernel,
        out_shape=[pltpu.VMEM((1024, 384), F32), pltpu.VMEM((128, 384), F32)],
        in_specs=[pl.BlockSpec(memory_space=pltpu.HBM), hbm, hbm, hbm, hbm],
        out_specs=[vm, vm],
        scratch_shapes=[
            pltpu.VMEM((3, 1024, 1024), BF),
            pltpu.VMEM((4, 768, 768), BF),
            pltpu.VMEM((3, 3, 1024, 128), BF),
            pltpu.VMEM((2, 3, 1024, 128), BF),
            pltpu.VMEM((3, 768, 128), F32),
            pltpu.VMEM((4, 384, 768), BF),
            pltpu.VMEM((24576, 128), F32),
            pltpu.VMEM((24576, 128), F32),
            pltpu.VMEM((384, 3072), BF),
            pltpu.VMEM((384, 1024), F32),
            pltpu.SMEM((1024,), jnp.int32),
            pltpu.SemaphoreType.DMA((8,)),
        ],
        compiler_params=pltpu.CompilerParams(vmem_limit_bytes=62 * MIB),
        name="project",
    )(order, x, a, v, u)


def solve_kernel(order, x_hbm, a_hbm, st, gt, cp_hbm, field, w,
                 xb, av, ap, xf, xg, ash, cp,
                 r1, r2, p2, r3, p4, r4, wf, nv,
                 rg1, rg2, pg2, rg3, rg3x, gfull,
                 lsem, xsem, s1, q1, s2, q2, s3, q3, s4, q4, s5, q5, s6, q6, s7, q7,
                 t1, v1, t2, v2, t3, v3, t3x, v3x, t4, v4, t5, v5):
    place = lax.axis_index("leaf")
    z = lax.axis_index("sub")
    k = lax.rem(place, 2)
    y = lax.rem(place // 2, 4)
    x = place // 8
    ia = jnp.where(k == 0, z, y)
    ib = jnp.where(k == 0, y, z)
    half = y // 2

    def device(xx, yy, kk, zz):
        return ((xx * 4 + yy) * 2 + kk, zz)

    def ring_a(d):
        t = lax.rem(ia + d, 4)
        return device(x, jnp.where(k == 0, y, t), k, jnp.where(k == 0, t, z))

    def ring_b(e, xx=None):
        t = lax.rem(ib + e, 4)
        return device(x if xx is None else xx, jnp.where(k == 0, t, y), k, jnp.where(k == 0, z, t))

    sibling = x + 1 - 2 * lax.rem(x, 2)
    other_core = device(x, y, 1 - k, z)
    xs = [device(xx, y, k, z) for xx in (sibling, lax.rem(x + 2, 4), lax.rem(sibling + 2, 4))]
    half_of = {d: jnp.where(k == 0, half, lax.rem(y + d, 4) // 2) for d in (1, 2, 3)}
    half_of[0] = half
    sends = []

    def send(src, dst, ssem, rsem, where):
        copy = pltpu.make_async_remote_copy(src_ref=src, dst_ref=dst, send_sem=ssem, recv_sem=rsem,
                                            device_id=where, device_id_type=MESH)
        copy.start()
        sends.append(copy)
        return copy

    def load(src, dst, sem):
        copy = pltpu.make_async_copy(src, dst, sem)
        copy.start()
        return copy

    xloads = {}
    for c in range(3):
        for q in range(4):
            xloads[c, q] = load(x_hbm.at[c, pl.ds(q * 256, 256), :], xb.at[q, c], xsem.at[c, q])
    aload = load(a_hbm, av, lsem.at[2])
    cload = load(cp_hbm, cp, lsem.at[3])

    partners = [other_core] + xs
    for d in range(1, 4):
        partners += [ring_a(d), ring_b(d), ring_b(d, sibling)]
    barrier = pltpu.get_barrier_semaphore()
    for where in partners:
        pl.semaphore_signal(barrier, inc=1, device_id=where, device_id_type=MESH)

    xrows = xf.reshape(24576, 128)

    def expand(c):
        for q in range(4):
            xloads[c, q].wait()

        @pl.loop(0, 64, unroll=4)
        def _(i):
            q = i // 16
            rows = xb[q, c, pl.ds(pl.multiple_of(lax.rem(i, 16) * 16, 16), 16), :].astype(F32)
            for h in range(2):
                for j in range(8):
                    xrows[pl.ds(c * 8192 + i * 128 + h * 64 + j, 8, stride=8), :] = (
                        rows[h * 8:h * 8 + 8, j * 128:j * 128 + 128])

    def gather(leaf):
        @pl.loop(0, 16, unroll=2)
        def _(i):
            for kk in range(16):
                p = i * 16 + kk
                src = lax.bitwise_and(order[leaf * 256 + p], 1023)
                for c in range(3):
                    xg[pl.ds(pl.multiple_of(p * 24 + c * 8, 8), 8), :] = xf[c, src]

    def repack(leaf):
        @pl.loop(0, 48, unroll=4)
        def _(i):
            c = i // 16
            off = pl.multiple_of(lax.rem(i, 16) * 16, 16)
            for j in range(8):
                lo = xg[pl.ds(i * 128 + j, 8, stride=8), :]
                hi = xg[pl.ds(i * 128 + 64 + j, 8, stride=8), :]
                xb[leaf, c, pl.ds(off, 16), pl.ds(j * 128, 128)] = jnp.concatenate([lo, hi], axis=0).astype(BF)

    expand(0)
    pl.semaphore_wait(barrier, len(partners))
    at = {}
    ghalf = [half] + [half_of[4 - d] for d in range(1, 4)]
    grows = pl.multiple_of(k * 64 + ia * 16, 16)

    def split(parts, h):
        return sum(jnp.where(hh == h, part, 0.0) for hh, part in zip(ghalf, parts))

    def bases_1():
        at["g1"] = send(gt.at[pl.ds(pl.multiple_of((1 - k) * 64, 64), 64)], rg1, t1.at[0], v1.at[0], other_core)

    def bases_2():
        at["g1"].wait_recv()
        rg1[...] += gt[pl.ds(pl.multiple_of(k * 64, 64), 64), :]
        for d in range(1, 4):
            rows = pl.multiple_of(lax.rem(ia + d, 4) * 16, 16)
            at["g2", d] = send(rg1.at[pl.ds(rows, 16)], rg2.at[d - 1], t2.at[d - 1], v2.at[d - 1], ring_a(d))

    def bases_3():
        for d in range(1, 4):
            at["g2", d].wait_recv()
        gp = [rg1[pl.ds(pl.multiple_of(ia * 16, 16), 16), :]] + [rg2[d] for d in range(3)]
        pg2[:, 0:128] = sum(p[:, 128:256] for p in gp)
        for h in range(2):
            pg2[:, 128 + h * 128:256 + h * 128] = split([p[:, 256:384] for p in gp], h)
            pg2[:, 384 + h * 128:512 + h * 128] = split([p[:, 0:128] for p in gp], h)
        for e in range(1, 4):
            at["g3", e] = send(pg2, rg3.at[e - 1], t3.at[e - 1], v3.at[e - 1], ring_b(e))
        for e in range(4):
            at["g3", 4 + e] = send(pg2.at[:, pl.ds(0, 128)], rg3x.at[e], t3x.at[e], v3x.at[e], ring_b(e, sibling))

    def bases_4():
        for e in range(1, 8):
            at["g3", e].wait_recv()
        gfull[pl.ds(grows, 16), 0:640] = pg2[...] + rg3[0] + rg3[1] + rg3[2]
        gfull[pl.ds(grows, 16), 640:768] = rg3x[0] + rg3x[1] + rg3x[2] + rg3x[3]
        for d in range(1, 4):
            part = gfull.at[pl.ds(grows, 16)]
            at["g4", d] = send(part, part, t4.at[d - 1], v4.at[d - 1], ring_a(d))

    def bases_5():
        for d in range(1, 4):
            at["g4", d].wait_recv()
        part = gfull.at[pl.ds(pl.multiple_of(k * 64, 64), 64)]
        at["g5"] = send(part, part, t5.at[0], v5.at[0], other_core)

    def permute_rows(leaf):
        if leaf == 0:
            aload.wait()
        for j in range(6):
            ash[j] = av[leaf, :, pl.ds(j * 128, 128)].astype(F32)
        for j in range(6):
            for c in range(3):
                ap[leaf, pl.ds(c * 256, 256), pl.ds(j * 128, 128)] = (
                    ash[j, pl.ds(c, 256, stride=3), :].astype(BF))

    def multiply(leaf, n):
        cols = pl.ds(n * 256, 256)
        f = jnp.dot(ap[leaf], xb[leaf, :, :, cols].reshape(768, 256), preferred_element_type=F32)
        field[:, pl.ds(leaf * 256, 256), cols] = f.reshape(3, 256, 256)

    pieces = [lambda: expand(1), lambda: expand(2)]
    for leaf in range(4):
        pieces += [lambda leaf=leaf: gather(leaf), lambda leaf=leaf: repack(leaf), lambda leaf=leaf: permute_rows(leaf)]
        pieces += [lambda leaf=leaf, n=n: multiply(leaf, n) for n in range(4)]

    def work(count):
        for _ in range(min(count, len(pieces))):
            pieces.pop(0)()

    def dot(a, b):
        return lax.dot_general(a, b, (((1,), (0,)), ((), ())), precision=HIGH, preferred_element_type=F32)

    def dot_t(a, b):
        return lax.dot_general(a, b, (((1,), (1,)), ((), ())), precision=HIGH, preferred_element_type=F32)

    def rounded(a):
        return a.astype(BF).astype(F32)

    def pair(own_first, own, other):
        return jnp.concatenate([jnp.where(own_first, own, other), jnp.where(own_first, other, own)], axis=1)

    def widen(part, hh):
        last = part[:, 256:384]
        return jnp.concatenate([part[:, 0:256], jnp.where(hh == 0, last, 0.0), jnp.where(hh == 1, last, 0.0)], axis=1)

    def narrow(block, hh):
        return jnp.concatenate([block[:, 0:256], jnp.where(hh == 0, block[:, 256:384], block[:, 384:512])], axis=1)

    def block_rows(ch, core, t, rows):
        return pl.ds(pl.multiple_of(ch * WIDE + core * CORE + t * RING, rows), rows)

    def to_core(ch):
        for d in (2, 1, 3, 0):
            src = st.at[block_rows(ch, 1 - k, lax.rem(ib + d, 4), RING)]
            at["c1", ch, d] = send(src, r1.at[ch, d], s1.at[ch, d], q1.at[ch, d], other_core)

    def to_ring_a(ch):
        for d in (2, 1, 3, 0):
            at["c1", ch, d].wait_recv()
            r1[ch, d] += st[block_rows(ch, k, lax.rem(ia + d, 4), RING), :]
            if d:
                at["c2", ch, d] = send(r1.at[ch, d], r2.at[ch, d - 1], s2.at[ch, d - 1], q2.at[ch, d - 1], ring_a(d))

    def to_ring_b(ch):
        for d in (1, 2, 3):
            at["c2", ch, d].wait_recv()
        total = widen(r1[ch, 0], half)
        for d in (1, 2, 3):
            total += widen(r2[ch, d - 1], half_of[4 - d])
        p2[ch] = total
        for e in (2, 1, 3):
            rows = pl.ds(pl.multiple_of(lax.rem(ib + e, 4) * OWN, OWN), OWN)
            at["c3", ch, e] = send(p2.at[ch, rows], r3.at[ch, e - 1], s3.at[ch, e - 1], q3.at[ch, e - 1], ring_b(e))

    def to_x(ch):
        for e in (1, 2, 3):
            at["c3", ch, e].wait_recv()
        rows = pl.ds(pl.multiple_of(ib * OWN, OWN), OWN)
        p4[ch] = p2[ch, rows, :] + r3[ch, 0] + r3[ch, 1] + r3[ch, 2]
        for i, lanes in ((2, 128), (1, 128), (0, 256)):
            at["c4", ch, i] = send(p4.at[ch, :, pl.ds(0, lanes)], r4.at[ch, i, :, pl.ds(0, lanes)],
                                   s4.at[ch, i], q4.at[ch, i], xs[i])

    def small_systems(ch):
        if ch == 0:
            cload.wait()
            at["g5"].wait_recv()
        for i in range(3):
            at["c4", ch, i].wait_recv()
        top = x // 2
        odd = lax.rem(x, 2)
        own0 = p4[ch, :, 0:128] + r4[ch, 0, :, 0:128]
        far0 = r4[ch, 1, :, 0:128] + r4[ch, 2, :, 0:128]
        w0 = rounded(dot_t(pair(top == 0, own0, far0), cp[0, pl.ds(pl.multiple_of(top * 128, 128), 128), :]))
        own1 = p4[ch, :, 128:256] - dot(w0, gfull[:, 0:128])
        far1 = r4[ch, 0, :, 128:256] - dot(w0, gfull[:, 640:768])
        w1 = rounded(dot_t(pair(odd == 0, own1, far1), cp[1, pl.ds(pl.multiple_of(odd * 128, 128), 128), :]))
        both = [p4[ch, :, 256 + h * 128:384 + h * 128] - dot(w0, gfull[:, 128 + h * 128:256 + h * 128])
                - dot(w1, gfull[:, 384 + h * 128:512 + h * 128]) for h in range(2)]
        w2 = rounded(dot_t(jnp.concatenate(both, axis=1), cp[2]))
        rows = pl.ds(pl.multiple_of(ib * OWN, OWN), OWN)
        wf[ch, rows, 0:128] = w0
        wf[ch, rows, 128:256] = w1
        wf[ch, rows, 256:512] = w2
        part = wf.at[ch, rows]
        for e in (2, 1, 3):
            at["c5", ch, e] = send(part, part, s5.at[ch, e - 1], q5.at[ch, e - 1], ring_b(e))

    def to_partner(ch, d):
        part = w.at[block_rows(ch, k, lax.rem(ia + d, 4), RING)]
        at["c7", ch, d] = send(part, part, s7.at[ch, d], q7.at[ch, d], other_core)

    def back_ring_a(ch):
        for e in (1, 2, 3):
            at["c5", ch, e].wait_recv()
        for h in range(2):
            nv[ch, h] = narrow(wf[ch], h)
        rows = block_rows(ch, k, ia, RING)
        for d in (2, 1, 3):
            at["c6", ch, d] = send(nv.at[ch, half_of[d]], w.at[rows], s6.at[ch, d - 1], q6.at[ch, d - 1], ring_a(d))
        w[rows, :] = narrow(wf[ch], half)
        to_partner(ch, 0)

    def back_core(ch):
        for d in (1, 3, 2):
            at["c6", ch, d].wait_recv()
            to_partner(ch, 4 - d)

    bases_1()
    to_core(0)
    to_core(1)
    work(1)
    bases_2()
    to_ring_a(0)
    to_ring_a(1)
    work(2)
    bases_3()
    work(6)
    to_ring_b(0)
    work(1)
    bases_4()
    work(1)
    to_ring_b(1)
    work(2)
    to_x(0)
    work(4)
    bases_5()
    to_x(1)
    small_systems(0)
    work(1)
    small_systems(1)
    work(5)
    back_ring_a(0)
    work(2)
    back_ring_a(1)
    work(99)
    back_core(0)
    back_core(1)
    work(99)
    for ch in range(CHUNKS):
        for d in range(4):
            at["c7", ch, d].wait_recv()
    for copy in sends:
        copy.wait_send()


def solve(order, x, a, st, gt, cp):
    vm = pl.BlockSpec(memory_space=pltpu.VMEM)
    hbm = pl.BlockSpec(memory_space=pl.ANY)
    dma = pltpu.SemaphoreType.DMA

    def shape(*dims):
        return pltpu.VMEM(dims, F32)

    n = CHUNKS
    sems = [(4,), (3, 4)]
    for s in [(n, 4), (n, 3), (n, 3), (n, 3), (n, 3), (n, 3), (n, 4), (1,), (3,), (3,), (4,), (3,), (1,)]:
        sems += [s, s]
    return pl.pallas_call(
        solve_kernel,
        out_shape=[pltpu.VMEM((3, 1024, 1024), F32), pltpu.VMEM((1024, 384), F32)],
        in_specs=[pl.BlockSpec(memory_space=pltpu.SMEM), hbm, hbm, vm, vm, hbm],
        out_specs=[vm, vm],
        scratch_shapes=[
            pltpu.VMEM((4, 3, 256, 1024), BF), pltpu.VMEM((4, 768, 768), BF), pltpu.VMEM((4, 768, 768), BF),
            shape(3, 1024, 8, 128), shape(6144, 128), shape(6, 768, 128), shape(3, 256, 256),
            shape(n, 4, RING, 384), shape(n, 3, RING, 384), shape(n, RING, 512),
            shape(n, 3, OWN, 512), shape(n, OWN, 512), shape(n, 3, OWN, 256), shape(n, RING, 512),
            shape(n, 2, RING, 384),
            shape(64, 384), shape(3, 16, 384), shape(16, 640), shape(3, 16, 640), shape(4, 16, 128), shape(128, 768),
        ] + [dma(s) for s in sems],
        compiler_params=pltpu.CompilerParams(vmem_limit_bytes=42 * MIB, collective_id=0, has_side_effects=True),
        name="leaf_solve_and_levels",
    )(order, x, a, st, gt, cp)


ROWS = 512


def update_kernel(field, u_hbm, wt, out, u, w, buf, usem, sem):
    loads = {}
    for c in range(3):
        for level in range(3):
            loads[c, level] = pltpu.make_async_copy(
                u_hbm.at[level, c], u.at[c, :, pl.ds(level * 128, 128)], usem.at[c, level])
            loads[c, level].start()
    w[...] = (-wt[...].T).astype(BF)
    copies = []
    for c in range(3):
        for level in range(3):
            loads[c, level].wait()
        for r in range(1024 // ROWS):
            rows = pl.ds(r * ROWS, ROWS)
            i = len(copies)
            slot = i % 4
            if i >= 4:
                copies[i - 4].wait()
            buf[slot] = field[c, rows, :] + jnp.dot(u[c, rows, :], w[...], preferred_element_type=F32)
            copies.append(pltpu.make_async_copy(buf.at[slot], out.at[c, rows, :], sem.at[slot]))
            copies[-1].start()
    for copy in copies[-4:]:
        copy.wait()


def update(field, u, wt):
    vm = pl.BlockSpec(memory_space=pltpu.VMEM)
    hbm = pl.BlockSpec(memory_space=pl.ANY)
    return pl.pallas_call(
        update_kernel,
        out_shape=jax.ShapeDtypeStruct((3, 1024, 1024), F32),
        in_specs=[vm, hbm, vm],
        out_specs=hbm,
        scratch_shapes=[
            pltpu.VMEM((3, 1024, 384), BF),
            pltpu.VMEM((384, 1024), BF),
            pltpu.VMEM((4, ROWS, 1024), F32),
            pltpu.SemaphoreType.DMA((3, 3)),
            pltpu.SemaphoreType.DMA((4,)),
        ],
        compiler_params=pltpu.CompilerParams(vmem_limit_bytes=20 * MIB),
        name="update",
    )(field, u, wt)


def body(right_sides, panel_order, leaf_inverse, test_basis, update_basis, coupling):
    sides = jnp.transpose(right_sides, (1, 0, 2))
    test = jnp.transpose(test_basis, (0, 2, 1, 3))
    upd = jnp.transpose(update_basis, (0, 2, 1, 3))
    st, gt = project(panel_order, sides, leaf_inverse, test, upd)
    field, w = solve(panel_order, sides, leaf_inverse, in_vmem(st), in_vmem(gt), coupling.reshape(3, 256, 256))
    out = update(in_vmem(field), upd, in_vmem(w))
    return jnp.transpose(out, (1, 0, 2))


def solution(mesh):
    in_specs = (
        P(("leaf", "sub"), None, None),
        P(("leaf", "sub")),
        P(("leaf", "sub"), None, None),
        P(None, ("leaf", "sub"), None, None),
        P(None, ("leaf", "sub"), None, None),
        P(None, "leaf", None, None),
    )
    out_specs = P(("leaf", "sub"), None, None)
    return jax.shard_map(body, mesh=mesh, in_specs=in_specs, out_specs=out_specs, check_vma=False)
```

```python
import jax
import jax.numpy as jnp
from jax import lax
from jax.experimental import pallas as pl
from jax.experimental.pallas import tpu as pltpu
from jax.sharding import PartitionSpec as P

BF = jnp.bfloat16
F32 = jnp.float32
MIB = 1 << 20
MESH = pl.DeviceIdType.MESH
HIGH = lax.Precision.HIGHEST
CHUNKS = 2
WIDE = 1024 // CHUNKS
CORE = WIDE // 2
RING = CORE // 4
OWN = RING // 4


def in_vmem(a):
    return pltpu.with_memory_space_constraint(a, pltpu.VMEM)


def project_kernel(order, x_hbm, a_hbm, v_hbm, u_hbm, st, gt,
                   xv, av, vv, uv, vsh, vit, bs, bd, bt, acc, places, sems):
    pairs = [(v_hbm, vv)] + [(a_hbm.at[leaf], av.at[leaf]) for leaf in range(4)]
    pairs += [(order, places), (u_hbm.at[pl.ds(0, 2)], uv), (x_hbm, xv)]
    loads = [pltpu.make_async_copy(s, d, sems.at[i]) for i, (s, d) in enumerate(pairs)]
    for copy in loads:
        copy.start()
    loads[0].wait()
    for leaf in range(4):
        for level in range(3):
            for c in range(3):
                vsh[level, pl.ds(c, 256, stride=3), :] = vv[level, c, pl.ds(leaf * 256, 256), :].astype(F32)
        for level in range(3):
            vit[leaf, pl.ds(level * 128, 128), :] = vsh[level].astype(BF).T
    for leaf in range(4):
        loads[1 + leaf].wait()
        b = jnp.dot(vit[leaf], av[leaf], preferred_element_type=F32)
        for level in range(3):
            bs[pl.ds(leaf * 6144 + level, 768, stride=8), :] = b[level * 128:level * 128 + 128].T

    loads[6].wait()
    g0 = jnp.zeros((128, 256), F32)
    g1 = jnp.zeros((128, 128), F32)
    over_rows = (((0,), (0,)), ((), ()))
    for c in range(3):
        v12 = jnp.concatenate([vv[1, c], vv[2, c]], axis=1)
        g0 += lax.dot_general(uv[0, c], v12, over_rows, preferred_element_type=F32)
        g1 += lax.dot_general(uv[1, c], vv[2, c], over_rows, preferred_element_type=F32)
    gt[:, 0:128] = g1
    gt[:, 128:384] = g0
    loads[5].wait()

    @pl.loop(0, 64)
    def _(i):
        for j in range(16):
            p = i * 16 + j
            dst = lax.bitwise_and(places[p], 1023) * 8
            for c in range(3):
                bd[pl.ds(pl.multiple_of(c * 8192 + dst, 8), 8), :] = (
                    bs[pl.ds(pl.multiple_of(p * 24 + c * 8, 8), 8), :])

    loads[7].wait()
    for c in range(3):
        for level in range(3):
            bt[pl.ds(level * 128, 128), pl.ds(c * 1024, 1024)] = (
                bd[pl.ds(c * 8192 + level, 1024, stride=8), :].astype(BF).T)
        for n in range(2):
            cols = pl.ds(n * 512, 512)
            part = jnp.dot(bt[:, pl.ds(c * 1024, 1024)], xv[c, :, cols], preferred_element_type=F32)
            if c == 0:
                acc[:, cols] = part
            elif c == 1:
                acc[:, cols] += part
            else:
                st[cols, :] = (acc[:, cols] + part).T


def project(order, x, a, v, u):
    vm = pl.BlockSpec(memory_space=pltpu.VMEM)
    hbm = pl.BlockSpec(memory_space=pl.ANY)
    return pl.pallas_call(
        project_kernel,
        out_shape=[pltpu.VMEM((1024, 384), F32), pltpu.VMEM((128, 384), F32)],
        in_specs=[pl.BlockSpec(memory_space=pltpu.HBM), hbm, hbm, hbm, hbm],
        out_specs=[vm, vm],
        scratch_shapes=[
            pltpu.VMEM((3, 1024, 1024), BF),
            pltpu.VMEM((4, 768, 768), BF),
            pltpu.VMEM((3, 3, 1024, 128), BF),
            pltpu.VMEM((2, 3, 1024, 128), BF),
            pltpu.VMEM((3, 768, 128), F32),
            pltpu.VMEM((4, 384, 768), BF),
            pltpu.VMEM((24576, 128), F32),
            pltpu.VMEM((24576, 128), F32),
            pltpu.VMEM((384, 3072), BF),
            pltpu.VMEM((384, 1024), F32),
            pltpu.SMEM((1024,), jnp.int32),
            pltpu.SemaphoreType.DMA((8,)),
        ],
        compiler_params=pltpu.CompilerParams(vmem_limit_bytes=62 * MIB),
        name="project",
    )(order, x, a, v, u)


def solve_kernel(order, x_hbm, a_hbm, st, gt, cp_hbm, field, w,
                 xb, av, ap, xf, xg, ash, cp,
                 r1, r2, p2, r3, p4, r4, wf, nv,
                 rg1, rg2, pg2, rg3, rg3x, gfull,
                 lsem, xsem, s1, q1, s2, q2, s3, q3, s4, q4, s5, q5, s6, q6, s7, q7,
                 t1, v1, t2, v2, t3, v3, t3x, v3x, t4, v4, t5, v5):
    place = lax.axis_index("leaf")
    z = lax.axis_index("sub")
    k = lax.rem(place, 2)
    y = lax.rem(place // 2, 4)
    x = place // 8
    ia = jnp.where(k == 0, z, y)
    ib = jnp.where(k == 0, y, z)
    half = y // 2

    def device(xx, yy, kk, zz):
        return ((xx * 4 + yy) * 2 + kk, zz)

    def ring_a(d):
        t = lax.rem(ia + d, 4)
        return device(x, jnp.where(k == 0, y, t), k, jnp.where(k == 0, t, z))

    def ring_b(e, xx=None):
        t = lax.rem(ib + e, 4)
        return device(x if xx is None else xx, jnp.where(k == 0, t, y), k, jnp.where(k == 0, z, t))

    sibling = x + 1 - 2 * lax.rem(x, 2)
    other_core = device(x, y, 1 - k, z)
    xs = [device(xx, y, k, z) for xx in (sibling, lax.rem(x + 2, 4), lax.rem(sibling + 2, 4))]
    half_of = {d: jnp.where(k == 0, half, lax.rem(y + d, 4) // 2) for d in (1, 2, 3)}
    half_of[0] = half
    sends = []

    def send(src, dst, ssem, rsem, where):
        copy = pltpu.make_async_remote_copy(src_ref=src, dst_ref=dst, send_sem=ssem, recv_sem=rsem,
                                            device_id=where, device_id_type=MESH)
        copy.start()
        sends.append(copy)
        return copy

    def load(src, dst, sem):
        copy = pltpu.make_async_copy(src, dst, sem)
        copy.start()
        return copy

    xloads = {}
    for c in range(3):
        for q in range(4):
            xloads[c, q] = load(x_hbm.at[c, pl.ds(q * 256, 256), :], xb.at[q, c], xsem.at[c, q])
    aload = load(a_hbm, av, lsem.at[2])
    cload = load(cp_hbm, cp, lsem.at[3])

    partners = [other_core] + xs
    for d in range(1, 4):
        partners += [ring_a(d), ring_b(d), ring_b(d, sibling)]
    barrier = pltpu.get_barrier_semaphore()
    for where in partners:
        pl.semaphore_signal(barrier, inc=1, device_id=where, device_id_type=MESH)

    xrows = xf.reshape(24576, 128)

    def expand(c):
        for q in range(4):
            xloads[c, q].wait()

        @pl.loop(0, 64, unroll=4)
        def _(i):
            q = i // 16
            rows = xb[q, c, pl.ds(pl.multiple_of(lax.rem(i, 16) * 16, 16), 16), :].astype(F32)
            for h in range(2):
                for j in range(8):
                    xrows[pl.ds(c * 8192 + i * 128 + h * 64 + j, 8, stride=8), :] = (
                        rows[h * 8:h * 8 + 8, j * 128:j * 128 + 128])

    def gather(leaf):
        @pl.loop(0, 16, unroll=2)
        def _(i):
            for kk in range(16):
                p = i * 16 + kk
                src = lax.bitwise_and(order[leaf * 256 + p], 1023)
                for c in range(3):
                    xg[pl.ds(pl.multiple_of(p * 24 + c * 8, 8), 8), :] = xf[c, src]

    def repack(leaf):
        @pl.loop(0, 48, unroll=4)
        def _(i):
            c = i // 16
            off = pl.multiple_of(lax.rem(i, 16) * 16, 16)
            for j in range(8):
                lo = xg[pl.ds(i * 128 + j, 8, stride=8), :]
                hi = xg[pl.ds(i * 128 + 64 + j, 8, stride=8), :]
                xb[leaf, c, pl.ds(off, 16), pl.ds(j * 128, 128)] = jnp.concatenate([lo, hi], axis=0).astype(BF)

    expand(0)
    pl.semaphore_wait(barrier, len(partners))
    at = {}
    ghalf = [half] + [half_of[4 - d] for d in range(1, 4)]
    grows = pl.multiple_of(k * 64 + ia * 16, 16)

    def split(parts, h):
        return sum(jnp.where(hh == h, part, 0.0) for hh, part in zip(ghalf, parts))

    def bases_1():
        at["g1"] = send(gt.at[pl.ds(pl.multiple_of((1 - k) * 64, 64), 64)], rg1, t1.at[0], v1.at[0], other_core)

    def bases_2():
        at["g1"].wait_recv()
        rg1[...] += gt[pl.ds(pl.multiple_of(k * 64, 64), 64), :]
        for d in range(1, 4):
            rows = pl.multiple_of(lax.rem(ia + d, 4) * 16, 16)
            at["g2", d] = send(rg1.at[pl.ds(rows, 16)], rg2.at[d - 1], t2.at[d - 1], v2.at[d - 1], ring_a(d))

    def bases_3():
        for d in range(1, 4):
            at["g2", d].wait_recv()
        gp = [rg1[pl.ds(pl.multiple_of(ia * 16, 16), 16), :]] + [rg2[d] for d in range(3)]
        pg2[:, 0:128] = sum(p[:, 128:256] for p in gp)
        for h in range(2):
            pg2[:, 128 + h * 128:256 + h * 128] = split([p[:, 256:384] for p in gp], h)
            pg2[:, 384 + h * 128:512 + h * 128] = split([p[:, 0:128] for p in gp], h)
        for e in range(1, 4):
            at["g3", e] = send(pg2, rg3.at[e - 1], t3.at[e - 1], v3.at[e - 1], ring_b(e))
        for e in range(4):
            at["g3", 4 + e] = send(pg2.at[:, pl.ds(0, 128)], rg3x.at[e], t3x.at[e], v3x.at[e], ring_b(e, sibling))

    def bases_4():
        for e in range(1, 8):
            at["g3", e].wait_recv()
        gfull[pl.ds(grows, 16), 0:640] = pg2[...] + rg3[0] + rg3[1] + rg3[2]
        gfull[pl.ds(grows, 16), 640:768] = rg3x[0] + rg3x[1] + rg3x[2] + rg3x[3]
        for d in range(1, 4):
            part = gfull.at[pl.ds(grows, 16)]
            at["g4", d] = send(part, part, t4.at[d - 1], v4.at[d - 1], ring_a(d))

    def bases_5():
        for d in range(1, 4):
            at["g4", d].wait_recv()
        part = gfull.at[pl.ds(pl.multiple_of(k * 64, 64), 64)]
        at["g5"] = send(part, part, t5.at[0], v5.at[0], other_core)

    def permute_rows(leaf):
        if leaf == 0:
            aload.wait()
        for j in range(6):
            ash[j] = av[leaf, :, pl.ds(j * 128, 128)].astype(F32)
        for j in range(6):
            for c in range(3):
                ap[leaf, pl.ds(c * 256, 256), pl.ds(j * 128, 128)] = (
                    ash[j, pl.ds(c, 256, stride=3), :].astype(BF))

    def multiply(leaf, n):
        cols = pl.ds(n * 256, 256)
        f = jnp.dot(ap[leaf], xb[leaf, :, :, cols].reshape(768, 256), preferred_element_type=F32)
        field[:, pl.ds(leaf * 256, 256), cols] = f.reshape(3, 256, 256)

    pieces = [lambda: expand(1), lambda: expand(2)]
    for leaf in range(4):
        pieces += [lambda leaf=leaf: gather(leaf), lambda leaf=leaf: repack(leaf), lambda leaf=leaf: permute_rows(leaf)]
        pieces += [lambda leaf=leaf, n=n: multiply(leaf, n) for n in range(4)]

    def work(count):
        for _ in range(min(count, len(pieces))):
            pieces.pop(0)()

    def dot(a, b):
        return lax.dot_general(a, b, (((1,), (0,)), ((), ())), precision=HIGH, preferred_element_type=F32)

    def dot_t(a, b):
        return lax.dot_general(a, b, (((1,), (1,)), ((), ())), precision=HIGH, preferred_element_type=F32)

    def rounded(a):
        return a.astype(BF).astype(F32)

    def pair(own_first, own, other):
        return jnp.concatenate([jnp.where(own_first, own, other), jnp.where(own_first, other, own)], axis=1)

    def widen(part, hh):
        last = part[:, 256:384]
        return jnp.concatenate([part[:, 0:256], jnp.where(hh == 0, last, 0.0), jnp.where(hh == 1, last, 0.0)], axis=1)

    def narrow(block, hh):
        return jnp.concatenate([block[:, 0:256], jnp.where(hh == 0, block[:, 256:384], block[:, 384:512])], axis=1)

    def block_rows(ch, core, t, rows):
        return pl.ds(pl.multiple_of(ch * WIDE + core * CORE + t * RING, rows), rows)

    def to_core(ch):
        for d in (2, 1, 3, 0):
            src = st.at[block_rows(ch, 1 - k, lax.rem(ib + d, 4), RING)]
            at["c1", ch, d] = send(src, r1.at[ch, d], s1.at[ch, d], q1.at[ch, d], other_core)

    def to_ring_a(ch):
        for d in (2, 1, 3, 0):
            at["c1", ch, d].wait_recv()
            r1[ch, d] += st[block_rows(ch, k, lax.rem(ia + d, 4), RING), :]
            if d:
                at["c2", ch, d] = send(r1.at[ch, d], r2.at[ch, d - 1], s2.at[ch, d - 1], q2.at[ch, d - 1], ring_a(d))

    def to_ring_b(ch):
        for d in (1, 2, 3):
            at["c2", ch, d].wait_recv()
        total = widen(r1[ch, 0], half)
        for d in (1, 2, 3):
            total += widen(r2[ch, d - 1], half_of[4 - d])
        p2[ch] = total
        for e in (2, 1, 3):
            rows = pl.ds(pl.multiple_of(lax.rem(ib + e, 4) * OWN, OWN), OWN)
            at["c3", ch, e] = send(p2.at[ch, rows], r3.at[ch, e - 1], s3.at[ch, e - 1], q3.at[ch, e - 1], ring_b(e))

    def to_x(ch):
        for e in (1, 2, 3):
            at["c3", ch, e].wait_recv()
        rows = pl.ds(pl.multiple_of(ib * OWN, OWN), OWN)
        p4[ch] = p2[ch, rows, :] + r3[ch, 0] + r3[ch, 1] + r3[ch, 2]
        for i, lanes in ((2, 128), (1, 128), (0, 256)):
            at["c4", ch, i] = send(p4.at[ch, :, pl.ds(0, lanes)], r4.at[ch, i, :, pl.ds(0, lanes)],
                                   s4.at[ch, i], q4.at[ch, i], xs[i])

    def small_systems(ch):
        if ch == 0:
            cload.wait()
            at["g5"].wait_recv()
        for i in range(3):
            at["c4", ch, i].wait_recv()
        top = x // 2
        odd = lax.rem(x, 2)
        own0 = p4[ch, :, 0:128] + r4[ch, 0, :, 0:128]
        far0 = r4[ch, 1, :, 0:128] + r4[ch, 2, :, 0:128]
        w0 = rounded(dot_t(pair(top == 0, own0, far0), cp[0, pl.ds(pl.multiple_of(top * 128, 128), 128), :]))
        t0 = dot(w0, gfull[:, 0:384])
        own1 = p4[ch, :, 128:256] - t0[:, 0:128]
        far1 = r4[ch, 0, :, 128:256] - dot(w0, gfull[:, 640:768])
        w1 = rounded(dot_t(pair(odd == 0, own1, far1), cp[1, pl.ds(pl.multiple_of(odd * 128, 128), 128), :]))
        both = p4[ch, :, 256:512] - t0[:, 128:384] - dot(w1, gfull[:, 384:640])
        w2 = rounded(dot_t(both, cp[2]))
        rows = pl.ds(pl.multiple_of(ib * OWN, OWN), OWN)
        wf[ch, rows, 0:128] = w0
        wf[ch, rows, 128:256] = w1
        wf[ch, rows, 256:512] = w2
        part = wf.at[ch, rows]
        for e in (2, 1, 3):
            at["c5", ch, e] = send(part, part, s5.at[ch, e - 1], q5.at[ch, e - 1], ring_b(e))

    def to_partner(ch, d):
        part = w.at[block_rows(ch, k, lax.rem(ia + d, 4), RING)]
        at["c7", ch, d] = send(part, part, s7.at[ch, d], q7.at[ch, d], other_core)

    def back_ring_a(ch):
        for e in (1, 2, 3):
            at["c5", ch, e].wait_recv()
        for h in range(2):
            nv[ch, h] = narrow(wf[ch], h)
        rows = block_rows(ch, k, ia, RING)
        for d in (2, 1, 3):
            at["c6", ch, d] = send(nv.at[ch, half_of[d]], w.at[rows], s6.at[ch, d - 1], q6.at[ch, d - 1], ring_a(d))
        w[rows, :] = narrow(wf[ch], half)
        to_partner(ch, 0)

    def back_core(ch):
        for d in (1, 3, 2):
            at["c6", ch, d].wait_recv()
            to_partner(ch, 4 - d)

    bases_1()
    to_core(0)
    to_core(1)
    work(1)
    bases_2()
    to_ring_a(0)
    to_ring_a(1)
    work(2)
    bases_3()
    work(6)
    to_ring_b(0)
    work(1)
    bases_4()
    work(1)
    to_ring_b(1)
    work(2)
    to_x(0)
    work(4)
    bases_5()
    to_x(1)
    small_systems(0)
    work(1)
    small_systems(1)
    work(5)
    back_ring_a(0)
    work(2)
    back_ring_a(1)
    work(99)
    back_core(0)
    back_core(1)
    work(99)
    for ch in range(CHUNKS):
        for d in range(4):
            at["c7", ch, d].wait_recv()
    for copy in sends:
        copy.wait_send()


def solve(order, x, a, st, gt, cp):
    vm = pl.BlockSpec(memory_space=pltpu.VMEM)
    hbm = pl.BlockSpec(memory_space=pl.ANY)
    dma = pltpu.SemaphoreType.DMA

    def shape(*dims):
        return pltpu.VMEM(dims, F32)

    n = CHUNKS
    sems = [(4,), (3, 4)]
    for s in [(n, 4), (n, 3), (n, 3), (n, 3), (n, 3), (n, 3), (n, 4), (1,), (3,), (3,), (4,), (3,), (1,)]:
        sems += [s, s]
    return pl.pallas_call(
        solve_kernel,
        out_shape=[pltpu.VMEM((3, 1024, 1024), F32), pltpu.VMEM((1024, 384), F32)],
        in_specs=[pl.BlockSpec(memory_space=pltpu.SMEM), hbm, hbm, vm, vm, hbm],
        out_specs=[vm, vm],
        scratch_shapes=[
            pltpu.VMEM((4, 3, 256, 1024), BF), pltpu.VMEM((4, 768, 768), BF), pltpu.VMEM((4, 768, 768), BF),
            shape(3, 1024, 8, 128), shape(6144, 128), shape(6, 768, 128), shape(3, 256, 256),
            shape(n, 4, RING, 384), shape(n, 3, RING, 384), shape(n, RING, 512),
            shape(n, 3, OWN, 512), shape(n, OWN, 512), shape(n, 3, OWN, 256), shape(n, RING, 512),
            shape(n, 2, RING, 384),
            shape(64, 384), shape(3, 16, 384), shape(16, 640), shape(3, 16, 640), shape(4, 16, 128), shape(128, 768),
        ] + [dma(s) for s in sems],
        compiler_params=pltpu.CompilerParams(vmem_limit_bytes=42 * MIB, collective_id=0, has_side_effects=True),
        name="leaf_solve_and_levels",
    )(order, x, a, st, gt, cp)


ROWS = 512
BLOCKS = [((0, 256), (256, 256), (512, 512)), ((0, 512), (512, 512)), ((0, 512), (512, 256), (768, 256))]


def update_kernel(field, u_hbm, wt, out, u, w, buf, usem, sem):
    loads = {}
    for c in range(3):
        for level in range(3):
            loads[c, level] = pltpu.make_async_copy(
                u_hbm.at[level, c], u.at[c, :, pl.ds(level * 128, 128)], usem.at[c, level])
            loads[c, level].start()
    w[...] = (-wt[...].T).astype(BF)
    copies = []
    for c in range(3):
        for level in range(3):
            loads[c, level].wait()
        for start, size in BLOCKS[c]:
            rows = pl.ds(start, size)
            i = len(copies)
            slot = i % 4
            if i >= 4:
                copies[i - 4].wait()
            part = buf.at[slot, pl.ds(0, size)]
            part[...] = field[c, rows, :] + jnp.dot(u[c, rows, :], w[...], preferred_element_type=F32)
            copies.append(pltpu.make_async_copy(part, out.at[c, rows, :], sem.at[slot]))
            copies[-1].start()
    for copy in copies[-4:]:
        copy.wait()


def update(field, u, wt):
    vm = pl.BlockSpec(memory_space=pltpu.VMEM)
    hbm = pl.BlockSpec(memory_space=pl.ANY)
    return pl.pallas_call(
        update_kernel,
        out_shape=jax.ShapeDtypeStruct((3, 1024, 1024), F32),
        in_specs=[vm, hbm, vm],
        out_specs=hbm,
        scratch_shapes=[
            pltpu.VMEM((3, 1024, 384), BF),
            pltpu.VMEM((384, 1024), BF),
            pltpu.VMEM((4, ROWS, 1024), F32),
            pltpu.SemaphoreType.DMA((3, 3)),
            pltpu.SemaphoreType.DMA((4,)),
        ],
        compiler_params=pltpu.CompilerParams(vmem_limit_bytes=20 * MIB),
        name="update",
    )(field, u, wt)


def body(right_sides, panel_order, leaf_inverse, test_basis, update_basis, coupling):
    sides = jnp.transpose(right_sides, (1, 0, 2))
    test = jnp.transpose(test_basis, (0, 2, 1, 3))
    upd = jnp.transpose(update_basis, (0, 2, 1, 3))
    st, gt = project(panel_order, sides, leaf_inverse, test, upd)
    field, w = solve(panel_order, sides, leaf_inverse, in_vmem(st), in_vmem(gt), coupling.reshape(3, 256, 256))
    out = update(in_vmem(field), upd, in_vmem(w))
    return jnp.transpose(out, (1, 0, 2))


def solution(mesh):
    in_specs = (
        P(("leaf", "sub"), None, None),
        P(("leaf", "sub")),
        P(("leaf", "sub"), None, None),
        P(None, ("leaf", "sub"), None, None),
        P(None, ("leaf", "sub"), None, None),
        P(None, "leaf", None, None),
    )
    out_specs = P(("leaf", "sub"), None, None)
    return jax.shard_map(body, mesh=mesh, in_specs=in_specs, out_specs=out_specs, check_vma=False)
```
